32 devices in a mesh: blk: 8 (over y, x, core), kv: 4 (over z).
Axes of the slice: x: 2, y: 2, z: 4, core: 2. Of those that a mesh axis runs over, the one named last changes fastest.
Arguments:
- tokens: bfloat16 [4096, 2560], P('blk'), may hold values from -6 to 6
- attn_gain: float32 [2560], replicated, may hold values from 0.1 to 1.9
- mlp_gain: float32 [2560], replicated, may hold values from 0.1 to 1.9
- w_query: float32 [2560, 2560], P(('blk', 'kv')), may hold values from -0.375 to 0.375
- w_key: float32 [2560, 640], P(('blk', 'kv')), may hold values from -0.125 to 0.125
- w_value: float32 [2560, 640], P(('blk', 'kv')), may hold values from -0.125 to 0.125
- w_gate: float32 [2560, 6912], P(('blk', 'kv')), may hold values from -0.125 to 0.125
- w_up: float32 [2560, 6912], P(('blk', 'kv')), may hold values from -0.125 to 0.125
- w_out: bfloat16 [2560, 2560], P('kv'), may hold values from -0.125 to 0.125
- w_down: bfloat16 [6912, 2560], P('kv'), may hold values from -0.078125 to 0.078125
- cache: bfloat16 [2, 64, 8, 80, 128], P(None, 'blk', 'kv'), may hold values from -300 to 300
- slot_prompt: int32 [64], replicated, may hold values from 0 to 7, as said below
- prefix_len: int32 [8], replicated, may hold values from 1 to 2048, as said below
- new_len: int32 [8], replicated, may hold values from 256 to 512, as said below
Outputs:
- mixed: bfloat16 [4096, 2560], P('blk', 'kv')
The draws below stay inside these ranges and needn't reach their ends.
Inputs may be any that keep to these rules, and one draw needn't show every extreme that they name: `slot_prompt`: the 8 slots of one index of blk hold at most 2 blocks of one prompt. One prompt, drawn afresh, has exactly 2 blocks on every index of blk; the other 6 slots of an index hold blocks of distinct prompts; every prompt has at least one block. `prefix_len`: A prompt with c slots has a prefix longer than (c - 1) * 128 and at most c * 128. Rows i >= new_len[p] of prompt p are padding.
All inputs are finite; a program needn't handle non-finite values.
Results may differ from the reference program's by a relative error of at most 0.019.
The reference program's roundings to bfloat16 on the way (of `normed`, `attended`, `middle`, `normed_mid` and `hidden`) count: a program that leaves them out, or rounds other values in their place, can miss the bound.
Values may be sent and summed in bfloat16 or wider, within the bound.
No kernel may reach another device: no remote copies, remote signals or barrier semaphores. Data moves between devices by JAX's collectives and lax.ppermute only.
A program may use at most 128 MiB of HBM per device.

```python
import math
import jax
import jax.numpy as jnp
from jax import lax

D = 2560
HEADS = 32
KV_HEADS = 8
HD = 80
FF = 6912
WINDOW = 4096
SINKS = 4
NEW = 512
BLOCK = 128
SLOTS = 8
CAP = 2
PROMPTS = 8
TOKENS = 4096
PREFIX_BLOCKS = 16


def slot_layout(key):
    base_key = jax.random.fold_in(key, 1234)
    pick_key, order_key, offset_key, shuffle_key, tail_key = jax.random.split(base_key, 5)
    heavy = jax.random.randint(pick_key, (), 0, PROMPTS)
    others = jax.random.permutation(order_key, PROMPTS - 1)
    offset_value = jax.random.randint(offset_key, (), 0, PROMPTS - 1)
    source = jnp.arange(PROMPTS, dtype=jnp.int32)[:, None]
    within = jnp.arange(SLOTS, dtype=jnp.int32)[None, :]
    cyclic = (source * (SLOTS - CAP) + within - CAP + offset_value) % (PROMPTS - 1)
    other_prompt = others[cyclic]
    other_prompt = other_prompt + (other_prompt >= heavy).astype(jnp.int32)
    table = jnp.where(within < CAP, heavy, other_prompt).astype(jnp.int32)
    shuffles = jax.vmap(lambda subkey: jax.random.permutation(subkey, SLOTS))(jax.random.split(shuffle_key, PROMPTS))
    table = jnp.take_along_axis(table, shuffles, axis=1).reshape(-1)
    counts = jnp.sum((table[:, None] == jnp.arange(PROMPTS, dtype=jnp.int32)[None, :]).astype(jnp.int32), axis=0)
    tails = jax.random.randint(tail_key, (PROMPTS,), 1, BLOCK + 1)
    tails = jnp.where(jnp.arange(PROMPTS, dtype=jnp.int32) == heavy, BLOCK, tails)
    lengths = (counts - 1) * BLOCK + tails
    return (table.astype(jnp.int32), lengths.astype(jnp.int32))


def draw_slot_prompt(key, part):
    return slot_layout(key)[0]


def draw_prefix_len(key, part):
    return slot_layout(key)[1]


def draw_new_len(key, part):
    length_key, pick_key = jax.random.split(jax.random.fold_in(key, 99))
    drawn = jax.random.randint(length_key, (PROMPTS,), NEW // 2, NEW + 1)
    longest = jax.random.randint(pick_key, (), 0, PROMPTS)
    return jnp.where(jnp.arange(PROMPTS, dtype=jnp.int32) == longest, NEW, drawn).astype(jnp.int32)


def draw_cache(key, part):
    full_shape = (2, PROMPTS * SLOTS, KV_HEADS, HD, BLOCK)
    noise_key = jax.random.fold_in(jax.random.fold_in(key, 5), 0)
    values = jnp.clip(jax.random.normal(noise_key, full_shape, dtype=jnp.float32), -5.0, 5.0)
    return values.astype(jnp.bfloat16)


def shard_levels(rng, extent, cuts, low, largest):
    gain = 1.0
    for dim, blocks in cuts:
        draws = jax.random.uniform(jax.random.fold_in(jax.random.fold_in(rng, 6), dim), (blocks,), jnp.float32, low / len(cuts), largest / len(cuts))
        gain = gain * jnp.repeat(jnp.exp(draws), extent[dim] // blocks).reshape((-1,) + (1,) * (len(extent) - 1 - dim))
    return gain


def bell_draw(own_key, extent, scale, reach, cuts=(), held_as=jnp.bfloat16):
    array = scale * jax.random.normal(own_key, extent, jnp.float32)
    if cuts:
        array = array * shard_levels(own_key, extent, cuts, -0.22, 0.18)
    return jnp.clip(array, -reach, reach).astype(held_as)


def setup_inputs(seed: int = 0) -> dict:
    seeds = jax.random.split(jax.random.key(seed), 15)
    tokens = bell_draw(seeds[0], (TOKENS, D), 1.0, 6.0, ((0, 8),))
    attn_gain = jnp.clip(1.0 + 0.18 * jax.random.normal(seeds[1], (D,), jnp.float32), 0.1, 1.9)
    mlp_gain = jnp.clip(1.0 + 0.18 * jax.random.normal(seeds[2], (D,), jnp.float32), 0.1, 1.9)
    w_query = bell_draw(seeds[3], (D, HEADS * HD), (D // 9) ** -0.5, 0.375, ((0, 32),), jnp.float32)
    w_key = bell_draw(seeds[4], (D, KV_HEADS * HD), D ** -0.5, 0.125, ((0, 32),), jnp.float32)
    w_value = bell_draw(seeds[5], (D, KV_HEADS * HD), D ** -0.5, 0.125, ((0, 32),), jnp.float32)
    w_gate = bell_draw(seeds[6], (D, FF), D ** -0.5, 0.125, ((0, 32),), jnp.float32)
    w_up = bell_draw(seeds[7], (D, FF), D ** -0.5, 0.125, ((0, 32),), jnp.float32)
    w_out = bell_draw(seeds[8], (HEADS * HD, D), (HEADS * HD) ** -0.5, 0.125, ((0, 4),))
    w_down = bell_draw(seeds[9], (FF, D), FF ** -0.5, 0.078125, ((0, 4),))
    cache = draw_cache(jax.random.fold_in(seeds[14], 71), 0)
    slot_prompt = draw_slot_prompt(jax.random.fold_in(seeds[14], 71), 0)
    prefix_len = draw_prefix_len(jax.random.fold_in(seeds[14], 71), 0)
    new_len = draw_new_len(jax.random.fold_in(seeds[14], 71), 0)
    return {"tokens": tokens, "attn_gain": attn_gain, "mlp_gain": mlp_gain, "w_query": w_query, "w_key": w_key, "w_value": w_value, "w_gate": w_gate, "w_up": w_up, "w_out": w_out, "w_down": w_down, "cache": cache, "slot_prompt": slot_prompt, "prefix_len": prefix_len, "new_len": new_len}


FLOOR_SCORE = -1e+30
EPSILON = 1e-05
ROPE_BASE = 10000.0

def rms_scale(row_data, gain_vec):
    values = row_data.astype(jnp.float32)
    mean_square = lax.optimization_barrier(jnp.mean(values * values, axis=-1, keepdims=True))
    return (values * lax.rsqrt(mean_square + EPSILON) * gain_vec).astype(jnp.bfloat16)

def rotate(values, positions):
    head_width = values.shape[-1]
    half_width = head_width // 2
    frequency = ROPE_BASE ** (-2.0 * jnp.arange(half_width, dtype=jnp.float32) / head_width)
    angles = positions.astype(jnp.float32)[:, None] * frequency[None, :]
    cosine = jnp.cos(angles)[:, None, :]
    sine_wave = jnp.sin(angles)[:, None, :]
    first_half = values[..., :half_width]
    second_half = values[..., half_width:]
    return jnp.concatenate([first_half * cosine - second_half * sine_wave, second_half * cosine + first_half * sine_wave], axis=-1)

def slot_ranks(slot_prompt, prompts, slots):
    onehot = (slot_prompt[:, None] == jnp.arange(prompts, dtype=jnp.int32)[None, :]).astype(jnp.int32)
    running = jnp.cumsum(onehot, axis=0)
    global_rank = lax.optimization_barrier(jnp.sum(onehot * (running - 1), axis=1))
    local_count = jnp.cumsum(onehot.reshape(-1, slots, prompts), axis=1).reshape(-1, prompts)
    local_rank = lax.optimization_barrier(jnp.sum(onehot * (local_count - 1), axis=1))
    return (global_rank.astype(jnp.int32), local_rank.astype(jnp.int32))

def visible(query_pos, key_pos):
    distance = query_pos - key_pos
    return (distance >= 0) & ((distance < WINDOW) | (key_pos < SINKS))

def reference(tokens, attn_gain, mlp_gain, w_query, w_key, w_value, w_gate, w_up, w_out, w_down, cache, slot_prompt, prefix_len, new_len):
    per_group = HEADS // KV_HEADS
    score_scale = 1.0 / math.sqrt(HD)
    normed = rms_scale(tokens, attn_gain)
    new_ids = jnp.arange(NEW, dtype=jnp.int32)
    positions = (prefix_len[:, None] + new_ids[None, :]).reshape(-1)
    query_all = jnp.dot(normed, w_query.astype(jnp.bfloat16), preferred_element_type=jnp.float32)
    query_all = rotate(query_all.reshape(TOKENS, HEADS, HD), positions).astype(jnp.bfloat16)
    key_all = jnp.dot(normed, w_key.astype(jnp.bfloat16), preferred_element_type=jnp.float32)
    key_all = rotate(key_all.reshape(TOKENS, KV_HEADS, HD), positions).astype(jnp.bfloat16)
    value_all = jnp.dot(normed, w_value.astype(jnp.bfloat16), preferred_element_type=jnp.float32)
    value_all = value_all.astype(jnp.bfloat16).reshape(TOKENS, KV_HEADS, HD)
    global_rank, local_rank = slot_ranks(slot_prompt, PROMPTS, SLOTS)
    slot_ids = jnp.arange(PROMPTS * SLOTS, dtype=jnp.int32)
    matched = (slot_prompt[None, None, :] == jnp.arange(PROMPTS, dtype=jnp.int32)[:, None, None]) & (global_rank[None, None, :] == jnp.arange(PREFIX_BLOCKS, dtype=jnp.int32)[None, :, None])
    table = lax.optimization_barrier(jnp.sum(jnp.where(matched, slot_ids[None, None, :], 0), axis=2)).astype(jnp.int32)
    cached_span = PREFIX_BLOCKS * BLOCK
    cached_ids = jnp.arange(cached_span, dtype=jnp.int32)

    def one_prompt(prompt):
        first_row = prompt * NEW
        row_block = lax.dynamic_slice_in_dim(query_all, first_row, NEW, 0)
        own_keys = lax.dynamic_slice_in_dim(key_all, first_row, NEW, 0)
        own_values = lax.dynamic_slice_in_dim(value_all, first_row, NEW, 0)
        picked = jnp.take(cache, table[prompt], axis=1)
        picked = jnp.transpose(picked, (0, 1, 4, 2, 3)).reshape(2, cached_span, KV_HEADS, HD)
        all_keys = jnp.concatenate([picked[0], own_keys], axis=0)
        all_values = jnp.concatenate([picked[1], own_values], axis=0)
        before = prefix_len[prompt]
        key_pos = jnp.concatenate([cached_ids, before + new_ids])
        key_live = jnp.concatenate([cached_ids < before, new_ids < new_len[prompt]])
        query_pos = before + new_ids
        seen_mask = key_live[None, :] & visible(query_pos[:, None], key_pos[None, :])

        def one_head(head_index):
            kv_group = head_index // per_group
            queries = lax.dynamic_index_in_dim(row_block, head_index, 1, keepdims=False)
            keys_here = lax.dynamic_index_in_dim(all_keys, kv_group, 1, keepdims=False)
            values_here = lax.dynamic_index_in_dim(all_values, kv_group, 1, keepdims=False)
            scores = jnp.dot(queries, keys_here.T, preferred_element_type=jnp.float32) * score_scale
            masked = jnp.where(seen_mask, scores, FLOOR_SCORE)
            row_max = lax.optimization_barrier(jnp.max(masked, axis=1, keepdims=True))
            weights = jnp.where(seen_mask, jnp.exp(masked - row_max), 0.0)
            totals = lax.optimization_barrier(jnp.sum(weights, axis=1, keepdims=True))
            return jnp.dot(weights.astype(jnp.bfloat16), values_here, preferred_element_type=jnp.float32) / totals
        head_out = lax.map(one_head, jnp.arange(HEADS, dtype=jnp.int32))
        return jnp.transpose(head_out, (1, 0, 2)).reshape(NEW, HEADS * HD).astype(jnp.bfloat16)
    attended = lax.map(one_prompt, jnp.arange(PROMPTS, dtype=jnp.int32)).reshape(TOKENS, HEADS * HD)
    middle = (tokens.astype(jnp.float32) + jnp.dot(attended, w_out, preferred_element_type=jnp.float32)).astype(jnp.bfloat16)
    normed_mid = rms_scale(middle, mlp_gain)
    gate_proj = jnp.dot(normed_mid, w_gate.astype(jnp.bfloat16), preferred_element_type=jnp.float32)
    up_proj = jnp.dot(normed_mid, w_up.astype(jnp.bfloat16), preferred_element_type=jnp.float32)
    hidden = (jax.nn.silu(gate_proj) * up_proj).astype(jnp.bfloat16)
    mixed = middle.astype(jnp.float32) + jnp.dot(hidden, w_down, preferred_element_type=jnp.float32)
    row_live = (new_ids[None, :] < new_len[:, None]).reshape(-1)
    return jnp.where(row_live[:, None], mixed, 0.0).astype(jnp.bfloat16)
```

```python
import math

import jax
import jax.numpy as jnp
from jax import lax
from jax.sharding import PartitionSpec as P

HEADS = 32
KV_HEADS = 8
HD = 80
WINDOW = 4096
SINKS = 4
BLOCK = 128
CAP = 2


FLOOR_SCORE = -1e30
EPSILON = 1e-05
ROPE_BASE = 10000.0


def rms_scale(row_data, gain_vec):
    values = row_data.astype(jnp.float32)
    mean_square = jnp.mean(values * values, axis=-1, keepdims=True)
    return (values * lax.rsqrt(mean_square + EPSILON) * gain_vec).astype(jnp.bfloat16)


def rotate(values, positions):
    head_width = values.shape[-1]
    half_width = head_width // 2
    frequency = ROPE_BASE ** (-2.0 * jnp.arange(half_width, dtype=jnp.float32) / head_width)
    angles = positions.astype(jnp.float32)[:, None] * frequency[None, :]
    cosine = jnp.cos(angles)[:, None, :]
    sine_wave = jnp.sin(angles)[:, None, :]
    first_half = values[..., :half_width]
    second_half = values[..., half_width:]
    return jnp.concatenate(
        [
            first_half * cosine - second_half * sine_wave,
            second_half * cosine + first_half * sine_wave,
        ],
        axis=-1,
    )


def slot_ranks(slot_prompt, prompts, slots):
    onehot = (slot_prompt[:, None] == jnp.arange(prompts, dtype=jnp.int32)[None, :]).astype(
        jnp.int32
    )
    running = jnp.cumsum(onehot, axis=0)
    global_rank = jnp.sum(onehot * (running - 1), axis=1)
    local_count = jnp.cumsum(onehot.reshape(-1, slots, prompts), axis=1).reshape(-1, prompts)
    local_rank = jnp.sum(onehot * (local_count - 1), axis=1)
    return (global_rank, local_rank)


def visible(query_pos, key_pos):
    distance = query_pos - key_pos
    return (distance >= 0) & ((distance < WINDOW) | (key_pos < SINKS))


def partial_block(scores, seen_mask):
    masked = jnp.where(seen_mask, scores, FLOOR_SCORE)
    row_max = jnp.max(masked, axis=-1)
    weights = jnp.where(seen_mask, jnp.exp(masked - row_max[..., None]), 0.0)
    return (row_max, jnp.sum(weights, axis=-1), weights.astype(jnp.bfloat16))


def combine(first_part, second_part):
    maxima = jnp.maximum(first_part[0], second_part[0])
    scale_first = jnp.exp(first_part[0] - maxima)
    scale_second = jnp.exp(second_part[0] - maxima)
    totals = first_part[1] * scale_first + second_part[1] * scale_second
    outputs = first_part[2] * scale_first[..., None] + second_part[2] * scale_second[..., None]
    return (maxima, totals, outputs)


def pack_groups(matrices, groups):
    pieces = []
    for group in range(groups):
        columns = []
        for matrix in matrices:
            width = matrix.shape[1] // groups
            columns.append(matrix[:, group * width : (group + 1) * width].astype(jnp.bfloat16))
        pieces.append(jnp.concatenate(columns, axis=1))
    return jnp.stack(pieces, axis=0)


def regroup(packed):
    moved = lax.all_to_all(packed, "kv", split_axis=0, concat_axis=0, tiled=True)
    rows = moved.reshape(-1, moved.shape[2])
    return lax.all_gather(rows, "blk", axis=0, tiled=True)


def shards(
    tokens,
    attn_gain,
    mlp_gain,
    w_query,
    w_key,
    w_value,
    w_gate,
    w_up,
    w_out,
    w_down,
    cache,
    slot_prompt,
    prefix_len,
    new_len,
):
    groups = lax.axis_size("kv")
    blk_index = lax.axis_index("blk")
    kv_index = lax.axis_index("kv")
    w_qkv = regroup(pack_groups((w_query, w_key, w_value), groups))
    w_pair = regroup(pack_groups((w_gate, w_up), groups))
    query_width = w_query.shape[1] // groups
    key_width = w_key.shape[1] // groups
    kv_local = key_width // HD
    per_group = HEADS // KV_HEADS
    new_rows = tokens.shape[0]
    prompts = prefix_len.shape[0]
    slots = cache.shape[1]
    score_scale = 1.0 / math.sqrt(HD)
    prefix_here = prefix_len[blk_index]
    live_count = new_len[blk_index]
    row_ids = jnp.arange(new_rows, dtype=jnp.int32)
    positions = prefix_here + row_ids
    offsets = jnp.arange(BLOCK, dtype=jnp.int32)
    normed = rms_scale(tokens, attn_gain)
    projected = jnp.dot(normed, w_qkv, preferred_element_type=jnp.float32)
    queries = rotate(projected[:, :query_width].reshape(new_rows, -1, HD), positions).astype(
        jnp.bfloat16
    )
    key_new = rotate(
        projected[:, query_width : query_width + key_width].reshape(new_rows, kv_local, HD),
        positions,
    ).astype(jnp.bfloat16)
    value_new = (
        projected[:, query_width + key_width :].reshape(new_rows, kv_local, HD).astype(jnp.bfloat16)
    )
    grouped_q = queries.reshape(new_rows, kv_local, per_group, HD)
    own_scores = (
        jnp.einsum("qgnd,kgd->gnqk", grouped_q, key_new, preferred_element_type=jnp.float32)
        * score_scale
    )
    own_mask = (row_ids[None, :] < live_count) & visible(positions[:, None], positions[None, :])
    own_max, own_sum, own_weights = partial_block(own_scores, own_mask)
    own_out = jnp.einsum(
        "gnqk,kgd->gnqd", own_weights, value_new, preferred_element_type=jnp.float32
    )
    running = (own_max, own_sum, own_out)
    global_rank, local_rank = slot_ranks(slot_prompt, prompts, slots)
    own_prompts = lax.dynamic_slice_in_dim(slot_prompt, blk_index * slots, slots)
    own_ranks = lax.dynamic_slice_in_dim(local_rank, blk_index * slots, slots)
    placed = own_prompts * CAP + own_ranks
    buffer_ids = jnp.arange(prompts * CAP, dtype=jnp.int32)
    matches = placed[None, :] == buffer_ids[:, None]
    source_slot = jnp.sum(
        jnp.where(matches, jnp.arange(slots, dtype=jnp.int32)[None, :], 0), axis=1
    )
    filled = jnp.any(matches, axis=1)
    outgoing = jnp.where(
        filled[None, :, None, None, None],
        jnp.take(cache, source_slot, axis=1),
        jnp.zeros((), cache.dtype),
    )
    arrived = lax.all_to_all(outgoing, "blk", split_axis=1, concat_axis=1, tiled=True)
    slot_ids = jnp.arange(prompts * slots, dtype=jnp.int32)
    landing = slot_ids // slots * CAP + local_rank
    for_me = slot_prompt == blk_index
    received = (landing[None, :] == buffer_ids[:, None]) & for_me[None, :]
    block_number = jnp.sum(jnp.where(received, global_rank[None, :], 0), axis=1)
    block_live = jnp.any(received, axis=1)
    total_slots = prompts * CAP
    group_slots = min(total_slots, max(1, 512 // BLOCK))
    step_count = total_slots // group_slots
    key_blocks = arrived[0].reshape(step_count, group_slots, kv_local, HD, BLOCK)
    value_blocks = arrived[1].reshape(step_count, group_slots, kv_local, HD, BLOCK)
    numbers = block_number.reshape(step_count, group_slots)
    live_flags = block_live.reshape(step_count, group_slots)

    def prefix_step(running_state, inputs):
        key_part, value_part, number_part, flag_part = inputs
        scores = (
            jnp.einsum("qgnd,sgdt->gnqst", grouped_q, key_part, preferred_element_type=jnp.float32)
            * score_scale
        )
        scores = scores.reshape(kv_local, per_group, new_rows, group_slots * BLOCK)
        key_pos = number_part[:, None] * BLOCK + offsets[None, :]
        key_live = (flag_part[:, None] & (key_pos < prefix_here)).reshape(-1)
        seen_mask = key_live[None, :] & visible(positions[:, None], key_pos.reshape(-1)[None, :])
        block_max, block_sum, weights = partial_block(scores, seen_mask)
        weights = weights.reshape(kv_local, per_group, new_rows, group_slots, BLOCK)
        block_out = jnp.einsum(
            "gnqst,sgdt->gnqd", weights, value_part, preferred_element_type=jnp.float32
        )
        return (combine(running_state, (block_max, block_sum, block_out)), None)

    running = lax.scan(prefix_step, running, (key_blocks, value_blocks, numbers, live_flags))[0]
    totals = running[1]
    outputs = running[2]
    attended = (
        jnp.transpose(outputs / totals[..., None], (2, 0, 1, 3))
        .reshape(new_rows, -1)
        .astype(jnp.bfloat16)
    )
    projected_out = jnp.dot(attended, w_out, preferred_element_type=jnp.float32)
    summed = lax.psum(projected_out.astype(jnp.bfloat16), "kv").astype(jnp.float32)
    middle = (tokens.astype(jnp.float32) + summed).astype(jnp.bfloat16)
    normed_mid = rms_scale(middle, mlp_gain)
    paired = jnp.dot(normed_mid, w_pair, preferred_element_type=jnp.float32)
    hidden_width = w_pair.shape[1] // 2
    hidden = (jax.nn.silu(paired[:, :hidden_width]) * paired[:, hidden_width:]).astype(jnp.bfloat16)
    down_part = jnp.dot(hidden, w_down, preferred_element_type=jnp.float32)
    reduced = lax.psum_scatter(
        down_part.astype(jnp.bfloat16), "kv", scatter_dimension=1, tiled=True
    ).astype(jnp.float32)
    out_width = reduced.shape[1]
    residual = lax.dynamic_slice_in_dim(middle, kv_index * out_width, out_width, 1).astype(
        jnp.float32
    )
    mixed = jnp.where((row_ids < live_count)[:, None], residual + reduced, 0.0)
    return mixed.astype(jnp.bfloat16)


def solution(mesh):
    return jax.shard_map(
        shards,
        mesh=mesh,
        in_specs=(
            P("blk", None),
            P(),
            P(),
            P(("blk", "kv"), None),
            P(("blk", "kv"), None),
            P(("blk", "kv"), None),
            P(("blk", "kv"), None),
            P(("blk", "kv"), None),
            P("kv", None),
            P("kv", None),
            P(None, "blk", "kv", None, None),
            P(),
            P(),
            P(),
        ),
        out_specs=P("blk", "kv"),
        check_vma=False,
    )
```

```python
import functools
import math

import jax
import jax.numpy as jnp
from jax import lax
from jax.experimental import pallas as pl
from jax.experimental.pallas import tpu as pltpu
from jax.sharding import PartitionSpec as P

HEADS = 32
KV_HEADS = 8
HD = 80
WINDOW = 4096
SINKS = 4
BLOCK = 128
CAP = 2


FLOOR_SCORE = -1e30
EPSILON = 1e-05
ROPE_BASE = 10000.0
FAR = 1 << 30
LANES = 128
TILE = 256
ROW_TILE = 128
VMEM_LIMIT = 56 * 1024 * 1024

ANY = pl.BlockSpec(memory_space=pl.ANY)
VMEM = pl.BlockSpec(memory_space=pltpu.VMEM)
SMEM = pl.BlockSpec(memory_space=pltpu.SMEM)


def rms_scale(row_data, gain_vec):
    values = row_data.astype(jnp.float32)
    mean_square = jnp.mean(values * values, axis=-1, keepdims=True)
    return (values * lax.rsqrt(mean_square + EPSILON) * gain_vec).astype(jnp.bfloat16)


def rope_tables(positions):
    half_width = HD // 2
    frequency = ROPE_BASE ** (-2.0 * jnp.arange(half_width, dtype=jnp.float32) / HD)
    angles = positions.astype(jnp.float32)[:, None] * frequency[None, :]
    cosine = jnp.cos(angles)
    sine = jnp.sin(angles)
    return (
        jnp.concatenate([cosine, cosine], axis=1),
        jnp.concatenate([-sine, sine], axis=1),
    )


def slot_ranks(slot_prompt, prompts, slots):
    onehot = (slot_prompt[:, None] == jnp.arange(prompts, dtype=jnp.int32)[None, :]).astype(
        jnp.int32
    )
    running = jnp.cumsum(onehot, axis=0)
    global_rank = jnp.sum(onehot * (running - 1), axis=1)
    local_count = jnp.cumsum(onehot.reshape(-1, slots, prompts), axis=1).reshape(-1, prompts)
    local_rank = jnp.sum(onehot * (local_count - 1), axis=1)
    return (global_rank, local_rank)


def swap(values, axis, bit):
    pairs = [(index, index ^ bit) for index in range(lax.axis_size(axis))]
    return lax.ppermute(values, axis, pairs)


def half_up(width):
    return (width // 2 + LANES - 1) // LANES * LANES


def group_columns(matrices, groups, spans):
    pieces = []
    for group in range(groups):
        columns = []
        for which, first, last in spans:
            start = group * (matrices[which].shape[1] // groups)
            columns.append(matrices[which][:, start + first : start + last])
        pieces.append(jnp.concatenate(columns, axis=1).astype(jnp.bfloat16))
    return jnp.stack(pieces, axis=0)


def exchange(packed):
    moved = lax.all_to_all(packed, "kv", split_axis=0, concat_axis=0, tiled=True)
    return moved.reshape(-1, moved.shape[2])


def plane_gather(piece, diagonal_bit):
    if lax.axis_size("blk") != 8:
        return None
    by_x = swap(piece, "blk", 2)
    by_y = swap(piece, "blk", 4)
    if diagonal_bit == 2:
        across = swap(by_y, "blk", 2)
    else:
        across = swap(by_x, "blk", 4)
    mine = [(0, piece), (2, by_x), (4, by_y), (6, across)]
    return mine + [(index ^ 1, swap(values, "blk", 1)) for index, values in mine]


def gather_rows(piece, diagonal_bit):
    gathered = plane_gather(piece, diagonal_bit)
    if gathered is None:
        return [(0, lax.all_gather(piece, "blk", axis=0, tiled=True))]
    return gathered


def on_columns(body, index, width, count):
    if width % LANES == 0:
        body(pl.ds(pl.multiple_of(index * width, LANES), width))
        return
    for choice in range(count):
        pl.when(index == choice)(functools.partial(body, pl.ds(choice * width, width)))


def row_copies(sources, refs, buffer, sem, blk_index, column):
    copies = []
    for (index, _), ref in zip(sources, refs):
        rows, width = ref.shape
        first = pl.multiple_of((blk_index ^ index) * rows, 16)
        copies.append(
            pltpu.make_async_copy(
                ref, buffer.at[pl.ds(first, rows), pl.ds(column, width)], sem
            )
        )
    return copies


def attention_kernel(
    left_sources,
    right_sources,
    kv_local,
    per_group,
    place_ref,
    normed_ref,
    cos_ref,
    sin_ref,
    blocks_ref,
    cached_ref,
    own_ref,
    *refs,
):
    count_left, count_right = len(left_sources), len(right_sources)
    left = refs[:count_left]
    right = refs[count_left : count_left + count_right]
    out_ref, weights, projected, queries, keys, values, scores, probs, sem = refs[
        count_left + count_right :
    ]
    blk_index = place_ref[0]
    prefix_here = place_ref[1]
    copies = row_copies(left_sources, left, weights, sem.at[0], blk_index, 0)
    copies += row_copies(
        right_sources, right, weights, sem.at[0], blk_index, left[0].shape[1]
    )
    for copy in copies:
        copy.start()
    new_rows = normed_ref.shape[0]
    cached = blocks_ref.shape[1] * BLOCK
    span = cached + new_rows
    for head in range(kv_local):
        for block in range(blocks_ref.shape[1]):
            place = pl.ds(block * BLOCK, BLOCK)
            keys[head, :, place] = blocks_ref[0, block, head]
            values[head, place, :] = blocks_ref[1, block, head].astype(jnp.float32).T.astype(
                jnp.bfloat16
            )
    for copy in copies:
        copy.wait()

    def project(step, carry):
        rows = pl.ds(pl.multiple_of(step * TILE, TILE), TILE)
        projected[rows, :] = jnp.dot(
            normed_ref[rows, :], weights[...], preferred_element_type=jnp.float32
        )
        return carry

    lax.fori_loop(0, new_rows // TILE, project, 0)

    def rotated(rows, column):
        part = projected[rows, column : column + HD]
        turned = jnp.concatenate([part[:, HD // 2 :], part[:, : HD // 2]], axis=1)
        return part * cos_ref[rows, :] + turned * sin_ref[rows, :]

    query_width = kv_local * per_group * HD
    for chunk in range(new_rows // ROW_TILE):
        rows = pl.ds(chunk * ROW_TILE, ROW_TILE)
        for head in range(kv_local):
            for sub in range(per_group):
                queries[chunk, head, sub * ROW_TILE : (sub + 1) * ROW_TILE, :] = rotated(
                    rows, (head * per_group + sub) * HD
                ).astype(jnp.bfloat16)
            fresh = rotated(rows, query_width + head * HD)
            place = pl.ds(cached + chunk * ROW_TILE, ROW_TILE)
            keys[head, :, place] = fresh.T.astype(jnp.bfloat16)
            column = query_width + (kv_local + head) * HD
            values[head, place, :] = projected[rows, column : column + HD].astype(jnp.bfloat16)

    factor = math.log2(math.e) / math.sqrt(HD)
    group = 16

    def attend(step, carry):
        for head in range(kv_local):
            scores[...] = jnp.dot(
                queries[step, head], keys[head], preferred_element_type=jnp.float32
            )

            def soften(part, inner):
                rows = pl.ds(pl.multiple_of(part * group, group), group)
                row_id = step * ROW_TILE + lax.rem(part * group, ROW_TILE) + (
                    lax.broadcasted_iota(jnp.int32, (group, 1), 0)
                )
                floor_pos = prefix_here + row_id - WINDOW
                seen = cached_ref[...] > floor_pos
                old = jnp.where(seen, scores[rows, :cached], FLOOR_SCORE)
                own_id = lax.broadcasted_iota(jnp.int32, (1, new_rows), 1)
                seen_own = (own_ref[...] > floor_pos) & (own_id <= row_id)
                new = jnp.where(seen_own, scores[rows, cached:], FLOOR_SCORE)
                top = jnp.maximum(
                    jnp.max(old, axis=1, keepdims=True), jnp.max(new, axis=1, keepdims=True)
                )
                shift = top * factor
                old = jnp.exp2(old * factor - shift)
                new = jnp.exp2(new * factor - shift)
                total = jnp.sum(old, axis=1, keepdims=True) + jnp.sum(
                    new, axis=1, keepdims=True
                )
                probs[rows, :cached] = old.astype(jnp.bfloat16)
                probs[rows, cached:] = new.astype(jnp.bfloat16)
                scores[rows, 0:LANES] = jnp.broadcast_to(total, (group, LANES))
                return inner

            lax.fori_loop(0, per_group * ROW_TILE // group, soften, 0, unroll=2)
            summed = jnp.dot(probs[...], values[head], preferred_element_type=jnp.float32)
            summed = (summed / scores[:, 0:HD]).astype(jnp.bfloat16)
            rows = pl.ds(pl.multiple_of(step * ROW_TILE, ROW_TILE), ROW_TILE)
            for sub in range(per_group):
                column = (head * per_group + sub) * HD
                out_ref[rows, column : column + HD] = summed[
                    sub * ROW_TILE : (sub + 1) * ROW_TILE
                ]
        return carry

    lax.fori_loop(0, new_rows // ROW_TILE, attend, 0)


def attend_rows(place, normed, tables, blocks, cached_pos, own_pos, left, right, per_group):
    new_rows = normed.shape[0]
    kv_local = blocks.shape[2]
    width = left[0][1].shape[1] + right[0][1].shape[1]
    cached = blocks.shape[1] * BLOCK
    span = cached + new_rows
    heads = kv_local * per_group
    chunk_rows = per_group * ROW_TILE
    arrays = [values for _, values in left + right]
    return pl.pallas_call(
        functools.partial(attention_kernel, left, right, kv_local, per_group),
        out_shape=jax.ShapeDtypeStruct((new_rows, heads * HD), jnp.bfloat16),
        in_specs=[SMEM] + [VMEM] * 6 + [ANY] * len(arrays),
        out_specs=VMEM,
        scratch_shapes=[
            pltpu.VMEM((normed.shape[1], width), jnp.bfloat16),
            pltpu.VMEM((new_rows, width), jnp.float32),
            pltpu.VMEM((new_rows // ROW_TILE, kv_local, chunk_rows, HD), jnp.bfloat16),
            pltpu.VMEM((kv_local, HD, span), jnp.bfloat16),
            pltpu.VMEM((kv_local, span, HD), jnp.bfloat16),
            pltpu.VMEM((chunk_rows, span), jnp.float32),
            pltpu.VMEM((chunk_rows, span), jnp.bfloat16),
            pltpu.SemaphoreType.DMA((1,)),
        ],
        compiler_params=pltpu.CompilerParams(vmem_limit_bytes=VMEM_LIMIT),
        cost_estimate=pl.CostEstimate(
            flops=2 * new_rows * normed.shape[1] * width + 8 * heads * new_rows * span * LANES,
            bytes_accessed=2 * normed.shape[1] * width,
            transcendentals=heads * new_rows * span,
        ),
        name="attention",
    )(place, normed, *tables, blocks, cached_pos, own_pos, *arrays)


def middle_kernel(
    counts, groups, place_ref, tokens_ref, gain_ref, *refs
):
    att = refs[:groups]
    own_ref = refs[groups]
    left_count, right_count = counts
    rest = refs[groups + 1 :]
    left = rest[:left_count]
    right = rest[left_count : left_count + right_count]
    normed_ref, residual_ref, gathered, weights, middle, sem = rest[left_count + right_count :]
    blk_index = place_ref[0]
    kv_index = place_ref[2]
    group_rows = own_ref.shape[0]
    copies = []
    if right_count:
        copies.append(pltpu.make_async_copy(own_ref, weights.at[pl.ds(0, group_rows)], sem.at[0]))
        column = 0
        for side in (left, right):
            part, width = side[0].shape[1:]
            for index, ref in enumerate(side):
                first = pl.multiple_of((blk_index ^ XOR_ORDER[index]) * part, 16)
                for other in range(1, groups):
                    copies.append(
                        pltpu.make_async_copy(
                            ref.at[other - 1],
                            weights.at[
                                pl.ds(other * group_rows + first, part), pl.ds(column, width)
                            ],
                            sem.at[0],
                        )
                    )
            column += width
    else:
        for other in range(groups):
            first = pl.multiple_of((kv_index ^ other) * group_rows, 16)
            copies.append(
                pltpu.make_async_copy(
                    left[0].at[pl.ds(first, group_rows)],
                    weights.at[pl.ds(other * group_rows, group_rows)],
                    sem.at[0],
                )
            )
    for copy in copies:
        copy.start()
    feature = att[0].shape[1]
    for other in range(groups):
        gathered[:, other * feature : (other + 1) * feature] = att[other][...]
    for copy in copies:
        copy.wait()
    new_rows, model = tokens_ref.shape
    tile = 2 * TILE

    def product(step, carry):
        columns = pl.ds(pl.multiple_of(step * tile, tile), tile)
        summed = jnp.dot(gathered[...], weights[:, columns], preferred_element_type=jnp.float32)
        middle[:, columns] = (tokens_ref[:, columns].astype(jnp.float32) + summed).astype(
            jnp.bfloat16
        )
        return carry

    lax.fori_loop(0, model // tile, product, 0)

    def scale(step, carry):
        rows = pl.ds(pl.multiple_of(step * 16, 16), 16)
        part = middle[rows, :].astype(jnp.float32)
        mean_square = jnp.mean(part * part, axis=1, keepdims=True)
        normed_ref[rows, :] = (part * lax.rsqrt(mean_square + EPSILON) * gain_ref[...]).astype(
            jnp.bfloat16
        )
        return carry

    lax.fori_loop(0, new_rows // 16, scale, 0, unroll=2)
    out_width = model // groups

    def keep(columns):
        residual_ref[...] = middle[:, columns]

    on_columns(keep, kv_index, out_width, groups)


XOR_ORDER = (0, 2, 4, 6, 1, 3, 5, 7)


def middle_rows(place, tokens, gain, attended, own, left, right):
    new_rows, model = tokens.shape
    groups = len(attended)
    arrays = left + right
    return pl.pallas_call(
        functools.partial(middle_kernel, (len(left), len(right)), groups),
        out_shape=(
            jax.ShapeDtypeStruct((new_rows, model), jnp.bfloat16),
            jax.ShapeDtypeStruct((new_rows, model // groups), jnp.bfloat16),
        ),
        in_specs=[SMEM, VMEM, VMEM] + [VMEM] * groups + [ANY] * (1 + len(arrays)),
        out_specs=(VMEM, VMEM),
        scratch_shapes=[
            pltpu.VMEM((new_rows, model), jnp.bfloat16),
            pltpu.VMEM((model, model), jnp.bfloat16),
            pltpu.VMEM((new_rows, model), jnp.bfloat16),
            pltpu.SemaphoreType.DMA((1,)),
        ],
        compiler_params=pltpu.CompilerParams(vmem_limit_bytes=VMEM_LIMIT),
        cost_estimate=pl.CostEstimate(
            flops=2 * new_rows * model * model,
            bytes_accessed=2 * model * model,
            transcendentals=0,
        ),
        name="middle",
    )(place, tokens, gain, *attended, own, *arrays)


def hidden_chunks(width):
    whole = width // LANES * LANES
    chunks = []
    first = 0
    while first < whole:
        units = min(TILE, whole - first)
        chunks.append((first, first, whole + first, units))
        first += units
    if width > whole:
        chunks.append((whole, 2 * whole, 2 * whole + width - whole, width - whole))
    return chunks


def mlp_kernel(left_sources, right_sources, groups, widths, place_ref, normed_ref, down_ref, *refs):
    count_left, count_right = len(left_sources), len(right_sources)
    left = refs[:count_left]
    right = refs[count_left : count_left + count_right]
    outs = refs[count_left + count_right : count_left + count_right + groups]
    first_half, second_half, down, hidden, sems = refs[count_left + count_right + groups :]
    blk_index = place_ref[0]
    kv_index = place_ref[2]
    loads = (
        row_copies(left_sources, left, first_half, sems.at[0], blk_index, 0),
        row_copies(right_sources, right, second_half, sems.at[1], blk_index, 0),
        [pltpu.make_async_copy(down_ref, down, sems.at[2])],
    )
    for copies in loads:
        for copy in copies:
            copy.start()
    base = 0
    for half, (width, buffer) in enumerate(zip(widths, (first_half, second_half))):
        for copy in loads[half]:
            copy.wait()
        for first, gate, up, units in hidden_chunks(width):
            if units < LANES:
                both = jnp.dot(
                    normed_ref[...],
                    buffer[:, gate : gate + 2 * units],
                    preferred_element_type=jnp.float32,
                )
                gated, raised = both[:, :units], both[:, units:]
            else:
                gated = jnp.dot(
                    normed_ref[...],
                    buffer[:, gate : gate + units],
                    preferred_element_type=jnp.float32,
                )
                raised = jnp.dot(
                    normed_ref[...], buffer[:, up : up + units], preferred_element_type=jnp.float32
                )
            hidden[:, base + first : base + first + units] = (
                gated / (1.0 + jnp.exp(-gated)) * raised
            ).astype(jnp.bfloat16)
        base += width
    for copy in loads[2]:
        copy.wait()
    out_width = outs[0].shape[1]
    for other in range(groups):

        def product(columns, out=outs[other]):
            out[...] = jnp.dot(
                hidden[...], down[:, columns], preferred_element_type=jnp.float32
            ).astype(out.dtype)

        on_columns(product, kv_index ^ other, out_width, groups)


def mlp_parts(place, normed, w_down, left, right, groups, widths):
    new_rows, model = normed.shape
    out_width = model // groups
    arrays = [values for _, values in left + right]
    return pl.pallas_call(
        functools.partial(mlp_kernel, left, right, groups, widths),
        out_shape=tuple(
            jax.ShapeDtypeStruct((new_rows, out_width), jnp.bfloat16 if other else jnp.float32)
            for other in range(groups)
        ),
        in_specs=[SMEM, VMEM, ANY] + [ANY] * len(arrays),
        out_specs=(VMEM,) * groups,
        scratch_shapes=[
            pltpu.VMEM((model, left[0][1].shape[1]), jnp.bfloat16),
            pltpu.VMEM((model, right[0][1].shape[1]), jnp.bfloat16),
            pltpu.VMEM(w_down.shape, jnp.bfloat16),
            pltpu.VMEM((new_rows, w_down.shape[0]), jnp.bfloat16),
            pltpu.SemaphoreType.DMA((3,)),
        ],
        compiler_params=pltpu.CompilerParams(vmem_limit_bytes=VMEM_LIMIT),
        cost_estimate=pl.CostEstimate(
            flops=6 * new_rows * model * w_down.shape[0],
            bytes_accessed=6 * model * w_down.shape[0],
            transcendentals=new_rows * w_down.shape[0],
        ),
        name="mlp",
    )(place, normed, w_down, *arrays)


def shards(
    tokens,
    attn_gain,
    mlp_gain,
    w_query,
    w_key,
    w_value,
    w_gate,
    w_up,
    w_out,
    w_down,
    cache,
    slot_prompt,
    prefix_len,
    new_len,
):
    groups = lax.axis_size("kv")
    blk_index = lax.axis_index("blk")
    kv_index = lax.axis_index("kv")
    query_width = w_query.shape[1] // groups
    key_width = w_key.shape[1] // groups
    per_group = HEADS // KV_HEADS
    new_rows = tokens.shape[0]
    prompts = prefix_len.shape[0]
    slots = cache.shape[1]
    prefix_here = prefix_len[blk_index]
    live_count = new_len[blk_index]
    place = jnp.stack([blk_index, prefix_here, kv_index]).astype(jnp.int32)

    cut = half_up(query_width + 2 * key_width)
    if cut <= query_width:
        spans = (
            [(0, 0, cut)],
            [(0, cut, query_width), (1, 0, key_width), (2, 0, key_width)],
        )
    else:
        spans = (
            [(0, 0, query_width), (1, 0, cut - query_width)],
            [(1, cut - query_width, key_width), (2, 0, key_width)],
        )
    qkv = [
        gather_rows(exchange(group_columns((w_query, w_key, w_value), groups, span)), bit)
        for span, bit in zip(spans, (2, 4))
    ]

    global_rank, local_rank = slot_ranks(slot_prompt, prompts, slots)
    own_prompts = lax.dynamic_slice_in_dim(slot_prompt, blk_index * slots, slots)
    own_ranks = lax.dynamic_slice_in_dim(local_rank, blk_index * slots, slots)
    placed = own_prompts * CAP + own_ranks
    buffer_ids = jnp.arange(prompts * CAP, dtype=jnp.int32)
    matches = placed[None, :] == buffer_ids[:, None]
    source_slot = jnp.sum(
        jnp.where(matches, jnp.arange(slots, dtype=jnp.int32)[None, :], 0), axis=1
    )
    outgoing = jnp.take(cache, source_slot, axis=1)
    arrived = lax.all_to_all(outgoing, "blk", split_axis=1, concat_axis=1, tiled=True)
    slot_ids = jnp.arange(prompts * slots, dtype=jnp.int32)
    landing = slot_ids // slots * CAP + local_rank
    for_me = slot_prompt == blk_index
    received = (landing[None, :] == buffer_ids[:, None]) & for_me[None, :]
    block_number = jnp.sum(jnp.where(received, global_rank[None, :], 0), axis=1)
    block_live = jnp.any(received, axis=1)
    key_pos = block_number[:, None] * BLOCK + jnp.arange(BLOCK, dtype=jnp.int32)[None, :]
    key_live = block_live[:, None] & (key_pos < prefix_here)
    cached_pos = jnp.where(key_live, jnp.where(key_pos < SINKS, FAR, key_pos), -FAR)
    cached_pos = cached_pos.reshape(1, -1)
    row_ids = jnp.arange(new_rows, dtype=jnp.int32)
    positions = prefix_here + row_ids
    own_pos = jnp.where(
        row_ids < live_count, jnp.where(positions < SINKS, FAR, positions), -FAR
    ).reshape(1, -1)

    normed = rms_scale(tokens, attn_gain)
    tables = rope_tables(positions)

    eighth = w_out.shape[0] // lax.axis_size("blk")
    if lax.axis_size("blk") == 8 and eighth % 16 == 0:
        share = lax.dynamic_slice_in_dim(w_out, blk_index * eighth, eighth, 0)
        shares = jnp.stack([swap(share, "kv", other) for other in range(1, groups)], axis=0)
        side = half_up(w_out.shape[1])
        out_sides = [
            [values for _, values in gather_rows(shares[:, :, :side], 2)],
            [values for _, values in gather_rows(shares[:, :, side:], 4)],
        ]
    else:
        out_sides = [[lax.all_gather(w_out, "kv", axis=0, tiled=True)], []]

    hidden_width = w_gate.shape[1] // groups
    cut = half_up(hidden_width)
    widths = (cut, hidden_width - cut)
    pair = []
    for first, last, bit in ((0, cut, 2), (cut, hidden_width, 4)):
        whole = first + (last - first) // LANES * LANES
        span = [(0, first, whole), (1, first, whole)]
        if whole < last:
            span += [(0, whole, last), (1, whole, last)]
        pair.append(gather_rows(exchange(group_columns((w_gate, w_up), groups, span)), bit))

    attended = attend_rows(
        place, normed, tables, arrived, cached_pos, own_pos, qkv[0], qkv[1], per_group
    )
    everyone = [attended] + [swap(attended, "kv", other) for other in range(1, groups)]
    normed_mid, residual = middle_rows(
        place, tokens, mlp_gain.reshape(1, -1), everyone, w_out, out_sides[0], out_sides[1]
    )
    parts = mlp_parts(place, normed_mid, w_down, pair[0], pair[1], groups, widths)
    reduced = parts[0]
    for other in range(1, groups):
        reduced = reduced + swap(parts[other], "kv", other).astype(jnp.float32)
    mixed = jnp.where(
        (row_ids < live_count)[:, None], residual.astype(jnp.float32) + reduced, 0.0
    )
    return mixed.astype(jnp.bfloat16)


def solution(mesh):
    return jax.shard_map(
        shards,
        mesh=mesh,
        in_specs=(
            P("blk", None),
            P(),
            P(),
            P(("blk", "kv"), None),
            P(("blk", "kv"), None),
            P(("blk", "kv"), None),
            P(("blk", "kv"), None),
            P(("blk", "kv"), None),
            P("kv", None),
            P("kv", None),
            P(None, "blk", "kv", None, None),
            P(),
            P(),
            P(),
        ),
        out_specs=P("blk", "kv"),
        check_vma=False,
    )
```

```python
import functools
import math

import jax
import jax.numpy as jnp
from jax import lax
from jax.experimental import pallas as pl
from jax.experimental.pallas import tpu as pltpu
from jax.sharding import PartitionSpec as P

HEADS = 32
KV_HEADS = 8
HD = 80
WINDOW = 4096
SINKS = 4
BLOCK = 128
CAP = 2


FLOOR_SCORE = -1e30
EPSILON = 1e-05
ROPE_BASE = 10000.0
FAR = 1 << 30
LANES = 128
TILE = 256
ROW_TILE = 128
VMEM_LIMIT = 56 * 1024 * 1024

ANY = pl.BlockSpec(memory_space=pl.ANY)
VMEM = pl.BlockSpec(memory_space=pltpu.VMEM)
SMEM = pl.BlockSpec(memory_space=pltpu.SMEM)


def rms_scale(row_data, gain_vec):
    values = row_data.astype(jnp.float32)
    mean_square = jnp.mean(values * values, axis=-1, keepdims=True)
    return (values * lax.rsqrt(mean_square + EPSILON) * gain_vec).astype(jnp.bfloat16)


def rope_tables(positions):
    half_width = HD // 2
    frequency = ROPE_BASE ** (-2.0 * jnp.arange(half_width, dtype=jnp.float32) / HD)
    angles = positions.astype(jnp.float32)[:, None] * frequency[None, :]
    cosine = jnp.cos(angles)
    sine = jnp.sin(angles)
    return (
        jnp.concatenate([cosine, cosine], axis=1),
        jnp.concatenate([-sine, sine], axis=1),
    )


def slot_ranks(slot_prompt, prompts, slots):
    onehot = (slot_prompt[:, None] == jnp.arange(prompts, dtype=jnp.int32)[None, :]).astype(
        jnp.int32
    )
    running = jnp.cumsum(onehot, axis=0)
    global_rank = jnp.sum(onehot * (running - 1), axis=1)
    local_count = jnp.cumsum(onehot.reshape(-1, slots, prompts), axis=1).reshape(-1, prompts)
    local_rank = jnp.sum(onehot * (local_count - 1), axis=1)
    return (global_rank, local_rank)


def swap(values, axis, bit):
    pairs = [(index, index ^ bit) for index in range(lax.axis_size(axis))]
    return lax.ppermute(values, axis, pairs)


def half_up(width):
    return (width // 2 + LANES - 1) // LANES * LANES


def pack_kernel(layouts, groups, place_ref, *refs):
    kv_index = place_ref[2]
    outs = refs[len(refs) - groups * len(layouts) :]
    for choice in range(groups):

        @pl.when(kv_index == choice)
        def _():
            for which, spans in enumerate(layouts):
                for other in range(groups):
                    out = outs[which * groups + other]
                    column = 0
                    for matrix, first, last in spans:
                        start = (choice ^ other) * (refs[matrix].shape[1] // groups)
                        width = last - first
                        out[:, column : column + width] = refs[matrix][
                            :, start + first : start + last
                        ].astype(jnp.bfloat16)
                        column += width


def pack(place, matrices, groups, layouts, name):
    rows = matrices[0].shape[0]
    shapes = []
    for spans in layouts:
        width = sum(last - first for _, first, last in spans)
        shapes += [jax.ShapeDtypeStruct((rows, width), jnp.bfloat16)] * groups
    flat = pl.pallas_call(
        functools.partial(pack_kernel, layouts, groups),
        out_shape=tuple(shapes),
        in_specs=[SMEM] + [VMEM] * len(matrices),
        out_specs=(VMEM,) * len(shapes),
        compiler_params=pltpu.CompilerParams(vmem_limit_bytes=VMEM_LIMIT),
        cost_estimate=pl.CostEstimate(
            flops=0,
            bytes_accessed=6 * rows * sum(matrix.shape[1] for matrix in matrices),
            transcendentals=0,
        ),
        name=name,
    )(place, *matrices)
    return [flat[first : first + groups] for first in range(0, len(flat), groups)]


def exchange(parts):
    moved = [parts[0]] + [swap(part, "kv", other) for other, part in enumerate(parts) if other]
    return jnp.concatenate(moved, axis=0)


def exchange_in_order(parts, kv_index):
    moved = jnp.stack(
        [parts[0]] + [swap(part, "kv", other) for other, part in enumerate(parts) if other], axis=0
    )
    order = jnp.arange(len(parts), dtype=jnp.int32) ^ kv_index
    return jnp.take(moved, order, axis=0).reshape(-1, moved.shape[2])


def after(values, *earlier):
    return lax.optimization_barrier((values, *earlier))[0]


def plane_gather(piece):
    rows = piece.shape[0]
    by_x = swap(piece, "blk", 2)
    by_y = swap(piece, "blk", 4)
    upper = swap(by_y[: rows // 2], "blk", 2)
    lower = swap(by_x[rows // 2 :], "blk", 4)
    mine = [(0, 0, piece), (2, 0, by_x), (4, 0, by_y), (6, 0, upper), (6, rows // 2, lower)]
    return mine + [(index ^ 1, first, swap(part, "blk", 1)) for index, first, part in mine]


def on_columns(body, index, width, count):
    if width % LANES == 0:
        body(pl.ds(pl.multiple_of(index * width, LANES), width))
        return
    for choice in range(count):
        pl.when(index == choice)(functools.partial(body, pl.ds(choice * width, width)))


def row_copies(sources, refs, buffer, sem, blk_index, kv_index, groups):
    copies = []
    total = buffer.shape[0]
    for (index, begin, _), ref in zip(sources, refs):
        rows = ref.shape[0]
        piece = total // 8
        block = piece // groups
        if rows == total and index is None:
            copies.append(pltpu.make_async_copy(ref, buffer, sem))
            continue
        for first in range(0, rows, block):
            if rows == total:
                base = first // piece * piece
            else:
                base = (blk_index ^ index) * piece
            other = (begin + first) % piece // block
            target = pl.multiple_of(base + (kv_index ^ other) * block, 16)
            copies.append(
                pltpu.make_async_copy(
                    ref.at[pl.ds(first, block)], buffer.at[pl.ds(target, block)], sem
                )
            )
    return copies


def attention_kernel(
    sources,
    groups,
    kv_local,
    per_group,
    place_ref,
    normed_ref,
    cos_ref,
    sin_ref,
    blocks_ref,
    cached_ref,
    own_ref,
    *refs,
):
    count = len(sources)
    pieces = refs[:count]
    (
        out_ref,
        weights,
        projected,
        queries,
        keys,
        values,
        scores,
        probs,
        folded,
        shifts,
        summed,
        sem,
    ) = refs[count:]
    blk_index = place_ref[0]
    prefix_here = place_ref[1]
    copies = row_copies(sources, pieces, weights, sem.at[0], blk_index, place_ref[2], groups)
    for copy in copies:
        copy.start()
    new_rows = normed_ref.shape[0]
    cached = blocks_ref.shape[1] * BLOCK
    span = cached + new_rows
    chunk_rows = per_group * ROW_TILE
    extra = keys.shape[1] - HD
    first_row = lax.broadcasted_iota(jnp.int32, (extra, 1), 0) == 0
    for head in range(kv_local):
        for block in range(blocks_ref.shape[1]):
            place = pl.ds(block * BLOCK, BLOCK)
            keys[head, :HD, place] = blocks_ref[0, block, head]
            values[head, place, :] = blocks_ref[1, block, head].astype(jnp.float32).T.astype(
                jnp.bfloat16
            )
        for first, flags in ((0, cached_ref), (cached, own_ref)):
            bias = jnp.where((flags[...] > -FAR) | jnp.logical_not(first_row), 0.0, FLOOR_SCORE)
            keys[head, HD:, pl.ds(first, flags.shape[1])] = bias.astype(jnp.bfloat16)
    marker = jnp.where(
        lax.broadcasted_iota(jnp.int32, (chunk_rows, extra), 1) == 0, 1.0, 0.0
    ).astype(jnp.bfloat16)
    for chunk in range(new_rows // ROW_TILE):
        for head in range(kv_local):
            queries[chunk, head, :, HD:] = marker
    for copy in copies:
        copy.wait()

    def project(step, carry):
        rows = pl.ds(pl.multiple_of(step * TILE, TILE), TILE)
        projected[rows, :] = jnp.dot(
            normed_ref[rows, :], weights[...], preferred_element_type=jnp.float32
        )
        return carry

    lax.fori_loop(0, new_rows // TILE, project, 0)

    def rotated(rows, column):
        part = projected[rows, column : column + HD]
        turned = jnp.concatenate([part[:, HD // 2 :], part[:, : HD // 2]], axis=1)
        return part * cos_ref[rows, :] + turned * sin_ref[rows, :]

    query_width = kv_local * per_group * HD
    for chunk in range(new_rows // ROW_TILE):
        rows = pl.ds(chunk * ROW_TILE, ROW_TILE)
        for head in range(kv_local):
            for sub in range(per_group):
                queries[chunk, head, sub * ROW_TILE : (sub + 1) * ROW_TILE, :HD] = rotated(
                    rows, (head * per_group + sub) * HD
                ).astype(jnp.bfloat16)
            fresh = rotated(rows, query_width + head * HD)
            place = pl.ds(cached + chunk * ROW_TILE, ROW_TILE)
            keys[head, :HD, place] = fresh.T.astype(jnp.bfloat16)
            column = query_width + (kv_local + head) * HD
            values[head, place, :] = projected[rows, column : column + HD].astype(jnp.bfloat16)

    factor = 1.0 / math.sqrt(HD)
    group = 64

    def tiles_of(step, head, first, width, own):
        scores[:, pl.ds(first, width)] = jnp.dot(
            queries[step, head], keys[head, :, pl.ds(first, width)],
            preferred_element_type=jnp.float32,
        )
        for part in range(chunk_rows // group):
            rows = pl.ds(part * group, group)
            if own:
                row_id = step * ROW_TILE + (part * group) % ROW_TILE + (
                    lax.broadcasted_iota(jnp.int32, (group, LANES), 0)
                )
            top = folded[rows, :]
            for lane in range(0, width, LANES):
                place = pl.ds(first + lane, LANES)
                piece = scores[rows, place]
                if own:
                    own_id = lane + lax.broadcasted_iota(jnp.int32, (group, LANES), 1)
                    piece = jnp.where(own_id <= row_id, piece, FLOOR_SCORE)
                    scores[rows, place] = piece
                top = jnp.maximum(top, piece)
            folded[rows, :] = top

    def weigh(head, first, width):
        for part in range(chunk_rows // group):
            rows = pl.ds(part * group, group)
            shift = shifts[rows, :]
            total = folded[rows, :]
            for lane in range(0, width, LANES):
                piece = jnp.exp(scores[rows, pl.ds(first + lane, LANES)] * factor - shift)
                total = total + piece
                probs[rows, lane : lane + LANES] = piece.astype(jnp.bfloat16)
            folded[rows, :] = total
        summed[...] += jnp.dot(
            probs[:, :width], values[head, pl.ds(first, width), :],
            preferred_element_type=jnp.float32,
        )

    step_keys = min(4 * LANES, cached)

    def attend(step, carry):
        for head in range(kv_local):
            folded[...] = jnp.full_like(folded, FLOOR_SCORE)

            def score_cached(part, inner):
                first = pl.multiple_of(part * step_keys, step_keys)
                tiles_of(step, head, first, step_keys, False)
                return inner

            lax.fori_loop(0, cached // step_keys, score_cached, 0)
            tiles_of(step, head, cached, new_rows, True)

            @pl.when(prefix_here + new_rows > WINDOW)
            def _():
                folded[...] = jnp.full_like(folded, FLOOR_SCORE)

                def narrow(part, inner):
                    rows = pl.ds(pl.multiple_of(part * 16, 16), 16)
                    row_id = step * ROW_TILE + lax.rem(part * 16, ROW_TILE) + (
                        lax.broadcasted_iota(jnp.int32, (16, 1), 0)
                    )
                    oldest = prefix_here + row_id - WINDOW
                    old = jnp.where(cached_ref[...] > oldest, scores[rows, :cached], FLOOR_SCORE)
                    new = jnp.where(own_ref[...] > oldest, scores[rows, cached:], FLOOR_SCORE)
                    scores[rows, :cached] = old
                    scores[rows, cached:] = new
                    top = jnp.maximum(
                        jnp.max(old, axis=1, keepdims=True), jnp.max(new, axis=1, keepdims=True)
                    )
                    folded[rows, :] = jnp.broadcast_to(top, (16, LANES))
                    return inner

                lax.fori_loop(0, chunk_rows // 16, narrow, 0)

            for part in range(chunk_rows // group):
                rows = pl.ds(part * group, group)
                top = jnp.max(folded[rows, :], axis=1, keepdims=True) * factor
                shifts[rows, :] = jnp.broadcast_to(top, (group, LANES))
            folded[...] = jnp.zeros_like(folded)
            summed[...] = jnp.zeros_like(summed)

            def weigh_cached(part, inner):
                first = pl.multiple_of(part * step_keys, step_keys)
                weigh(head, first, step_keys)
                return inner

            lax.fori_loop(0, cached // step_keys, weigh_cached, 0)
            weigh(head, cached, new_rows)
            rows = pl.ds(pl.multiple_of(step * ROW_TILE, ROW_TILE), ROW_TILE)
            for sub in range(per_group):
                part = pl.ds(sub * ROW_TILE, ROW_TILE)
                total = jnp.sum(folded[part, :], axis=1, keepdims=True)
                column = (head * per_group + sub) * HD
                out_ref[rows, column : column + HD] = (summed[part, :] / total).astype(
                    jnp.bfloat16
                )
        return carry

    lax.fori_loop(0, new_rows // ROW_TILE, attend, 0)


def attend_rows(place, normed, tables, blocks, cached_pos, own_pos, sources, groups, per_group):
    new_rows = normed.shape[0]
    kv_local = blocks.shape[2]
    arrays = [values for _, _, values in sources]
    width = arrays[0].shape[1]
    cached = blocks.shape[1] * BLOCK
    span = cached + new_rows
    heads = kv_local * per_group
    chunk_rows = per_group * ROW_TILE
    widest = max(new_rows, min(4 * LANES, cached))
    return pl.pallas_call(
        functools.partial(attention_kernel, sources, groups, kv_local, per_group),
        out_shape=jax.ShapeDtypeStruct((new_rows, heads * HD), jnp.bfloat16),
        in_specs=[SMEM] + [VMEM] * 6 + [ANY] * len(arrays),
        out_specs=VMEM,
        scratch_shapes=[
            pltpu.VMEM((normed.shape[1], width), jnp.bfloat16),
            pltpu.VMEM((new_rows, width), jnp.float32),
            pltpu.VMEM((new_rows // ROW_TILE, kv_local, chunk_rows, HD + 16), jnp.bfloat16),
            pltpu.VMEM((kv_local, HD + 16, span), jnp.bfloat16),
            pltpu.VMEM((kv_local, span, HD), jnp.bfloat16),
            pltpu.VMEM((chunk_rows, span), jnp.float32),
            pltpu.VMEM((chunk_rows, widest), jnp.bfloat16),
            pltpu.VMEM((chunk_rows, LANES), jnp.float32),
            pltpu.VMEM((chunk_rows, LANES), jnp.float32),
            pltpu.VMEM((chunk_rows, HD), jnp.float32),
            pltpu.SemaphoreType.DMA((1,)),
        ],
        compiler_params=pltpu.CompilerParams(vmem_limit_bytes=VMEM_LIMIT),
        cost_estimate=pl.CostEstimate(
            flops=2 * new_rows * normed.shape[1] * width + 8 * heads * new_rows * span * LANES,
            bytes_accessed=2 * normed.shape[1] * width,
            transcendentals=heads * new_rows * span,
        ),
        name="attention",
    )(place, normed, *tables, blocks, cached_pos, own_pos, *arrays)


def middle_kernel(sources, groups, place_ref, tokens_ref, gain_ref, *refs):
    att = refs[:groups]
    own_ref = refs[groups]
    rest = refs[groups + 1 :]
    shares = rest[: len(sources)]
    normed_ref, residual_ref, gathered, weights, middle, sem = rest[len(sources) :]
    blk_index = place_ref[0]
    kv_index = place_ref[2]
    group_rows = own_ref.shape[0]
    copies = []
    if shares[0].ndim == 3:
        copies.append(pltpu.make_async_copy(own_ref, weights.at[pl.ds(0, group_rows)], sem.at[0]))
        for (index, _, _), ref in zip(sources, shares):
            part = ref.shape[1]
            first = pl.multiple_of((blk_index ^ index) * part, 16)
            for other in range(1, groups):
                copies.append(
                    pltpu.make_async_copy(
                        ref.at[other - 1],
                        weights.at[pl.ds(other * group_rows + first, part)],
                        sem.at[0],
                    )
                )
    else:
        for other in range(groups):
            first = pl.multiple_of((kv_index ^ other) * group_rows, 16)
            copies.append(
                pltpu.make_async_copy(
                    shares[0].at[pl.ds(first, group_rows)],
                    weights.at[pl.ds(other * group_rows, group_rows)],
                    sem.at[0],
                )
            )
    for copy in copies:
        copy.start()
    feature = att[0].shape[1]
    for other in range(groups):
        gathered[:, other * feature : (other + 1) * feature] = att[other][...]
    for copy in copies:
        copy.wait()
    new_rows, model = tokens_ref.shape
    tile = 2 * TILE

    def product(step, carry):
        columns = pl.ds(pl.multiple_of(step * tile, tile), tile)
        summed = jnp.dot(gathered[...], weights[:, columns], preferred_element_type=jnp.float32)
        middle[:, columns] = (tokens_ref[:, columns].astype(jnp.float32) + summed).astype(
            jnp.bfloat16
        )
        return carry

    lax.fori_loop(0, model // tile, product, 0)

    def scale(step, carry):
        rows = pl.ds(pl.multiple_of(step * 16, 16), 16)
        part = middle[rows, :].astype(jnp.float32)
        mean_square = jnp.mean(part * part, axis=1, keepdims=True)
        normed_ref[rows, :] = (part * lax.rsqrt(mean_square + EPSILON) * gain_ref[...]).astype(
            jnp.bfloat16
        )
        return carry

    lax.fori_loop(0, new_rows // 16, scale, 0, unroll=2)
    out_width = model // groups

    def keep(columns):
        residual_ref[...] = middle[:, columns]

    on_columns(keep, kv_index, out_width, groups)


def middle_rows(place, tokens, gain, attended, own, sources):
    new_rows, model = tokens.shape
    groups = len(attended)
    arrays = [values for _, _, values in sources]
    return pl.pallas_call(
        functools.partial(middle_kernel, sources, groups),
        out_shape=(
            jax.ShapeDtypeStruct((new_rows, model), jnp.bfloat16),
            jax.ShapeDtypeStruct((new_rows, model // groups), jnp.bfloat16),
        ),
        in_specs=[SMEM, VMEM, VMEM] + [VMEM] * groups + [ANY] * (1 + len(arrays)),
        out_specs=(VMEM, VMEM),
        scratch_shapes=[
            pltpu.VMEM((new_rows, model), jnp.bfloat16),
            pltpu.VMEM((model, model), jnp.bfloat16),
            pltpu.VMEM((new_rows, model), jnp.bfloat16),
            pltpu.SemaphoreType.DMA((1,)),
        ],
        compiler_params=pltpu.CompilerParams(vmem_limit_bytes=VMEM_LIMIT),
        cost_estimate=pl.CostEstimate(
            flops=2 * new_rows * model * model,
            bytes_accessed=2 * model * model,
            transcendentals=0,
        ),
        name="middle",
    )(place, tokens, gain, *attended, own, *arrays)


def hidden_chunks(width):
    whole = width // LANES * LANES
    chunks = []
    first = 0
    while first < whole:
        units = min(TILE, whole - first)
        chunks.append((first, first, whole + first, units))
        first += units
    if width > whole:
        chunks.append((whole, 2 * whole, 2 * whole + width - whole, width - whole))
    return chunks


def mlp_kernel(sources, groups, widths, place_ref, normed_ref, down_ref, left, right, *refs):
    outs = refs[:groups]
    first_half, second_half, down, hidden, sems = refs[groups:]
    kv_index = place_ref[2]
    blk_index = place_ref[0]
    loads = (
        row_copies(sources[:1], [left], first_half, sems.at[0], blk_index, kv_index, groups),
        row_copies(sources[1:], [right], second_half, sems.at[1], blk_index, kv_index, groups),
        [pltpu.make_async_copy(down_ref, down, sems.at[2])],
    )
    for copies in loads:
        for copy in copies:
            copy.start()
    base = 0
    for half, (width, buffer) in enumerate(zip(widths, (first_half, second_half))):
        for copy in loads[half]:
            copy.wait()
        for first, gate, up, units in hidden_chunks(width):
            if units < LANES:
                both = jnp.dot(
                    normed_ref[...],
                    buffer[:, gate : gate + 2 * units],
                    preferred_element_type=jnp.float32,
                )
                gated, raised = both[:, :units], both[:, units:]
            else:
                gated = jnp.dot(
                    normed_ref[...],
                    buffer[:, gate : gate + units],
                    preferred_element_type=jnp.float32,
                )
                raised = jnp.dot(
                    normed_ref[...], buffer[:, up : up + units], preferred_element_type=jnp.float32
                )
            hidden[:, base + first : base + first + units] = (
                gated / (1.0 + jnp.exp(-gated)) * raised
            ).astype(jnp.bfloat16)
        base += width
    for copy in loads[2]:
        copy.wait()
    out_width = outs[0].shape[1]
    for other in range(groups):

        def product(columns, out=outs[other]):
            out[...] = jnp.dot(
                hidden[...], down[:, columns], preferred_element_type=jnp.float32
            ).astype(out.dtype)

        on_columns(product, kv_index ^ other, out_width, groups)


def mlp_parts(place, normed, w_down, sources, groups, widths):
    (_, _, left), (_, _, right) = sources
    new_rows, model = normed.shape
    out_width = model // groups
    return pl.pallas_call(
        functools.partial(mlp_kernel, sources, groups, widths),
        out_shape=tuple(
            jax.ShapeDtypeStruct((new_rows, out_width), jnp.bfloat16 if other else jnp.float32)
            for other in range(groups)
        ),
        in_specs=[SMEM, VMEM, ANY, ANY, ANY],
        out_specs=(VMEM,) * groups,
        scratch_shapes=[
            pltpu.VMEM(left.shape, jnp.bfloat16),
            pltpu.VMEM(right.shape, jnp.bfloat16),
            pltpu.VMEM(w_down.shape, jnp.bfloat16),
            pltpu.VMEM((new_rows, w_down.shape[0]), jnp.bfloat16),
            pltpu.SemaphoreType.DMA((3,)),
        ],
        compiler_params=pltpu.CompilerParams(vmem_limit_bytes=VMEM_LIMIT),
        cost_estimate=pl.CostEstimate(
            flops=6 * new_rows * model * w_down.shape[0],
            bytes_accessed=6 * model * w_down.shape[0],
            transcendentals=new_rows * w_down.shape[0],
        ),
        name="mlp",
    )(place, normed, w_down, left, right)


def shards(
    tokens,
    attn_gain,
    mlp_gain,
    w_query,
    w_key,
    w_value,
    w_gate,
    w_up,
    w_out,
    w_down,
    cache,
    slot_prompt,
    prefix_len,
    new_len,
):
    groups = lax.axis_size("kv")
    blk_index = lax.axis_index("blk")
    kv_index = lax.axis_index("kv")
    query_width = w_query.shape[1] // groups
    key_width = w_key.shape[1] // groups
    per_group = HEADS // KV_HEADS
    new_rows = tokens.shape[0]
    prompts = prefix_len.shape[0]
    slots = cache.shape[1]
    prefix_here = prefix_len[blk_index]
    live_count = new_len[blk_index]
    place = jnp.stack([blk_index, prefix_here, kv_index]).astype(jnp.int32)

    global_rank, local_rank = slot_ranks(slot_prompt, prompts, slots)
    own_prompts = lax.dynamic_slice_in_dim(slot_prompt, blk_index * slots, slots)
    own_ranks = lax.dynamic_slice_in_dim(local_rank, blk_index * slots, slots)
    placed = own_prompts * CAP + own_ranks
    buffer_ids = jnp.arange(prompts * CAP, dtype=jnp.int32)
    matches = placed[None, :] == buffer_ids[:, None]
    source_slot = jnp.sum(
        jnp.where(matches, jnp.arange(slots, dtype=jnp.int32)[None, :], 0), axis=1
    )
    outgoing = jnp.take(cache, source_slot, axis=1)
    arrived = lax.all_to_all(outgoing, "blk", split_axis=1, concat_axis=1, tiled=True)
    slot_ids = jnp.arange(prompts * slots, dtype=jnp.int32)
    landing = slot_ids // slots * CAP + local_rank
    for_me = slot_prompt == blk_index
    received = (landing[None, :] == buffer_ids[:, None]) & for_me[None, :]
    block_number = jnp.sum(jnp.where(received, global_rank[None, :], 0), axis=1)
    block_live = jnp.any(received, axis=1)
    key_pos = block_number[:, None] * BLOCK + jnp.arange(BLOCK, dtype=jnp.int32)[None, :]
    key_live = block_live[:, None] & (key_pos < prefix_here)
    cached_pos = jnp.where(key_live, jnp.where(key_pos < SINKS, FAR, key_pos), -FAR)
    cached_pos = cached_pos.reshape(1, -1)
    row_ids = jnp.arange(new_rows, dtype=jnp.int32)
    positions = prefix_here + row_ids
    own_pos = jnp.where(
        row_ids < live_count, jnp.where(positions < SINKS, FAR, positions), -FAR
    ).reshape(1, -1)

    in_place = lax.axis_size("blk") == 8 and w_query.shape[0] % 16 == 0
    spans = [(0, 0, query_width), (1, 0, key_width), (2, 0, key_width)]
    (qkv_parts,) = pack(place, (w_query, w_key, w_value), groups, [spans], "pack_qkv")
    if in_place:
        moved_qkv = exchange(qkv_parts)
        qkv = plane_gather(after(moved_qkv, arrived))
        near, across = [qkv[at][2] for at in (1, 2)], [qkv[at][2] for at in (3, 4)]
    else:
        moved_qkv = exchange_in_order(qkv_parts, kv_index)
        qkv = [(None, 0, lax.all_gather(moved_qkv, "blk", axis=0, tiled=True))]
        near, across = [moved_qkv], [moved_qkv]

    normed = rms_scale(tokens, attn_gain)
    tables = rope_tables(positions)

    hidden_width = w_gate.shape[1] // groups
    cut = half_up(hidden_width)
    widths = (cut, hidden_width - cut)
    layouts = []
    for first, last in ((0, cut), (cut, hidden_width)):
        whole = first + (last - first) // LANES * LANES
        layouts.append([(0, first, whole), (1, first, whole)])
        if whole < last:
            layouts[-1] += [(0, whole, last), (1, whole, last)]
    pair = []
    moved = moved_qkv
    packed = pack(place, (w_gate, w_up), groups, layouts, "pack_pair")
    for parts, earlier in zip(packed, (near, across)):
        parts = after(parts, moved)
        if in_place:
            moved = exchange(parts)
            index = 0
        else:
            moved = exchange_in_order(parts, kv_index)
            index = None
        ready = after(moved, *earlier)
        pair.append((index, 0, lax.all_gather(ready, "blk", axis=0, tiled=True)))

    eighth = w_out.shape[0] // lax.axis_size("blk")
    spread = in_place and eighth % 16 == 0
    if spread:
        share = lax.dynamic_slice_in_dim(w_out, blk_index * eighth, eighth, 0)
        share = after(share, moved, *[values for _, _, values in qkv])
        shares = jnp.stack([swap(share, "kv", other) for other in range(1, groups)], axis=0)

    attended = attend_rows(
        place, normed, tables, arrived, cached_pos, own_pos, qkv, groups, per_group
    )
    if spread:
        shares = after(shares, attended)
        by_x = swap(shares, "blk", 2)
        by_y = swap(shares, "blk", 4)
        mine = [(0, 0, shares), (2, 0, by_x), (4, 0, by_y), (6, 0, swap(by_y, "blk", 2))]
        w_out_sources = mine + [
            (index ^ 1, first, swap(part, "blk", 1)) for index, first, part in mine
        ]
    else:
        w_out_sources = [(0, 0, lax.all_gather(w_out, "kv", axis=0, tiled=True))]

    everyone = [attended] + [swap(attended, "kv", other) for other in range(1, groups)]
    normed_mid, residual = middle_rows(
        place, tokens, mlp_gain.reshape(1, -1), everyone, w_out, w_out_sources
    )
    parts = mlp_parts(place, normed_mid, w_down, pair, groups, widths)
    reduced = parts[0]
    for other in range(1, groups):
        reduced = reduced + swap(parts[other], "kv", other).astype(jnp.float32)
    mixed = jnp.where(
        (row_ids < live_count)[:, None], residual.astype(jnp.float32) + reduced, 0.0
    )
    return mixed.astype(jnp.bfloat16)


def solution(mesh):
    return jax.shard_map(
        shards,
        mesh=mesh,
        in_specs=(
            P("blk", None),
            P(),
            P(),
            P(("blk", "kv"), None),
            P(("blk", "kv"), None),
            P(("blk", "kv"), None),
            P(("blk", "kv"), None),
            P(("blk", "kv"), None),
            P("kv", None),
            P("kv", None),
            P(None, "blk", "kv", None, None),
            P(),
            P(),
            P(),
        ),
        out_specs=P("blk", "kv"),
        check_vma=False,
    )
```

```python
import functools
import math

import jax
import jax.numpy as jnp
from jax import lax
from jax.experimental import pallas as pl
from jax.experimental.pallas import tpu as pltpu
from jax.sharding import PartitionSpec as P

HEADS = 32
KV_HEADS = 8
HD = 80
WINDOW = 4096
SINKS = 4
BLOCK = 128
CAP = 2


FLOOR_SCORE = -1e30
EPSILON = 1e-05
ROPE_BASE = 10000.0
FAR = 1 << 30
LANES = 128
TILE = 256
ROW_TILE = 128
VMEM_LIMIT = 56 * 1024 * 1024

ANY = pl.BlockSpec(memory_space=pl.ANY)
VMEM = pl.BlockSpec(memory_space=pltpu.VMEM)
SMEM = pl.BlockSpec(memory_space=pltpu.SMEM)


def rms_scale(row_data, gain_vec):
    values = row_data.astype(jnp.float32)
    mean_square = jnp.mean(values * values, axis=-1, keepdims=True)
    return (values * lax.rsqrt(mean_square + EPSILON) * gain_vec).astype(jnp.bfloat16)


def rope_tables(positions):
    half_width = HD // 2
    frequency = ROPE_BASE ** (-2.0 * jnp.arange(half_width, dtype=jnp.float32) / HD)
    angles = positions.astype(jnp.float32)[:, None] * frequency[None, :]
    cosine = jnp.cos(angles)
    sine = jnp.sin(angles)
    return (
        jnp.concatenate([cosine, cosine], axis=1),
        jnp.concatenate([-sine, sine], axis=1),
    )


def slot_ranks(slot_prompt, prompts, slots):
    onehot = (slot_prompt[:, None] == jnp.arange(prompts, dtype=jnp.int32)[None, :]).astype(
        jnp.int32
    )
    running = jnp.cumsum(onehot, axis=0)
    global_rank = jnp.sum(onehot * (running - 1), axis=1)
    local_count = jnp.cumsum(onehot.reshape(-1, slots, prompts), axis=1).reshape(-1, prompts)
    local_rank = jnp.sum(onehot * (local_count - 1), axis=1)
    return (global_rank, local_rank)


def swap(values, axis, bit):
    pairs = [(index, index ^ bit) for index in range(lax.axis_size(axis))]
    return lax.ppermute(values, axis, pairs)


def half_up(width):
    return (width // 2 + LANES - 1) // LANES * LANES


def pack_kernel(layouts, groups, *refs):
    kv_index = lax.axis_index("kv")
    outs = refs[len(refs) - groups * len(layouts) :]
    for choice in range(groups):

        @pl.when(kv_index == choice)
        def _():
            for which, spans in enumerate(layouts):
                for other in range(groups):
                    out = outs[which * groups + other]
                    column = 0
                    for matrix, first, last in spans:
                        start = (choice ^ other) * (refs[matrix].shape[1] // groups)
                        width = last - first
                        out[:, column : column + width] = refs[matrix][
                            :, start + first : start + last
                        ].astype(jnp.bfloat16)
                        column += width


def pack(matrices, groups, layouts, name):
    rows = matrices[0].shape[0]
    shapes = []
    for spans in layouts:
        width = sum(last - first for _, first, last in spans)
        shapes += [jax.ShapeDtypeStruct((rows, width), jnp.bfloat16)] * groups
    flat = pl.pallas_call(
        functools.partial(pack_kernel, layouts, groups),
        out_shape=tuple(shapes),
        in_specs=[VMEM] * len(matrices),
        out_specs=(VMEM,) * len(shapes),
        compiler_params=pltpu.CompilerParams(vmem_limit_bytes=VMEM_LIMIT),
        cost_estimate=pl.CostEstimate(
            flops=0,
            bytes_accessed=6 * rows * sum(matrix.shape[1] for matrix in matrices),
            transcendentals=0,
        ),
        name=name,
    )(*matrices)
    return [flat[first : first + groups] for first in range(0, len(flat), groups)]


def exchange(parts):
    moved = [parts[0]] + [swap(part, "kv", other) for other, part in enumerate(parts) if other]
    return jnp.concatenate(moved, axis=0)


def exchange_in_order(parts, kv_index):
    moved = jnp.stack(
        [parts[0]] + [swap(part, "kv", other) for other, part in enumerate(parts) if other], axis=0
    )
    order = jnp.arange(len(parts), dtype=jnp.int32) ^ kv_index
    return jnp.take(moved, order, axis=0).reshape(-1, moved.shape[2])


def after(values, *earlier):
    return lax.optimization_barrier((values, *earlier))[0]


def plane_gather(piece):
    rows = piece.shape[0]
    by_x = swap(piece, "blk", 2)
    by_y = swap(piece, "blk", 4)
    upper = swap(by_y[: rows // 2], "blk", 2)
    lower = swap(by_x[rows // 2 :], "blk", 4)
    mine = [(0, 0, piece), (2, 0, by_x), (4, 0, by_y), (6, 0, upper), (6, rows // 2, lower)]
    return mine + [(index ^ 1, first, swap(part, "blk", 1)) for index, first, part in mine]


def on_columns(body, index, width, count):
    if width % LANES == 0:
        body(pl.ds(pl.multiple_of(index * width, LANES), width))
        return
    for choice in range(count):
        pl.when(index == choice)(functools.partial(body, pl.ds(choice * width, width)))


def row_copies(sources, refs, buffer, sem, blk_index, kv_index, groups):
    copies = []
    total = buffer.shape[0]
    for (index, begin, _), ref in zip(sources, refs):
        rows = ref.shape[0]
        piece = total // 8
        block = piece // groups
        if rows == total and index is None:
            copies.append(pltpu.make_async_copy(ref, buffer, sem))
            continue
        for first in range(0, rows, block):
            if rows == total:
                base = first // piece * piece
            else:
                base = (blk_index ^ index) * piece
            other = (begin + first) % piece // block
            target = pl.multiple_of(base + (kv_index ^ other) * block, 16)
            copies.append(
                pltpu.make_async_copy(
                    ref.at[pl.ds(first, block)], buffer.at[pl.ds(target, block)], sem
                )
            )
    return copies


EXTRA = 16


def cache_kernel(blocks_ref, flags_ref, keys, values):
    first_row = lax.broadcasted_iota(jnp.int32, (EXTRA, 1), 0) == 0
    bias = jnp.where((flags_ref[...] > -FAR) | jnp.logical_not(first_row), 0.0, FLOOR_SCORE)
    for head in range(blocks_ref.shape[2]):
        keys[head, HD:, :] = bias.astype(jnp.bfloat16)
        for block in range(blocks_ref.shape[1]):
            place = pl.ds(block * BLOCK, BLOCK)
            keys[head, :HD, place] = blocks_ref[0, block, head]
            values[head, place, :] = blocks_ref[1, block, head].astype(jnp.float32).T.astype(
                jnp.bfloat16
            )


def cached_rows(blocks, flags):
    kv_local = blocks.shape[2]
    cached = flags.shape[1]
    return pl.pallas_call(
        cache_kernel,
        out_shape=(
            jax.ShapeDtypeStruct((kv_local, HD + EXTRA, cached), jnp.bfloat16),
            jax.ShapeDtypeStruct((kv_local, cached, HD), jnp.bfloat16),
        ),
        in_specs=[VMEM, VMEM],
        out_specs=(VMEM, VMEM),
        compiler_params=pltpu.CompilerParams(vmem_limit_bytes=VMEM_LIMIT),
        cost_estimate=pl.CostEstimate(
            flops=0, bytes_accessed=4 * blocks.size, transcendentals=0
        ),
        name="cached",
    )(blocks, flags)


def project_kernel(
    sources, groups, kv_local, per_group, place_ref, normed_ref, cos_ref, sin_ref, flags_ref, *refs
):
    count = len(sources)
    pieces = refs[:count]
    queries, keys, values, weights, projected, sem = refs[count:]
    copies = row_copies(sources, pieces, weights, sem.at[0], place_ref[0], place_ref[2], groups)
    for copy in copies:
        copy.start()
    new_rows = normed_ref.shape[0]
    chunk_rows = per_group * ROW_TILE
    first_row = lax.broadcasted_iota(jnp.int32, (EXTRA, 1), 0) == 0
    bias = jnp.where((flags_ref[...] > -FAR) | jnp.logical_not(first_row), 0.0, FLOOR_SCORE)
    marker = jnp.where(
        lax.broadcasted_iota(jnp.int32, (chunk_rows, EXTRA), 1) == 0, 1.0, 0.0
    ).astype(jnp.bfloat16)
    for head in range(kv_local):
        keys[head, HD:, :] = bias.astype(jnp.bfloat16)
        for chunk in range(new_rows // ROW_TILE):
            queries[chunk, head, :, HD:] = marker
    for copy in copies:
        copy.wait()

    def project(step, carry):
        rows = pl.ds(pl.multiple_of(step * TILE, TILE), TILE)
        projected[rows, :] = jnp.dot(
            normed_ref[rows, :], weights[...], preferred_element_type=jnp.float32
        )
        return carry

    lax.fori_loop(0, new_rows // TILE, project, 0)

    def rotated(rows, column):
        part = projected[rows, column : column + HD]
        turned = jnp.concatenate([part[:, HD // 2 :], part[:, : HD // 2]], axis=1)
        return part * cos_ref[rows, :] + turned * sin_ref[rows, :]

    query_width = kv_local * per_group * HD
    for chunk in range(new_rows // ROW_TILE):
        rows = pl.ds(chunk * ROW_TILE, ROW_TILE)
        for head in range(kv_local):
            for sub in range(per_group):
                queries[chunk, head, sub * ROW_TILE : (sub + 1) * ROW_TILE, :HD] = rotated(
                    rows, (head * per_group + sub) * HD
                ).astype(jnp.bfloat16)
            keys[head, :HD, rows] = rotated(rows, query_width + head * HD).T.astype(jnp.bfloat16)
            column = query_width + (kv_local + head) * HD
            values[head, rows, :] = projected[rows, column : column + HD].astype(jnp.bfloat16)


def project_rows(place, normed, tables, flags, sources, groups, kv_local, per_group):
    new_rows = normed.shape[0]
    arrays = [values for _, _, values in sources]
    width = arrays[0].shape[1]
    chunks = new_rows // ROW_TILE
    return pl.pallas_call(
        functools.partial(project_kernel, sources, groups, kv_local, per_group),
        out_shape=(
            jax.ShapeDtypeStruct(
                (chunks, kv_local, per_group * ROW_TILE, HD + EXTRA), jnp.bfloat16
            ),
            jax.ShapeDtypeStruct((kv_local, HD + EXTRA, new_rows), jnp.bfloat16),
            jax.ShapeDtypeStruct((kv_local, new_rows, HD), jnp.bfloat16),
        ),
        in_specs=[SMEM] + [VMEM] * 4 + [ANY] * len(arrays),
        out_specs=(VMEM,) * 3,
        scratch_shapes=[
            pltpu.VMEM((normed.shape[1], width), jnp.bfloat16),
            pltpu.VMEM((new_rows, width), jnp.float32),
            pltpu.SemaphoreType.DMA((1,)),
        ],
        compiler_params=pltpu.CompilerParams(vmem_limit_bytes=VMEM_LIMIT),
        cost_estimate=pl.CostEstimate(
            flops=2 * new_rows * normed.shape[1] * width,
            bytes_accessed=2 * normed.shape[1] * width,
            transcendentals=0,
        ),
        name="project",
    )(place, normed, *tables, flags, *arrays)


def attention_kernel(
    first_step,
    place_ref,
    queries,
    cached_keys,
    cached_values,
    own_keys,
    own_values,
    cached_ref,
    own_ref,
    out_ref,
    scores,
    probs,
    folded,
    shifts,
    summed,
):
    prefix_here = place_ref[1]
    kv_local, _, cached = cached_keys.shape
    new_rows = own_keys.shape[2]
    chunk_rows = queries.shape[2]
    per_group = chunk_rows // ROW_TILE
    factor = math.log2(math.e) / math.sqrt(HD)
    group = 64
    widest = min(4 * LANES, cached)
    tiles = [
        (first, cached_keys, cached_values, first, widest) for first in range(0, cached, widest)
    ]
    tiles.append((cached, own_keys, own_values, 0, new_rows))

    def score(step, head, first, keys, _, begin, width):
        scores[head, :, pl.ds(first, width)] = jnp.dot(
            queries[step, head],
            keys[head, :, pl.ds(begin, width)],
            preferred_element_type=jnp.float32,
        )
        own = keys is own_keys
        for part in range(chunk_rows // group):
            rows = pl.ds(part * group, group)
            if own:
                row_id = (first_step + step) * ROW_TILE + (part * group) % ROW_TILE + (
                    lax.broadcasted_iota(jnp.int32, (group, LANES), 0)
                )
            top = folded[head, rows, :]
            for lane in range(0, width, LANES):
                place = pl.ds(first + lane, LANES)
                piece = scores[head, rows, place]
                if own:
                    own_id = lane + lax.broadcasted_iota(jnp.int32, (group, LANES), 1)
                    piece = jnp.where(own_id <= row_id, piece, FLOOR_SCORE)
                    scores[head, rows, place] = piece
                top = jnp.maximum(top, piece)
            folded[head, rows, :] = top

    def narrow(step, head):
        def some(part, inner):
            rows = pl.ds(pl.multiple_of(part * 16, 16), 16)
            row_id = (first_step + step) * ROW_TILE + lax.rem(part * 16, ROW_TILE) + (
                lax.broadcasted_iota(jnp.int32, (16, 1), 0)
            )
            oldest = prefix_here + row_id - WINDOW
            old = jnp.where(cached_ref[...] > oldest, scores[head, rows, :cached], FLOOR_SCORE)
            new = jnp.where(own_ref[...] > oldest, scores[head, rows, cached:], FLOOR_SCORE)
            scores[head, rows, :cached] = old
            scores[head, rows, cached:] = new
            top = jnp.maximum(
                jnp.max(old, axis=1, keepdims=True), jnp.max(new, axis=1, keepdims=True)
            )
            folded[head, rows, :] = jnp.broadcast_to(top, (16, LANES))
            return inner

        lax.fori_loop(0, chunk_rows // 16, some, 0)

    def weigh(head, start, first, _, values, begin, width):
        for part in range(chunk_rows // group):
            rows = pl.ds(part * group, group)
            shift = shifts[head, rows, :]
            total = None if start else folded[head, rows, :]
            for lane in range(0, width, LANES):
                place = pl.ds(first + lane, LANES)
                piece = jnp.exp2(scores[head, rows, place] * factor - shift)
                total = piece if total is None else total + piece
                probs[head, rows, place] = piece.astype(jnp.bfloat16)
            folded[head, rows, :] = total
        return jnp.dot(
            probs[head, :, pl.ds(first, width)],
            values[head, pl.ds(begin, width), :],
            preferred_element_type=jnp.float32,
        )

    def attend(windowed, step, carry):
        for head in range(kv_local):
            folded[head] = jnp.full(folded.shape[1:], FLOOR_SCORE, jnp.float32)
            for tile in tiles:
                score(step, head, *tile)
        for head in range(kv_local):
            if windowed:
                narrow(step, head)
            for part in range(chunk_rows // group):
                rows = pl.ds(part * group, group)
                top = jnp.max(folded[head, rows, :], axis=1, keepdims=True) * factor
                shifts[head, rows, :] = jnp.broadcast_to(top, (group, LANES))
            for which, tile in enumerate(tiles):
                part = weigh(head, which == 0, *tile)
                summed[head] = part if which == 0 else summed[head] + part
            rows = pl.ds(pl.multiple_of(step * ROW_TILE, ROW_TILE), ROW_TILE)
            for sub in range(per_group):
                part = pl.ds(sub * ROW_TILE, ROW_TILE)
                total = jnp.sum(folded[head, part, :], axis=1, keepdims=True)
                column = (head * per_group + sub) * HD
                out_ref[rows, column : column + HD] = (summed[head, part, :] / total).astype(
                    jnp.bfloat16
                )
        return carry

    behind = prefix_here + new_rows > WINDOW
    for windowed in (False, True):

        @pl.when(behind == windowed)
        def _():
            lax.fori_loop(0, queries.shape[0], functools.partial(attend, windowed), 0)


def attend_rows(place, first_step, queries, cached, own, cached_pos, own_pos):
    chunks, kv_local, chunk_rows, _ = queries.shape
    span = cached_pos.shape[1] + own_pos.shape[1]
    heads = kv_local * chunk_rows // ROW_TILE
    new_rows = chunks * ROW_TILE
    return pl.pallas_call(
        functools.partial(attention_kernel, first_step),
        out_shape=jax.ShapeDtypeStruct((new_rows, heads * HD), jnp.bfloat16),
        in_specs=[SMEM] + [VMEM] * 7,
        out_specs=VMEM,
        scratch_shapes=[
            pltpu.VMEM((kv_local, chunk_rows, span), jnp.float32),
            pltpu.VMEM((kv_local, chunk_rows, span), jnp.bfloat16),
            pltpu.VMEM((kv_local, chunk_rows, LANES), jnp.float32),
            pltpu.VMEM((kv_local, chunk_rows, LANES), jnp.float32),
            pltpu.VMEM((kv_local, chunk_rows, HD), jnp.float32),
        ],
        compiler_params=pltpu.CompilerParams(vmem_limit_bytes=VMEM_LIMIT),
        cost_estimate=pl.CostEstimate(
            flops=8 * heads * new_rows * span * LANES,
            bytes_accessed=4 * span * LANES * kv_local,
            transcendentals=heads * new_rows * span,
        ),
        name="attention",
    )(place, queries, *cached, *own, cached_pos, own_pos)


def middle_kernel(sources, groups, place_ref, tokens_ref, gain_ref, *refs):
    parts = len(refs) - len(sources) - 7
    att = refs[:parts]
    own_ref = refs[parts]
    rest = refs[parts + 1 :]
    shares = rest[: len(sources)]
    normed_ref, residual_ref, gathered, weights, middle, sem = rest[len(sources) :]
    blk_index = place_ref[0]
    kv_index = place_ref[2]
    group_rows = own_ref.shape[0]
    new_rows, model = tokens_ref.shape
    tile = 2 * TILE
    loads = []
    for step in range(model // tile):
        columns = pl.ds(step * tile, tile)
        copies = []
        if shares[0].ndim == 3:
            copies.append((own_ref.at[:, columns], weights.at[pl.ds(0, group_rows), columns]))
            for (index, _, _), ref in zip(sources, shares):
                part = ref.shape[1]
                first = pl.multiple_of((blk_index ^ index) * part, 16)
                for other in range(1, groups):
                    rows = pl.ds(other * group_rows + first, part)
                    copies.append((ref.at[other - 1, :, columns], weights.at[rows, columns]))
        else:
            for other in range(groups):
                first = pl.multiple_of((kv_index ^ other) * group_rows, 16)
                rows = pl.ds(other * group_rows, group_rows)
                copies.append(
                    (shares[0].at[pl.ds(first, group_rows), columns], weights.at[rows, columns])
                )
        loads.append(
            [pltpu.make_async_copy(source, target, sem.at[step]) for source, target in copies]
        )
        for copy in loads[-1]:
            copy.start()
    some_rows, feature = att[0].shape
    for at, part in enumerate(att):
        first, other = at // groups * some_rows, at % groups
        gathered[first : first + some_rows, other * feature : (other + 1) * feature] = part[...]
    for step in range(model // tile):
        columns = pl.ds(step * tile, tile)
        for copy in loads[step]:
            copy.wait()
        summed = jnp.dot(gathered[...], weights[:, columns], preferred_element_type=jnp.float32)
        middle[:, columns] = (tokens_ref[:, columns].astype(jnp.float32) + summed).astype(
            jnp.bfloat16
        )

    def scale(step, carry):
        rows = pl.ds(pl.multiple_of(step * 16, 16), 16)
        part = middle[rows, :].astype(jnp.float32)
        mean_square = jnp.mean(part * part, axis=1, keepdims=True)
        normed_ref[rows, :] = (part * lax.rsqrt(mean_square + EPSILON) * gain_ref[...]).astype(
            jnp.bfloat16
        )
        return carry

    lax.fori_loop(0, new_rows // 16, scale, 0, unroll=2)
    out_width = model // groups

    def keep(columns):
        residual_ref[...] = middle[:, columns]

    on_columns(keep, kv_index, out_width, groups)


def middle_rows(place, tokens, gain, attended, own, sources, groups):
    new_rows, model = tokens.shape
    arrays = [values for _, _, values in sources]
    return pl.pallas_call(
        functools.partial(middle_kernel, sources, groups),
        out_shape=(
            jax.ShapeDtypeStruct((new_rows, model), jnp.bfloat16),
            jax.ShapeDtypeStruct((new_rows, model // groups), jnp.bfloat16),
        ),
        in_specs=[SMEM, VMEM, VMEM] + [VMEM] * len(attended) + [ANY] * (1 + len(arrays)),
        out_specs=(VMEM, VMEM),
        scratch_shapes=[
            pltpu.VMEM((new_rows, model), jnp.bfloat16),
            pltpu.VMEM((model, model), jnp.bfloat16),
            pltpu.VMEM((new_rows, model), jnp.bfloat16),
            pltpu.SemaphoreType.DMA((model // (2 * TILE),)),
        ],
        compiler_params=pltpu.CompilerParams(vmem_limit_bytes=VMEM_LIMIT),
        cost_estimate=pl.CostEstimate(
            flops=2 * new_rows * model * model,
            bytes_accessed=2 * model * model,
            transcendentals=0,
        ),
        name="middle",
    )(place, tokens, gain, *attended, own, *arrays)


def hidden_chunks(width):
    whole = width // LANES * LANES
    chunks = []
    first = 0
    while first < whole:
        units = min(TILE, whole - first)
        chunks.append((first, first, whole + first, units))
        first += units
    if width > whole:
        chunks.append((whole, 2 * whole, 2 * whole + width - whole, width - whole))
    return chunks


def mlp_kernel(groups, widths, place_ref, normed_ref, down_ref, left, right, *refs):
    outs = refs[:groups]
    first_half, second_half, down, hidden, sems = refs[groups:]
    kv_index = place_ref[2]
    chunks = []
    base = 0
    for width, source, buffer in zip(widths, (left, right), (first_half, second_half)):
        for first, gate, up, units in hidden_chunks(width):
            if units < LANES:
                spans = [(gate, 2 * units)]
            else:
                spans = [(gate, units), (up, units)]
            copies = [
                pltpu.make_async_copy(
                    source.at[:, pl.ds(column, count)],
                    buffer.at[:, pl.ds(column, count)],
                    sems.at[len(chunks)],
                )
                for column, count in spans
            ]
            chunks.append((buffer, spans, base + first, units, copies))
        base += width
    last = pltpu.make_async_copy(down_ref, down, sems.at[len(chunks)])
    ahead = 3
    for _, _, _, _, copies in chunks[:ahead]:
        for copy in copies:
            copy.start()
    for at, (buffer, spans, first, units, copies) in enumerate(chunks):
        for copy in copies:
            copy.wait()
        if at + ahead < len(chunks):
            for copy in chunks[at + ahead][4]:
                copy.start()
        elif at + ahead == len(chunks):
            last.start()
        products = [
            jnp.dot(
                normed_ref[...],
                buffer[:, column : column + count],
                preferred_element_type=jnp.float32,
            )
            for column, count in spans
        ]
        if len(products) == 2:
            gated, raised = products
        else:
            gated, raised = products[0][:, :units], products[0][:, units:]
        hidden[:, first : first + units] = (gated / (1.0 + jnp.exp(-gated)) * raised).astype(
            jnp.bfloat16
        )
    last.wait()
    out_width = outs[0].shape[1]
    for other in range(groups):

        def product(columns, out=outs[other]):
            out[...] = jnp.dot(
                hidden[...], down[:, columns], preferred_element_type=jnp.float32
            ).astype(out.dtype)

        on_columns(product, kv_index ^ other, out_width, groups)


def mlp_parts(place, normed, w_down, left, right, groups, widths):
    new_rows, model = normed.shape
    out_width = model // groups
    return pl.pallas_call(
        functools.partial(mlp_kernel, groups, widths),
        out_shape=tuple(
            jax.ShapeDtypeStruct((new_rows, out_width), jnp.bfloat16 if other else jnp.float32)
            for other in range(groups)
        ),
        in_specs=[SMEM, VMEM, ANY, ANY, ANY],
        out_specs=(VMEM,) * groups,
        scratch_shapes=[
            pltpu.VMEM(left.shape, jnp.bfloat16),
            pltpu.VMEM(right.shape, jnp.bfloat16),
            pltpu.VMEM(w_down.shape, jnp.bfloat16),
            pltpu.VMEM((new_rows, w_down.shape[0]), jnp.bfloat16),
            pltpu.SemaphoreType.DMA((1 + sum(len(hidden_chunks(width)) for width in widths),)),
        ],
        compiler_params=pltpu.CompilerParams(vmem_limit_bytes=VMEM_LIMIT),
        cost_estimate=pl.CostEstimate(
            flops=6 * new_rows * model * w_down.shape[0],
            bytes_accessed=6 * model * w_down.shape[0],
            transcendentals=new_rows * w_down.shape[0],
        ),
        name="mlp",
    )(place, normed, w_down, left, right)


def shards(
    tokens,
    attn_gain,
    mlp_gain,
    w_query,
    w_key,
    w_value,
    w_gate,
    w_up,
    w_out,
    w_down,
    cache,
    slot_prompt,
    prefix_len,
    new_len,
):
    groups = lax.axis_size("kv")
    blk_index = lax.axis_index("blk")
    kv_index = lax.axis_index("kv")
    query_width = w_query.shape[1] // groups
    key_width = w_key.shape[1] // groups
    per_group = HEADS // KV_HEADS
    new_rows = tokens.shape[0]
    prompts = prefix_len.shape[0]
    slots = cache.shape[1]
    prefix_here = prefix_len[blk_index]
    live_count = new_len[blk_index]
    place = jnp.stack([blk_index, prefix_here, kv_index]).astype(jnp.int32)

    global_rank, local_rank = slot_ranks(slot_prompt, prompts, slots)
    own_prompts = lax.dynamic_slice_in_dim(slot_prompt, blk_index * slots, slots)
    own_ranks = lax.dynamic_slice_in_dim(local_rank, blk_index * slots, slots)
    placed = own_prompts * CAP + own_ranks
    buffer_ids = jnp.arange(prompts * CAP, dtype=jnp.int32)
    matches = placed[None, :] == buffer_ids[:, None]
    source_slot = jnp.sum(
        jnp.where(matches, jnp.arange(slots, dtype=jnp.int32)[None, :], 0), axis=1
    )
    outgoing = jnp.take(cache, source_slot, axis=1)
    arrived = lax.all_to_all(outgoing, "blk", split_axis=1, concat_axis=1, tiled=True)
    slot_ids = jnp.arange(prompts * slots, dtype=jnp.int32)
    landing = slot_ids // slots * CAP + local_rank
    for_me = slot_prompt == blk_index
    received = (landing[None, :] == buffer_ids[:, None]) & for_me[None, :]
    block_number = jnp.sum(jnp.where(received, global_rank[None, :], 0), axis=1)
    block_live = jnp.any(received, axis=1)
    key_pos = block_number[:, None] * BLOCK + jnp.arange(BLOCK, dtype=jnp.int32)[None, :]
    key_live = block_live[:, None] & (key_pos < prefix_here)
    cached_pos = jnp.where(key_live, jnp.where(key_pos < SINKS, FAR, key_pos), -FAR)
    cached_pos = cached_pos.reshape(1, -1)
    row_ids = jnp.arange(new_rows, dtype=jnp.int32)
    positions = prefix_here + row_ids
    own_pos = jnp.where(
        row_ids < live_count, jnp.where(positions < SINKS, FAR, positions), -FAR
    ).reshape(1, -1)

    normed = rms_scale(tokens, attn_gain)
    tables = rope_tables(positions)

    in_place = lax.axis_size("blk") == 8 and w_query.shape[0] % 16 == 0
    spans = [(0, 0, query_width), (1, 0, key_width), (2, 0, key_width)]
    (qkv_parts,) = pack((w_query, w_key, w_value), groups, [spans], "pack_qkv")
    if in_place:
        moved_qkv = exchange(qkv_parts)
        qkv = plane_gather(after(moved_qkv, normed, *tables, own_pos))
        across = [qkv[at][2] for at in (3, 4)]
    else:
        moved_qkv = exchange_in_order(qkv_parts, kv_index)
        qkv = [(None, 0, lax.all_gather(moved_qkv, "blk", axis=0, tiled=True))]
        across = [moved_qkv]

    hidden_width = w_gate.shape[1] // groups
    cut = half_up(hidden_width)
    widths = (cut, hidden_width - cut)
    layouts = []
    for first, last in ((0, cut), (cut, hidden_width)):
        whole = first + (last - first) // LANES * LANES
        layouts.append([(0, first, whole), (1, first, whole)])
        if whole < last:
            layouts[-1] += [(0, whole, last), (1, whole, last)]
    packed = pack((w_gate, w_up), groups, layouts, "pack_pair")

    moved = exchange_in_order(after(packed[1], moved_qkv, arrived), kv_index)
    second_half = lax.all_gather(after(moved, *across), "blk", axis=0, tiled=True)

    eighth = w_out.shape[0] // lax.axis_size("blk")
    spread = in_place and eighth % 16 == 0
    if spread:
        share = lax.dynamic_slice_in_dim(w_out, blk_index * eighth, eighth, 0)
        share = after(share, *across)
        shares = jnp.stack([swap(share, "kv", other) for other in range(1, groups)], axis=0)

    cached = cached_rows(arrived, cached_pos)
    queries, *own = project_rows(
        place, normed, tables, own_pos, qkv, groups, cache.shape[2], per_group
    )
    half = queries.shape[0] // 2
    upper = attend_rows(place, 0, queries[:half], cached, own, cached_pos, own_pos)
    earlier = (upper, shares) if spread else (upper,)
    moved = exchange_in_order(after(packed[0], *earlier), kv_index)
    if spread:
        shares = after(shares, upper)
        by_x = swap(shares, "blk", 2)
        by_y = swap(shares, "blk", 4)
    lower = attend_rows(place, half, queries[half:], cached, own, cached_pos, own_pos)
    earlier = (lower, by_x, by_y) if spread else (lower,)
    first_half = lax.all_gather(after(moved, *earlier), "blk", axis=0, tiled=True)
    attended = jnp.concatenate([upper, lower], axis=0)
    everyone = [attended] + [swap(attended, "kv", other) for other in range(1, groups)]

    if spread:
        by_y = after(by_y, lower)
        mine = [(0, 0, shares), (2, 0, by_x), (4, 0, by_y), (6, 0, swap(by_y, "blk", 2))]
        w_out_sources = mine + [
            (index ^ 1, first, swap(part, "blk", 1)) for index, first, part in mine
        ]
    else:
        w_out_sources = [(0, 0, lax.all_gather(w_out, "kv", axis=0, tiled=True))]

    normed_mid, residual = middle_rows(
        place, tokens, mlp_gain.reshape(1, -1), everyone, w_out, w_out_sources, groups
    )
    parts = mlp_parts(place, normed_mid, w_down, first_half, second_half, groups, widths)
    reduced = parts[0]
    for other in range(1, groups):
        reduced = reduced + swap(parts[other], "kv", other).astype(jnp.float32)
    mixed = jnp.where(
        (row_ids < live_count)[:, None], residual.astype(jnp.float32) + reduced, 0.0
    )
    return mixed.astype(jnp.bfloat16)


def solution(mesh):
    return jax.shard_map(
        shards,
        mesh=mesh,
        in_specs=(
            P("blk", None),
            P(),
            P(),
            P(("blk", "kv"), None),
            P(("blk", "kv"), None),
            P(("blk", "kv"), None),
            P(("blk", "kv"), None),
            P(("blk", "kv"), None),
            P("kv", None),
            P("kv", None),
            P(None, "blk", "kv", None, None),
            P(),
            P(),
            P(),
        ),
        out_specs=P("blk", "kv"),
        check_vma=False,
    )
```

```python
import functools
import math

import jax
import jax.numpy as jnp
from jax import lax
from jax.experimental import pallas as pl
from jax.experimental.pallas import tpu as pltpu
from jax.sharding import PartitionSpec as P

HEADS = 32
KV_HEADS = 8
HD = 80
WINDOW = 4096
SINKS = 4
BLOCK = 128
CAP = 2


FLOOR_SCORE = -1e30
EPSILON = 1e-05
ROPE_BASE = 10000.0
FAR = 1 << 30
LANES = 128
TILE = 256
ROW_TILE = 128
VMEM_LIMIT = 56 * 1024 * 1024

ANY = pl.BlockSpec(memory_space=pl.ANY)
VMEM = pl.BlockSpec(memory_space=pltpu.VMEM)
SMEM = pl.BlockSpec(memory_space=pltpu.SMEM)


def rms_scale(row_data, gain_vec):
    values = row_data.astype(jnp.float32)
    mean_square = jnp.mean(values * values, axis=-1, keepdims=True)
    return (values * lax.rsqrt(mean_square + EPSILON) * gain_vec).astype(jnp.bfloat16)


def rope_tables(positions):
    half_width = HD // 2
    frequency = ROPE_BASE ** (-2.0 * jnp.arange(half_width, dtype=jnp.float32) / HD)
    angles = positions.astype(jnp.float32)[:, None] * frequency[None, :]
    cosine = jnp.cos(angles)
    sine = jnp.sin(angles)
    return (
        jnp.concatenate([cosine, cosine], axis=1),
        jnp.concatenate([-sine, sine], axis=1),
    )


def slot_ranks(slot_prompt, prompts, slots):
    onehot = (slot_prompt[:, None] == jnp.arange(prompts, dtype=jnp.int32)[None, :]).astype(
        jnp.int32
    )
    running = jnp.cumsum(onehot, axis=0)
    global_rank = jnp.sum(onehot * (running - 1), axis=1)
    local_count = jnp.cumsum(onehot.reshape(-1, slots, prompts), axis=1).reshape(-1, prompts)
    local_rank = jnp.sum(onehot * (local_count - 1), axis=1)
    return (global_rank, local_rank)


def swap(values, axis, bit):
    pairs = [(index, index ^ bit) for index in range(lax.axis_size(axis))]
    return lax.ppermute(values, axis, pairs)


def half_up(width):
    return (width // 2 + LANES - 1) // LANES * LANES


def pack_kernel(layouts, groups, *refs):
    kv_index = lax.axis_index("kv")
    outs = refs[len(refs) - groups * len(layouts) :]
    for choice in range(groups):

        @pl.when(kv_index == choice)
        def _():
            for which, spans in enumerate(layouts):
                for other in range(groups):
                    out = outs[which * groups + other]
                    column = 0
                    for matrix, first, last in spans:
                        start = (choice ^ other) * (refs[matrix].shape[1] // groups)
                        width = last - first
                        out[:, column : column + width] = refs[matrix][
                            :, start + first : start + last
                        ].astype(jnp.bfloat16)
                        column += width


def pack(matrices, groups, layouts, name):
    rows = matrices[0].shape[0]
    shapes = []
    for spans in layouts:
        width = sum(last - first for _, first, last in spans)
        shapes += [jax.ShapeDtypeStruct((rows, width), jnp.bfloat16)] * groups
    flat = pl.pallas_call(
        functools.partial(pack_kernel, layouts, groups),
        out_shape=tuple(shapes),
        in_specs=[VMEM] * len(matrices),
        out_specs=(VMEM,) * len(shapes),
        compiler_params=pltpu.CompilerParams(vmem_limit_bytes=VMEM_LIMIT),
        cost_estimate=pl.CostEstimate(
            flops=0,
            bytes_accessed=6 * rows * sum(matrix.shape[1] for matrix in matrices),
            transcendentals=0,
        ),
        name=name,
    )(*matrices)
    return [flat[first : first + groups] for first in range(0, len(flat), groups)]


def exchange(parts):
    moved = [parts[0]] + [swap(part, "kv", other) for other, part in enumerate(parts) if other]
    return jnp.concatenate(moved, axis=0)


def exchange_in_order(parts, kv_index):
    moved = jnp.stack(
        [parts[0]] + [swap(part, "kv", other) for other, part in enumerate(parts) if other], axis=0
    )
    order = jnp.arange(len(parts), dtype=jnp.int32) ^ kv_index
    return jnp.take(moved, order, axis=0).reshape(-1, moved.shape[2])


def after(values, *earlier):
    return lax.optimization_barrier((values, *earlier))[0]


def plane_gather(piece, meanwhile, later):
    rows = piece.shape[0]
    by_x = swap(piece, "blk", 2)
    by_y = swap(piece, "blk", 4)
    upper = swap(after(by_y[: rows // 2], *meanwhile), "blk", 2)
    lower = swap(after(by_x[rows // 2 :], *meanwhile), "blk", 4)
    near = jnp.concatenate([after(piece, upper, lower, *later), by_x, by_y], axis=0)
    near = swap(near, "blk", 1)
    mine = [(0, 0, piece), (2, 0, by_x), (4, 0, by_y), (6, 0, upper), (6, rows // 2, lower)]
    other = [((1, 3, 5), 0, near)]
    other += [(index ^ 1, first, swap(part, "blk", 1)) for index, first, part in mine[3:]]
    return mine + other


def on_columns(body, index, width, count):
    if width % LANES == 0:
        body(pl.ds(pl.multiple_of(index * width, LANES), width))
        return
    for choice in range(count):
        pl.when(index == choice)(functools.partial(body, pl.ds(choice * width, width)))


def row_copies(sources, refs, buffer, sem, blk_index, kv_index, groups):
    copies = []
    total = buffer.shape[0]
    for (index, begin, _), ref in zip(sources, refs):
        rows = ref.shape[0]
        piece = total // 8
        block = piece // groups
        if rows == total and index is None:
            copies.append(pltpu.make_async_copy(ref, buffer, sem))
            continue
        for first in range(0, rows, block):
            piece_index = index[first // piece] if isinstance(index, tuple) else index
            other = (begin + first) % piece // block
            target = (blk_index ^ piece_index) * piece + (kv_index ^ other) * block
            copies.append(
                pltpu.make_async_copy(
                    ref.at[pl.ds(first, block)],
                    buffer.at[pl.ds(pl.multiple_of(target, 16), block)],
                    sem,
                )
            )
    return copies


EXTRA = 16


def cache_kernel(blocks_ref, flags_ref, keys, values):
    first_row = lax.broadcasted_iota(jnp.int32, (EXTRA, 1), 0) == 0
    bias = jnp.where((flags_ref[...] > -FAR) | jnp.logical_not(first_row), 0.0, FLOOR_SCORE)
    for head in range(blocks_ref.shape[2]):
        keys[head, HD:, :] = bias.astype(jnp.bfloat16)
        for block in range(blocks_ref.shape[1]):
            place = pl.ds(block * BLOCK, BLOCK)
            keys[head, :HD, place] = blocks_ref[0, block, head]
            values[head, place, :] = blocks_ref[1, block, head].astype(jnp.float32).T.astype(
                jnp.bfloat16
            )


def cached_rows(blocks, flags):
    kv_local = blocks.shape[2]
    cached = flags.shape[1]
    return pl.pallas_call(
        cache_kernel,
        out_shape=(
            jax.ShapeDtypeStruct((kv_local, HD + EXTRA, cached), jnp.bfloat16),
            jax.ShapeDtypeStruct((kv_local, cached, HD), jnp.bfloat16),
        ),
        in_specs=[VMEM, VMEM],
        out_specs=(VMEM, VMEM),
        compiler_params=pltpu.CompilerParams(vmem_limit_bytes=VMEM_LIMIT),
        cost_estimate=pl.CostEstimate(
            flops=0, bytes_accessed=4 * blocks.size, transcendentals=0
        ),
        name="cached",
    )(blocks, flags)


def project_kernel(
    sources, groups, kv_local, per_group, place_ref, normed_ref, cos_ref, sin_ref, flags_ref, *refs
):
    count = len(sources)
    pieces = refs[:count]
    upper, lower, keys, values, weights, projected, sem = refs[count:]
    half = upper.shape[0]
    copies = row_copies(sources, pieces, weights, sem.at[0], place_ref[0], place_ref[2], groups)
    for copy in copies:
        copy.start()
    new_rows = normed_ref.shape[0]
    chunk_rows = per_group * ROW_TILE
    first_row = lax.broadcasted_iota(jnp.int32, (EXTRA, 1), 0) == 0
    bias = jnp.where((flags_ref[...] > -FAR) | jnp.logical_not(first_row), 0.0, FLOOR_SCORE)
    marker = jnp.where(
        lax.broadcasted_iota(jnp.int32, (chunk_rows, EXTRA), 1) == 0, 1.0, 0.0
    ).astype(jnp.bfloat16)
    for head in range(kv_local):
        keys[head, HD:, :] = bias.astype(jnp.bfloat16)
        for chunk in range(half):
            upper[chunk, head, :, HD:] = marker
            lower[chunk, head, :, HD:] = marker
    for copy in copies:
        copy.wait()
    width = weights.shape[1]
    for first in range(0, width, 2 * TILE):
        columns = slice(first, min(first + 2 * TILE, width))
        projected[:, columns] = jnp.dot(
            normed_ref[...], weights[:, columns], preferred_element_type=jnp.float32
        )

    def rotated(rows, column):
        part = projected[rows, column : column + HD]
        turned = jnp.concatenate([part[:, HD // 2 :], part[:, : HD // 2]], axis=1)
        return part * cos_ref[rows, :] + turned * sin_ref[rows, :]

    query_width = kv_local * per_group * HD
    for chunk in range(new_rows // ROW_TILE):
        rows = pl.ds(chunk * ROW_TILE, ROW_TILE)
        for head in range(kv_local):
            for sub in range(per_group):
                queries = upper if chunk < half else lower
                queries[chunk % half, head, sub * ROW_TILE : (sub + 1) * ROW_TILE, :HD] = rotated(
                    rows, (head * per_group + sub) * HD
                ).astype(jnp.bfloat16)
            keys[head, :HD, rows] = rotated(rows, query_width + head * HD).T.astype(jnp.bfloat16)
            column = query_width + (kv_local + head) * HD
            values[head, rows, :] = projected[rows, column : column + HD].astype(jnp.bfloat16)


def project_rows(place, normed, tables, flags, sources, groups, kv_local, per_group):
    new_rows = normed.shape[0]
    arrays = [values for _, _, values in sources]
    width = arrays[0].shape[1]
    queries = jax.ShapeDtypeStruct(
        (new_rows // ROW_TILE // 2, kv_local, per_group * ROW_TILE, HD + EXTRA), jnp.bfloat16
    )
    upper, lower, keys, values = pl.pallas_call(
        functools.partial(project_kernel, sources, groups, kv_local, per_group),
        out_shape=(
            queries,
            queries,
            jax.ShapeDtypeStruct((kv_local, HD + EXTRA, new_rows), jnp.bfloat16),
            jax.ShapeDtypeStruct((kv_local, new_rows, HD), jnp.bfloat16),
        ),
        in_specs=[SMEM] + [VMEM] * 4 + [ANY] * len(arrays),
        out_specs=(VMEM,) * 4,
        scratch_shapes=[
            pltpu.VMEM((normed.shape[1], width), jnp.bfloat16),
            pltpu.VMEM((new_rows, width), jnp.float32),
            pltpu.SemaphoreType.DMA((1,)),
        ],
        compiler_params=pltpu.CompilerParams(vmem_limit_bytes=VMEM_LIMIT),
        cost_estimate=pl.CostEstimate(
            flops=2 * new_rows * normed.shape[1] * width,
            bytes_accessed=2 * normed.shape[1] * width,
            transcendentals=0,
        ),
        name="project",
    )(place, normed, *tables, flags, *arrays)
    return (upper, lower), (keys, values)


def attention_kernel(
    first_step,
    place_ref,
    queries,
    cached_keys,
    cached_values,
    own_keys,
    own_values,
    cached_ref,
    own_ref,
    out_ref,
    scores,
    probs,
    folded,
    shifts,
    summed,
):
    prefix_here = place_ref[1]
    kv_local, _, cached = cached_keys.shape
    new_rows = own_keys.shape[2]
    chunk_rows = queries.shape[2]
    per_group = chunk_rows // ROW_TILE
    factor = math.log2(math.e) / math.sqrt(HD)
    group = 64
    widest = min(4 * LANES, cached)
    tiles = [
        (first, cached_keys, cached_values, first, widest) for first in range(0, cached, widest)
    ]
    tiles.append((cached, own_keys, own_values, 0, new_rows))

    def score(step, head, first, keys, _, begin, width):
        scores[head, :, pl.ds(first, width)] = jnp.dot(
            queries[step, head],
            keys[head, :, pl.ds(begin, width)],
            preferred_element_type=jnp.float32,
        )
        own = keys is own_keys
        for part in range(chunk_rows // group):
            rows = pl.ds(part * group, group)
            if own:
                row_id = (first_step + step) * ROW_TILE + (part * group) % ROW_TILE + (
                    lax.broadcasted_iota(jnp.int32, (group, LANES), 0)
                )
            top = folded[head, rows, :]
            for lane in range(0, width, LANES):
                place = pl.ds(first + lane, LANES)
                piece = scores[head, rows, place]
                if own:
                    own_id = lane + lax.broadcasted_iota(jnp.int32, (group, LANES), 1)
                    piece = jnp.where(own_id <= row_id, piece, FLOOR_SCORE)
                    scores[head, rows, place] = piece
                top = jnp.maximum(top, piece)
            folded[head, rows, :] = top

    def narrow(step, head):
        def some(part, inner):
            rows = pl.ds(pl.multiple_of(part * 16, 16), 16)
            row_id = (first_step + step) * ROW_TILE + lax.rem(part * 16, ROW_TILE) + (
                lax.broadcasted_iota(jnp.int32, (16, 1), 0)
            )
            oldest = prefix_here + row_id - WINDOW
            old = jnp.where(cached_ref[...] > oldest, scores[head, rows, :cached], FLOOR_SCORE)
            new = jnp.where(own_ref[...] > oldest, scores[head, rows, cached:], FLOOR_SCORE)
            scores[head, rows, :cached] = old
            scores[head, rows, cached:] = new
            top = jnp.maximum(
                jnp.max(old, axis=1, keepdims=True), jnp.max(new, axis=1, keepdims=True)
            )
            folded[head, rows, :] = jnp.broadcast_to(top, (16, LANES))
            return inner

        lax.fori_loop(0, chunk_rows // 16, some, 0)

    def weigh(head, start, first, _, values, begin, width):
        for part in range(chunk_rows // group):
            rows = pl.ds(part * group, group)
            shift = shifts[head, rows, :]
            total = None if start else folded[head, rows, :]
            for lane in range(0, width, LANES):
                place = pl.ds(first + lane, LANES)
                piece = jnp.exp2(scores[head, rows, place] * factor - shift)
                total = piece if total is None else total + piece
                probs[head, rows, place] = piece.astype(jnp.bfloat16)
            folded[head, rows, :] = total
        return jnp.dot(
            probs[head, :, pl.ds(first, width)],
            values[head, pl.ds(begin, width), :],
            preferred_element_type=jnp.float32,
        )

    def attend(windowed, step, carry):
        for head in range(kv_local):
            folded[head] = jnp.full(folded.shape[1:], FLOOR_SCORE, jnp.float32)
            for tile in tiles:
                score(step, head, *tile)
        for head in range(kv_local):
            if windowed:
                narrow(step, head)
            for part in range(chunk_rows // group):
                rows = pl.ds(part * group, group)
                top = jnp.max(folded[head, rows, :], axis=1, keepdims=True) * factor
                shifts[head, rows, :] = jnp.broadcast_to(top, (group, LANES))
            for which, tile in enumerate(tiles):
                part = weigh(head, which == 0, *tile)
                summed[head] = part if which == 0 else summed[head] + part
            rows = pl.ds(pl.multiple_of(step * ROW_TILE, ROW_TILE), ROW_TILE)
            for sub in range(per_group):
                part = pl.ds(sub * ROW_TILE, ROW_TILE)
                total = jnp.sum(folded[head, part, :], axis=1, keepdims=True)
                column = (head * per_group + sub) * HD
                out_ref[rows, column : column + HD] = (summed[head, part, :] / total).astype(
                    jnp.bfloat16
                )
        return carry

    behind = prefix_here + new_rows > WINDOW
    for windowed in (False, True):

        @pl.when(behind == windowed)
        def _():
            lax.fori_loop(0, queries.shape[0], functools.partial(attend, windowed), 0)


def attend_rows(place, first_step, queries, cached, own, cached_pos, own_pos):
    chunks, kv_local, chunk_rows, _ = queries.shape
    span = cached_pos.shape[1] + own_pos.shape[1]
    heads = kv_local * chunk_rows // ROW_TILE
    new_rows = chunks * ROW_TILE
    return pl.pallas_call(
        functools.partial(attention_kernel, first_step),
        out_shape=jax.ShapeDtypeStruct((new_rows, heads * HD), jnp.bfloat16),
        in_specs=[SMEM] + [VMEM] * 7,
        out_specs=VMEM,
        scratch_shapes=[
            pltpu.VMEM((kv_local, chunk_rows, span), jnp.float32),
            pltpu.VMEM((kv_local, chunk_rows, span), jnp.bfloat16),
            pltpu.VMEM((kv_local, chunk_rows, LANES), jnp.float32),
            pltpu.VMEM((kv_local, chunk_rows, LANES), jnp.float32),
            pltpu.VMEM((kv_local, chunk_rows, HD), jnp.float32),
        ],
        compiler_params=pltpu.CompilerParams(vmem_limit_bytes=VMEM_LIMIT),
        cost_estimate=pl.CostEstimate(
            flops=8 * heads * new_rows * span * LANES,
            bytes_accessed=4 * span * LANES * kv_local,
            transcendentals=heads * new_rows * span,
        ),
        name="attention",
    )(place, queries, *cached, *own, cached_pos, own_pos)


def middle_kernel(sources, groups, place_ref, tokens_ref, gain_ref, *refs):
    parts = len(refs) - len(sources) - 7
    att = refs[:parts]
    own_ref = refs[parts]
    rest = refs[parts + 1 :]
    shares = rest[: len(sources)]
    normed_ref, residual_ref, gathered, weights, middle, sem = rest[len(sources) :]
    blk_index = place_ref[0]
    kv_index = place_ref[2]
    group_rows = own_ref.shape[0]
    new_rows, model = tokens_ref.shape
    tile = 2 * TILE
    loads = []
    for step in range(model // tile):
        columns = pl.ds(step * tile, tile)
        copies = []
        if shares[0].ndim == 3:
            copies.append((own_ref.at[:, columns], weights.at[pl.ds(0, group_rows), columns]))
            for (indices, _, _), ref in zip(sources, shares):
                part = ref.shape[1]
                for at, index in enumerate(indices):
                    first = pl.multiple_of((blk_index ^ index) * part, 16)
                    for other in range(1, groups):
                        lead = at * (groups - 1) + other - 1
                        rows = pl.ds(other * group_rows + first, part)
                        copies.append((ref.at[lead, :, columns], weights.at[rows, columns]))
        else:
            for other in range(groups):
                first = pl.multiple_of((kv_index ^ other) * group_rows, 16)
                rows = pl.ds(other * group_rows, group_rows)
                copies.append(
                    (shares[0].at[pl.ds(first, group_rows), columns], weights.at[rows, columns])
                )
        loads.append(
            [pltpu.make_async_copy(source, target, sem.at[step]) for source, target in copies]
        )
        for copy in loads[-1]:
            copy.start()
    some_rows, feature = att[0].shape
    for at, part in enumerate(att):
        first, other = at // groups * some_rows, at % groups
        gathered[first : first + some_rows, other * feature : (other + 1) * feature] = part[...]
    for step in range(model // tile):
        columns = pl.ds(step * tile, tile)
        for copy in loads[step]:
            copy.wait()
        summed = jnp.dot(gathered[...], weights[:, columns], preferred_element_type=jnp.float32)
        middle[:, columns] = (tokens_ref[:, columns].astype(jnp.float32) + summed).astype(
            jnp.bfloat16
        )

    def scale(step, carry):
        rows = pl.ds(pl.multiple_of(step * 16, 16), 16)
        part = middle[rows, :].astype(jnp.float32)
        mean_square = jnp.mean(part * part, axis=1, keepdims=True)
        normed_ref[rows, :] = (part * lax.rsqrt(mean_square + EPSILON) * gain_ref[...]).astype(
            jnp.bfloat16
        )
        return carry

    lax.fori_loop(0, new_rows // 16, scale, 0, unroll=2)
    out_width = model // groups

    def keep(columns):
        residual_ref[...] = middle[:, columns]

    on_columns(keep, kv_index, out_width, groups)


def middle_rows(place, tokens, gain, attended, own, sources, groups):
    new_rows, model = tokens.shape
    arrays = [values for _, _, values in sources]
    return pl.pallas_call(
        functools.partial(middle_kernel, sources, groups),
        out_shape=(
            jax.ShapeDtypeStruct((new_rows, model), jnp.bfloat16),
            jax.ShapeDtypeStruct((new_rows, model // groups), jnp.bfloat16),
        ),
        in_specs=[SMEM, VMEM, VMEM] + [VMEM] * len(attended) + [ANY] * (1 + len(arrays)),
        out_specs=(VMEM, VMEM),
        scratch_shapes=[
            pltpu.VMEM((new_rows, model), jnp.bfloat16),
            pltpu.VMEM((model, model), jnp.bfloat16),
            pltpu.VMEM((new_rows, model), jnp.bfloat16),
            pltpu.SemaphoreType.DMA((model // (2 * TILE),)),
        ],
        compiler_params=pltpu.CompilerParams(vmem_limit_bytes=VMEM_LIMIT),
        cost_estimate=pl.CostEstimate(
            flops=2 * new_rows * model * model,
            bytes_accessed=2 * model * model,
            transcendentals=0,
        ),
        name="middle",
    )(place, tokens, gain, *attended, own, *arrays)


def hidden_chunks(width):
    return [(first, min(TILE, width - first)) for first in range(0, width, TILE)]


def mlp_kernel(groups, widths, place_ref, normed_ref, down_ref, left, right, *refs):
    outs = refs[:groups]
    first_half, second_half, down, hidden, sems = refs[groups:]
    kv_index = place_ref[2]
    chunks = []
    base = 0
    for width, source, buffer in zip(widths, (left, right), (first_half, second_half)):
        for first, units in hidden_chunks(width):
            columns = pl.ds(2 * first, 2 * units)
            copy = pltpu.make_async_copy(
                source.at[:, columns], buffer.at[:, columns], sems.at[len(chunks)]
            )
            chunks.append((buffer, columns, base + first, units, copy))
        base += width
    last = pltpu.make_async_copy(down_ref, down, sems.at[len(chunks)])
    ahead = 3
    for _, _, _, _, copy in chunks[:ahead]:
        copy.start()
    for at, (buffer, columns, first, units, copy) in enumerate(chunks):
        copy.wait()
        if at + ahead < len(chunks):
            chunks[at + ahead][4].start()
        elif at + ahead == len(chunks):
            last.start()
        both = jnp.dot(normed_ref[...], buffer[:, columns], preferred_element_type=jnp.float32)
        gated, raised = both[:, :units], both[:, units:]
        hidden[:, first : first + units] = (gated / (1.0 + jnp.exp(-gated)) * raised).astype(
            jnp.bfloat16
        )
    last.wait()
    out_width = outs[0].shape[1]
    for other in range(groups):

        def product(columns, out=outs[other]):
            out[...] = jnp.dot(
                hidden[...], down[:, columns], preferred_element_type=jnp.float32
            ).astype(out.dtype)

        on_columns(product, kv_index ^ other, out_width, groups)


def mlp_parts(place, normed, w_down, left, right, groups, widths):
    new_rows, model = normed.shape
    out_width = model // groups
    return pl.pallas_call(
        functools.partial(mlp_kernel, groups, widths),
        out_shape=tuple(
            jax.ShapeDtypeStruct((new_rows, out_width), jnp.bfloat16 if other else jnp.float32)
            for other in range(groups)
        ),
        in_specs=[SMEM, VMEM, ANY, ANY, ANY],
        out_specs=(VMEM,) * groups,
        scratch_shapes=[
            pltpu.VMEM(left.shape, jnp.bfloat16),
            pltpu.VMEM(right.shape, jnp.bfloat16),
            pltpu.VMEM(w_down.shape, jnp.bfloat16),
            pltpu.VMEM((new_rows, w_down.shape[0]), jnp.bfloat16),
            pltpu.SemaphoreType.DMA((1 + sum(len(hidden_chunks(width)) for width in widths),)),
        ],
        compiler_params=pltpu.CompilerParams(vmem_limit_bytes=VMEM_LIMIT),
        cost_estimate=pl.CostEstimate(
            flops=6 * new_rows * model * w_down.shape[0],
            bytes_accessed=6 * model * w_down.shape[0],
            transcendentals=new_rows * w_down.shape[0],
        ),
        name="mlp",
    )(place, normed, w_down, left, right)


def shards(
    tokens,
    attn_gain,
    mlp_gain,
    w_query,
    w_key,
    w_value,
    w_gate,
    w_up,
    w_out,
    w_down,
    cache,
    slot_prompt,
    prefix_len,
    new_len,
):
    groups = lax.axis_size("kv")
    blk_index = lax.axis_index("blk")
    kv_index = lax.axis_index("kv")
    query_width = w_query.shape[1] // groups
    key_width = w_key.shape[1] // groups
    per_group = HEADS // KV_HEADS
    new_rows = tokens.shape[0]
    prompts = prefix_len.shape[0]
    slots = cache.shape[1]
    prefix_here = prefix_len[blk_index]
    live_count = new_len[blk_index]
    place = jnp.stack([blk_index, prefix_here, kv_index]).astype(jnp.int32)

    global_rank, local_rank = slot_ranks(slot_prompt, prompts, slots)
    own_prompts = lax.dynamic_slice_in_dim(slot_prompt, blk_index * slots, slots)
    own_ranks = lax.dynamic_slice_in_dim(local_rank, blk_index * slots, slots)
    placed = own_prompts * CAP + own_ranks
    buffer_ids = jnp.arange(prompts * CAP, dtype=jnp.int32)
    matches = placed[None, :] == buffer_ids[:, None]
    source_slot = jnp.sum(
        jnp.where(matches, jnp.arange(slots, dtype=jnp.int32)[None, :], 0), axis=1
    )
    outgoing = jnp.take(cache, source_slot, axis=1)
    arrived = lax.all_to_all(outgoing, "blk", split_axis=1, concat_axis=1, tiled=True)
    slot_ids = jnp.arange(prompts * slots, dtype=jnp.int32)
    landing = slot_ids // slots * CAP + local_rank
    for_me = slot_prompt == blk_index
    received = (landing[None, :] == buffer_ids[:, None]) & for_me[None, :]
    block_number = jnp.sum(jnp.where(received, global_rank[None, :], 0), axis=1)
    block_live = jnp.any(received, axis=1)
    key_pos = block_number[:, None] * BLOCK + jnp.arange(BLOCK, dtype=jnp.int32)[None, :]
    key_live = block_live[:, None] & (key_pos < prefix_here)
    cached_pos = jnp.where(key_live, jnp.where(key_pos < SINKS, FAR, key_pos), -FAR)
    cached_pos = cached_pos.reshape(1, -1)
    row_ids = jnp.arange(new_rows, dtype=jnp.int32)
    positions = prefix_here + row_ids
    own_pos = jnp.where(
        row_ids < live_count, jnp.where(positions < SINKS, FAR, positions), -FAR
    ).reshape(1, -1)

    normed = rms_scale(tokens, attn_gain)
    tables = rope_tables(positions)
    cached = cached_rows(arrived, cached_pos)

    hidden_width = w_gate.shape[1] // groups
    cut = hidden_width // (2 * TILE) * TILE
    widths = (cut, hidden_width - cut)
    layouts = []
    base = 0
    for width in widths:
        layout = []
        for first, units in hidden_chunks(width):
            start = base + first
            layout += [(0, start, start + units), (1, start, start + units)]
        layouts.append(layout)
        base += width
    packed = pack((w_gate, w_up), groups, layouts, "pack_pair")

    in_place = lax.axis_size("blk") == 8 and w_query.shape[0] % 16 == 0
    eighth = w_out.shape[0] // lax.axis_size("blk")
    spread = in_place and eighth % 16 == 0
    if spread:
        share = lax.dynamic_slice_in_dim(w_out, blk_index * eighth, eighth, 0)
        shares = lax.all_gather(share, "kv", axis=0)

    spans = [(0, 0, query_width), (1, 0, key_width), (2, 0, key_width)]
    (qkv_parts,) = pack((w_query, w_key, w_value), groups, [spans], "pack_qkv")
    if in_place:
        moved_qkv = exchange(qkv_parts)
        meanwhile = (place, normed, *tables, own_pos, cached_pos, *cached)
        qkv = plane_gather(after(moved_qkv, packed[0][0]), meanwhile, [shares] if spread else [])
        settled = [values for _, _, values in qkv]
        across = settled[3:5]
    else:
        moved_qkv = exchange_in_order(qkv_parts, kv_index)
        qkv = [(None, 0, lax.all_gather(moved_qkv, "blk", axis=0, tiled=True))]
        settled = across = [moved_qkv]

    if spread:
        others = jnp.arange(1, groups, dtype=jnp.int32) ^ kv_index
        shares = after(jnp.take(shares, others, axis=0), *settled)
        near = (swap(shares, "blk", 2), swap(shares, "blk", 4))

    moved = exchange_in_order(after(packed[0], moved_qkv, arrived), kv_index)
    first_half = lax.all_gather(after(moved, *across), "blk", axis=0, tiled=True)
    moved_second = exchange_in_order(after(packed[1], *settled), kv_index)

    queries, own = project_rows(
        place, normed, tables, own_pos, qkv, groups, cache.shape[2], per_group
    )
    half = queries[0].shape[0]
    upper = attend_rows(place, 0, queries[0], cached, own, cached_pos, own_pos)
    lower = attend_rows(place, half, queries[1], cached, own, cached_pos, own_pos)
    earlier = (upper, lower, *near) if spread else (upper, lower)
    second_half = lax.all_gather(after(moved_second, *earlier), "blk", axis=0, tiled=True)
    attended = jnp.concatenate([upper, lower], axis=0)
    everyone = [attended] + [swap(attended, "kv", other) for other in range(1, groups)]

    if spread:
        by_x, by_y = near
        by_y = after(by_y, upper, lower)
        diagonal = swap(by_y, "blk", 2)
        trio = swap(jnp.concatenate([shares, by_x, by_y], axis=0), "blk", 1)
        w_out_sources = [
            ((0,), 0, shares),
            ((2,), 0, by_x),
            ((4,), 0, by_y),
            ((6,), 0, diagonal),
            ((1, 3, 5), 0, trio),
            ((7,), 0, swap(diagonal, "blk", 1)),
        ]
    else:
        w_out_sources = [(0, 0, lax.all_gather(w_out, "kv", axis=0, tiled=True))]

    normed_mid, residual = middle_rows(
        place, tokens, mlp_gain.reshape(1, -1), everyone, w_out, w_out_sources, groups
    )
    parts = mlp_parts(place, normed_mid, w_down, first_half, second_half, groups, widths)
    reduced = parts[0]
    for other in range(1, groups):
        reduced = reduced + swap(parts[other], "kv", other).astype(jnp.float32)
    mixed = jnp.where(
        (row_ids < live_count)[:, None], residual.astype(jnp.float32) + reduced, 0.0
    )
    return mixed.astype(jnp.bfloat16)


def solution(mesh):
    return jax.shard_map(
        shards,
        mesh=mesh,
        in_specs=(
            P("blk", None),
            P(),
            P(),
            P(("blk", "kv"), None),
            P(("blk", "kv"), None),
            P(("blk", "kv"), None),
            P(("blk", "kv"), None),
            P(("blk", "kv"), None),
            P("kv", None),
            P("kv", None),
            P(None, "blk", "kv", None, None),
            P(),
            P(),
            P(),
        ),
        out_specs=P("blk", "kv"),
        check_vma=False,
    )
```

```python
import functools
import math

import jax
import jax.numpy as jnp
from jax import lax
from jax.experimental import pallas as pl
from jax.experimental.pallas import tpu as pltpu
from jax.sharding import PartitionSpec as P

HEADS = 32
KV_HEADS = 8
HD = 80
WINDOW = 4096
SINKS = 4
BLOCK = 128
CAP = 2


FLOOR_SCORE = -1e30
EPSILON = 1e-05
ROPE_BASE = 10000.0
FAR = 1 << 30
LANES = 128
TILE = 256
ROW_TILE = 128
VMEM_LIMIT = 56 * 1024 * 1024

ANY = pl.BlockSpec(memory_space=pl.ANY)
VMEM = pl.BlockSpec(memory_space=pltpu.VMEM)
SMEM = pl.BlockSpec(memory_space=pltpu.SMEM)


def rms_scale(row_data, gain_vec):
    values = row_data.astype(jnp.float32)
    mean_square = jnp.mean(values * values, axis=-1, keepdims=True)
    return (values * lax.rsqrt(mean_square + EPSILON) * gain_vec).astype(jnp.bfloat16)


def rope_tables(positions):
    half_width = HD // 2
    frequency = ROPE_BASE ** (-2.0 * jnp.arange(half_width, dtype=jnp.float32) / HD)
    angles = positions.astype(jnp.float32)[:, None] * frequency[None, :]
    cosine = jnp.cos(angles)
    sine = jnp.sin(angles)
    return (
        jnp.concatenate([cosine, cosine], axis=1),
        jnp.concatenate([-sine, sine], axis=1),
    )


def slot_ranks(slot_prompt, prompts, slots):
    onehot = (slot_prompt[:, None] == jnp.arange(prompts, dtype=jnp.int32)[None, :]).astype(
        jnp.int32
    )
    running = jnp.cumsum(onehot, axis=0)
    global_rank = jnp.sum(onehot * (running - 1), axis=1)
    local_count = jnp.cumsum(onehot.reshape(-1, slots, prompts), axis=1).reshape(-1, prompts)
    local_rank = jnp.sum(onehot * (local_count - 1), axis=1)
    return (global_rank, local_rank)


def swap(values, axis, bit):
    pairs = [(index, index ^ bit) for index in range(lax.axis_size(axis))]
    return lax.ppermute(values, axis, pairs)


def half_up(width):
    return (width // 2 + LANES - 1) // LANES * LANES


def pack_kernel(layouts, groups, *refs):
    kv_index = lax.axis_index("kv")
    outs = refs[len(refs) - groups * len(layouts) :]
    for choice in range(groups):

        @pl.when(kv_index == choice)
        def _():
            for which, spans in enumerate(layouts):
                for other in range(groups):
                    out = outs[which * groups + other]
                    column = 0
                    for matrix, first, last in spans:
                        start = (choice ^ other) * (refs[matrix].shape[1] // groups)
                        width = last - first
                        out[:, column : column + width] = refs[matrix][
                            :, start + first : start + last
                        ].astype(jnp.bfloat16)
                        column += width


def pack(matrices, groups, layouts, name):
    rows = matrices[0].shape[0]
    shapes = []
    for spans in layouts:
        width = sum(last - first for _, first, last in spans)
        shapes += [jax.ShapeDtypeStruct((rows, width), jnp.bfloat16)] * groups
    flat = pl.pallas_call(
        functools.partial(pack_kernel, layouts, groups),
        out_shape=tuple(shapes),
        in_specs=[VMEM] * len(matrices),
        out_specs=(VMEM,) * len(shapes),
        compiler_params=pltpu.CompilerParams(vmem_limit_bytes=VMEM_LIMIT),
        cost_estimate=pl.CostEstimate(
            flops=0,
            bytes_accessed=6 * rows * sum(matrix.shape[1] for matrix in matrices),
            transcendentals=0,
        ),
        name=name,
    )(*matrices)
    return [flat[first : first + groups] for first in range(0, len(flat), groups)]


def exchange(parts):
    moved = [parts[0]] + [swap(part, "kv", other) for other, part in enumerate(parts) if other]
    return jnp.concatenate(moved, axis=0)


def exchange_in_order(parts, kv_index):
    moved = jnp.stack(
        [parts[0]] + [swap(part, "kv", other) for other, part in enumerate(parts) if other], axis=0
    )
    order = jnp.arange(len(parts), dtype=jnp.int32) ^ kv_index
    return jnp.take(moved, order, axis=0).reshape(-1, moved.shape[2])


def after(values, *earlier):
    return lax.optimization_barrier((values, *earlier))[0]


def plane_gather(piece, meanwhile):
    rows = piece.shape[0]
    by_x = swap(piece, "blk", 2)
    by_y = swap(piece, "blk", 4)
    upper = swap(after(by_y[: rows // 2], *meanwhile), "blk", 2)
    lower = swap(after(by_x[rows // 2 :], *meanwhile), "blk", 4)
    near = jnp.concatenate([after(piece, upper, lower), by_x, by_y], axis=0)
    near = swap(near, "blk", 1)
    mine = [(0, 0, piece), (2, 0, by_x), (4, 0, by_y), (6, 0, upper), (6, rows // 2, lower)]
    other = [((1, 3, 5), 0, near)]
    other += [(index ^ 1, first, swap(part, "blk", 1)) for index, first, part in mine[3:]]
    return mine + other


def on_columns(body, index, width, count):
    if width % LANES == 0:
        body(pl.ds(pl.multiple_of(index * width, LANES), width))
        return
    for choice in range(count):
        pl.when(index == choice)(functools.partial(body, pl.ds(choice * width, width)))


def row_copies(sources, refs, buffer, sem, blk_index, kv_index, groups):
    copies = []
    total = buffer.shape[0]
    for (index, begin, _), ref in zip(sources, refs):
        rows = ref.shape[0]
        piece = total // 8
        block = piece // groups
        if rows == total and index is None:
            copies.append(pltpu.make_async_copy(ref, buffer, sem))
            continue
        for first in range(0, rows, block):
            piece_index = index[first // piece] if isinstance(index, tuple) else index
            other = (begin + first) % piece // block
            target = (blk_index ^ piece_index) * piece + (kv_index ^ other) * block
            copies.append(
                pltpu.make_async_copy(
                    ref.at[pl.ds(first, block)],
                    buffer.at[pl.ds(pl.multiple_of(target, 16), block)],
                    sem,
                )
            )
    return copies


EXTRA = 16


def cache_kernel(blocks_ref, flags_ref, keys, values):
    first_row = lax.broadcasted_iota(jnp.int32, (EXTRA, 1), 0) == 0
    bias = jnp.where((flags_ref[...] > -FAR) | jnp.logical_not(first_row), 0.0, FLOOR_SCORE)
    for head in range(blocks_ref.shape[2]):
        keys[head, HD:, :] = bias.astype(jnp.bfloat16)
        for block in range(blocks_ref.shape[1]):
            place = pl.ds(block * BLOCK, BLOCK)
            keys[head, :HD, place] = blocks_ref[0, block, head]
            values[head, place, :] = blocks_ref[1, block, head].astype(jnp.float32).T.astype(
                jnp.bfloat16
            )


def cached_rows(blocks, flags):
    kv_local = blocks.shape[2]
    cached = flags.shape[1]
    return pl.pallas_call(
        cache_kernel,
        out_shape=(
            jax.ShapeDtypeStruct((kv_local, HD + EXTRA, cached), jnp.bfloat16),
            jax.ShapeDtypeStruct((kv_local, cached, HD), jnp.bfloat16),
        ),
        in_specs=[VMEM, VMEM],
        out_specs=(VMEM, VMEM),
        compiler_params=pltpu.CompilerParams(vmem_limit_bytes=VMEM_LIMIT),
        cost_estimate=pl.CostEstimate(
            flops=0, bytes_accessed=4 * blocks.size, transcendentals=0
        ),
        name="cached",
    )(blocks, flags)


def project_kernel(
    sources, groups, kv_local, per_group, place_ref, normed_ref, cos_ref, sin_ref, flags_ref, *refs
):
    count = len(sources)
    pieces = refs[:count]
    upper, lower, keys, values, weights, projected, sem = refs[count:]
    half = upper.shape[0]
    copies = row_copies(sources, pieces, weights, sem.at[0], place_ref[0], place_ref[2], groups)
    for copy in copies:
        copy.start()
    new_rows = normed_ref.shape[0]
    chunk_rows = per_group * ROW_TILE
    first_row = lax.broadcasted_iota(jnp.int32, (EXTRA, 1), 0) == 0
    bias = jnp.where((flags_ref[...] > -FAR) | jnp.logical_not(first_row), 0.0, FLOOR_SCORE)
    marker = jnp.where(
        lax.broadcasted_iota(jnp.int32, (chunk_rows, EXTRA), 1) == 0, 1.0, 0.0
    ).astype(jnp.bfloat16)
    for head in range(kv_local):
        keys[head, HD:, :] = bias.astype(jnp.bfloat16)
        for chunk in range(half):
            upper[chunk, head, :, HD:] = marker
            lower[chunk, head, :, HD:] = marker
    for copy in copies:
        copy.wait()
    width = weights.shape[1]
    for first in range(0, width, 2 * TILE):
        columns = slice(first, min(first + 2 * TILE, width))
        projected[:, columns] = jnp.dot(
            normed_ref[...], weights[:, columns], preferred_element_type=jnp.float32
        )

    def rotated(rows, column):
        part = projected[rows, column : column + HD]
        turned = jnp.concatenate([part[:, HD // 2 :], part[:, : HD // 2]], axis=1)
        return part * cos_ref[rows, :] + turned * sin_ref[rows, :]

    query_width = kv_local * per_group * HD
    for chunk in range(new_rows // ROW_TILE):
        rows = pl.ds(chunk * ROW_TILE, ROW_TILE)
        for head in range(kv_local):
            for sub in range(per_group):
                queries = upper if chunk < half else lower
                queries[chunk % half, head, sub * ROW_TILE : (sub + 1) * ROW_TILE, :HD] = rotated(
                    rows, (head * per_group + sub) * HD
                ).astype(jnp.bfloat16)
            keys[head, :HD, rows] = rotated(rows, query_width + head * HD).T.astype(jnp.bfloat16)
            column = query_width + (kv_local + head) * HD
            values[head, rows, :] = projected[rows, column : column + HD].astype(jnp.bfloat16)


def project_rows(place, normed, tables, flags, sources, groups, kv_local, per_group):
    new_rows = normed.shape[0]
    arrays = [values for _, _, values in sources]
    width = arrays[0].shape[1]
    queries = jax.ShapeDtypeStruct(
        (new_rows // ROW_TILE // 2, kv_local, per_group * ROW_TILE, HD + EXTRA), jnp.bfloat16
    )
    upper, lower, keys, values = pl.pallas_call(
        functools.partial(project_kernel, sources, groups, kv_local, per_group),
        out_shape=(
            queries,
            queries,
            jax.ShapeDtypeStruct((kv_local, HD + EXTRA, new_rows), jnp.bfloat16),
            jax.ShapeDtypeStruct((kv_local, new_rows, HD), jnp.bfloat16),
        ),
        in_specs=[SMEM] + [VMEM] * 4 + [ANY] * len(arrays),
        out_specs=(VMEM,) * 4,
        scratch_shapes=[
            pltpu.VMEM((normed.shape[1], width), jnp.bfloat16),
            pltpu.VMEM((new_rows, width), jnp.float32),
            pltpu.SemaphoreType.DMA((1,)),
        ],
        compiler_params=pltpu.CompilerParams(vmem_limit_bytes=VMEM_LIMIT),
        cost_estimate=pl.CostEstimate(
            flops=2 * new_rows * normed.shape[1] * width,
            bytes_accessed=2 * normed.shape[1] * width,
            transcendentals=0,
        ),
        name="project",
    )(place, normed, *tables, flags, *arrays)
    return (upper, lower), (keys, values)


def attention_kernel(
    first_step,
    place_ref,
    queries,
    cached_keys,
    cached_values,
    own_keys,
    own_values,
    cached_ref,
    own_ref,
    out_ref,
    scores,
    probs,
    folded,
    shifts,
    summed,
):
    prefix_here = place_ref[1]
    kv_local, _, cached = cached_keys.shape
    new_rows = own_keys.shape[2]
    chunk_rows = queries.shape[2]
    per_group = chunk_rows // ROW_TILE
    factor = math.log2(math.e) / math.sqrt(HD)
    group = 64
    widest = min(4 * LANES, cached)
    tiles = [
        (first, cached_keys, cached_values, first, widest) for first in range(0, cached, widest)
    ]
    tiles.append((cached, own_keys, own_values, 0, new_rows))

    def score(step, head, first, keys, _, begin, width):
        scores[head, :, pl.ds(first, width)] = jnp.dot(
            queries[step, head],
            keys[head, :, pl.ds(begin, width)],
            preferred_element_type=jnp.float32,
        )
        own = keys is own_keys
        for part in range(chunk_rows // group):
            rows = pl.ds(part * group, group)
            if own:
                row_id = (first_step + step) * ROW_TILE + (part * group) % ROW_TILE + (
                    lax.broadcasted_iota(jnp.int32, (group, LANES), 0)
                )
            top = folded[head, rows, :]
            for lane in range(0, width, LANES):
                place = pl.ds(first + lane, LANES)
                piece = scores[head, rows, place]
                if own:
                    own_id = lane + lax.broadcasted_iota(jnp.int32, (group, LANES), 1)
                    piece = jnp.where(own_id <= row_id, piece, FLOOR_SCORE)
                    scores[head, rows, place] = piece
                top = jnp.maximum(top, piece)
            folded[head, rows, :] = top

    def narrow(step, head):
        def some(part, inner):
            rows = pl.ds(pl.multiple_of(part * 16, 16), 16)
            row_id = (first_step + step) * ROW_TILE + lax.rem(part * 16, ROW_TILE) + (
                lax.broadcasted_iota(jnp.int32, (16, 1), 0)
            )
            oldest = prefix_here + row_id - WINDOW
            old = jnp.where(cached_ref[...] > oldest, scores[head, rows, :cached], FLOOR_SCORE)
            new = jnp.where(own_ref[...] > oldest, scores[head, rows, cached:], FLOOR_SCORE)
            scores[head, rows, :cached] = old
            scores[head, rows, cached:] = new
            top = jnp.maximum(
                jnp.max(old, axis=1, keepdims=True), jnp.max(new, axis=1, keepdims=True)
            )
            folded[head, rows, :] = jnp.broadcast_to(top, (16, LANES))
            return inner

        lax.fori_loop(0, chunk_rows // 16, some, 0)

    def weigh(head, start, first, _, values, begin, width):
        for part in range(chunk_rows // group):
            rows = pl.ds(part * group, group)
            shift = shifts[head, rows, :]
            total = None if start else folded[head, rows, :]
            for lane in range(0, width, LANES):
                place = pl.ds(first + lane, LANES)
                piece = jnp.exp2(scores[head, rows, place] * factor - shift)
                total = piece if total is None else total + piece
                probs[head, rows, place] = piece.astype(jnp.bfloat16)
            folded[head, rows, :] = total
        return jnp.dot(
            probs[head, :, pl.ds(first, width)],
            values[head, pl.ds(begin, width), :],
            preferred_element_type=jnp.float32,
        )

    def attend(windowed, step, carry):
        for head in range(kv_local):
            folded[head] = jnp.full(folded.shape[1:], FLOOR_SCORE, jnp.float32)
            for tile in tiles:
                score(step, head, *tile)
        for head in range(kv_local):
            if windowed:
                narrow(step, head)
            for part in range(chunk_rows // group):
                rows = pl.ds(part * group, group)
                top = jnp.max(folded[head, rows, :], axis=1, keepdims=True) * factor
                shifts[head, rows, :] = jnp.broadcast_to(top, (group, LANES))
            for which, tile in enumerate(tiles):
                part = weigh(head, which == 0, *tile)
                summed[head] = part if which == 0 else summed[head] + part
            rows = pl.ds(pl.multiple_of(step * ROW_TILE, ROW_TILE), ROW_TILE)
            for sub in range(per_group):
                part = pl.ds(sub * ROW_TILE, ROW_TILE)
                total = jnp.sum(folded[head, part, :], axis=1, keepdims=True)
                column = (head * per_group + sub) * HD
                out_ref[rows, column : column + HD] = (summed[head, part, :] / total).astype(
                    jnp.bfloat16
                )
        return carry

    behind = prefix_here + new_rows > WINDOW
    for windowed in (False, True):

        @pl.when(behind == windowed)
        def _():
            lax.fori_loop(0, queries.shape[0], functools.partial(attend, windowed), 0)


def attend_rows(place, first_step, queries, cached, own, cached_pos, own_pos):
    chunks, kv_local, chunk_rows, _ = queries.shape
    span = cached_pos.shape[1] + own_pos.shape[1]
    heads = kv_local * chunk_rows // ROW_TILE
    new_rows = chunks * ROW_TILE
    return pl.pallas_call(
        functools.partial(attention_kernel, first_step),
        out_shape=jax.ShapeDtypeStruct((new_rows, heads * HD), jnp.bfloat16),
        in_specs=[SMEM] + [VMEM] * 7,
        out_specs=VMEM,
        scratch_shapes=[
            pltpu.VMEM((kv_local, chunk_rows, span), jnp.float32),
            pltpu.VMEM((kv_local, chunk_rows, span), jnp.bfloat16),
            pltpu.VMEM((kv_local, chunk_rows, LANES), jnp.float32),
            pltpu.VMEM((kv_local, chunk_rows, LANES), jnp.float32),
            pltpu.VMEM((kv_local, chunk_rows, HD), jnp.float32),
        ],
        compiler_params=pltpu.CompilerParams(vmem_limit_bytes=VMEM_LIMIT),
        cost_estimate=pl.CostEstimate(
            flops=8 * heads * new_rows * span * LANES,
            bytes_accessed=4 * span * LANES * kv_local,
            transcendentals=heads * new_rows * span,
        ),
        name="attention",
    )(place, queries, *cached, *own, cached_pos, own_pos)


def out_kernel(groups, upper_ref, lower_ref, weights_ref, *refs):
    outs, rows_ref = refs[:groups], refs[groups]
    kv_index = lax.axis_index("kv")
    half = upper_ref.shape[0]
    count = 2 * half // groups
    for choice in range(groups):

        @pl.when(kv_index == choice)
        def _():
            for other in range(groups):
                first = (choice ^ other) * count
                source = upper_ref if first < half else lower_ref
                rows_ref[other * count : (other + 1) * count, :] = source[
                    first % half : first % half + count, :
                ]

    for column in range(0, weights_ref.shape[1], 2 * TILE):
        columns = slice(column, column + 2 * TILE)
        product = jnp.dot(
            rows_ref[...], weights_ref[:, columns], preferred_element_type=jnp.float32
        )
        for other in range(groups):
            outs[other][:, columns] = product[other * count : (other + 1) * count].astype(
                outs[other].dtype
            )


def out_terms(upper, lower, w_out, groups):
    rows, feature = 2 * upper.shape[0], upper.shape[1]
    model = w_out.shape[1]
    return pl.pallas_call(
        functools.partial(out_kernel, groups),
        out_shape=tuple(
            jax.ShapeDtypeStruct((rows // groups, model), jnp.bfloat16 if other else jnp.float32)
            for other in range(groups)
        ),
        in_specs=[VMEM] * 3,
        out_specs=(VMEM,) * groups,
        scratch_shapes=[pltpu.VMEM((rows, feature), jnp.bfloat16)],
        compiler_params=pltpu.CompilerParams(vmem_limit_bytes=VMEM_LIMIT),
        cost_estimate=pl.CostEstimate(
            flops=2 * rows * feature * model, bytes_accessed=2 * feature * model, transcendentals=0
        ),
        name="out",
    )(upper, lower, w_out)


def gather_groups(piece):
    groups = lax.axis_size("kv")
    pieces = {0: piece}
    for other in sorted(range(1, groups), key=lambda other: (bin(other).count("1"), -other)):
        low = other & -other
        pieces[other] = swap(pieces[other ^ low], "kv", low)
    return [pieces[other] for other in range(groups)]


def sum_at_owner(parts):
    parts = list(parts)
    for other in sorted(range(1, len(parts)), key=lambda other: -bin(other).count("1")):
        low = other & -other
        target = other ^ low
        came = swap(parts[other], "kv", low)
        added = parts[target].astype(jnp.float32) + came.astype(jnp.float32)
        parts[target] = added.astype(jnp.bfloat16) if target else added
    return parts[0]


def hidden_chunks(width):
    return [(first, min(TILE, width - first)) for first in range(0, width, TILE)]


def mlp_kernel(groups, widths, place_ref, gain_ref, down_ref, left, right, *refs):
    pieces = refs[:groups]
    outs = refs[groups : 2 * groups]
    residual_ref, normed_ref, first_half, second_half, down, hidden, sems = refs[2 * groups :]
    kv_index = place_ref[2]
    chunks = []
    base = 0
    for width, source, buffer in zip(widths, (left, right), (first_half, second_half)):
        for first, units in hidden_chunks(width):
            columns = pl.ds(2 * first, 2 * units)
            copy = pltpu.make_async_copy(
                source.at[:, columns], buffer.at[:, columns], sems.at[len(chunks)]
            )
            chunks.append((buffer, columns, base + first, units, copy))
        base += width
    last = pltpu.make_async_copy(down_ref, down, sems.at[len(chunks)])
    ahead = 3
    for _, _, _, _, copy in chunks[:ahead]:
        copy.start()
    count = pieces[0].shape[0]
    out_width = outs[0].shape[1]
    for other in range(groups):
        start = (kv_index ^ other) * count

        def scale(step, carry, piece=pieces[other], start=start):
            part = piece[pl.ds(pl.multiple_of(step * 16, 16), 16), :].astype(jnp.float32)
            mean_square = jnp.mean(part * part, axis=1, keepdims=True)
            place = pl.ds(pl.multiple_of(start + step * 16, 16), 16)
            normed_ref[place, :] = (
                part * lax.rsqrt(mean_square + EPSILON) * gain_ref[...]
            ).astype(jnp.bfloat16)
            return carry

        lax.fori_loop(0, count // 16, scale, 0, unroll=2)

        def keep(columns, piece=pieces[other], start=start):
            residual_ref[pl.ds(pl.multiple_of(start, 16), count), :] = piece[:, columns]

        on_columns(keep, kv_index, out_width, groups)
    for at, (buffer, columns, first, units, copy) in enumerate(chunks):
        copy.wait()
        if at + ahead < len(chunks):
            chunks[at + ahead][4].start()
        elif at + ahead == len(chunks):
            last.start()
        both = jnp.dot(normed_ref[...], buffer[:, columns], preferred_element_type=jnp.float32)
        gated, raised = both[:, :units], both[:, units:]
        hidden[:, first : first + units] = (gated / (1.0 + jnp.exp(-gated)) * raised).astype(
            jnp.bfloat16
        )
    last.wait()
    for other in range(groups):

        def product(columns, out=outs[other]):
            out[...] = jnp.dot(
                hidden[...], down[:, columns], preferred_element_type=jnp.float32
            ).astype(out.dtype)

        on_columns(product, kv_index ^ other, out_width, groups)


def mlp_parts(place, gain, middle, w_down, left, right, groups, widths):
    count, model = middle[0].shape
    new_rows = groups * count
    out_width = model // groups
    chunk_count = sum(len(hidden_chunks(width)) for width in widths)
    return pl.pallas_call(
        functools.partial(mlp_kernel, groups, widths),
        out_shape=tuple(
            jax.ShapeDtypeStruct((new_rows, out_width), jnp.bfloat16 if other else jnp.float32)
            for other in range(groups)
        )
        + (jax.ShapeDtypeStruct((new_rows, out_width), jnp.bfloat16),),
        in_specs=[SMEM, VMEM, ANY, ANY, ANY] + [VMEM] * groups,
        out_specs=(VMEM,) * (groups + 1),
        scratch_shapes=[
            pltpu.VMEM((new_rows, model), jnp.bfloat16),
            pltpu.VMEM(left.shape, jnp.bfloat16),
            pltpu.VMEM(right.shape, jnp.bfloat16),
            pltpu.VMEM(w_down.shape, jnp.bfloat16),
            pltpu.VMEM((new_rows, w_down.shape[0]), jnp.bfloat16),
            pltpu.SemaphoreType.DMA((1 + chunk_count,)),
        ],
        compiler_params=pltpu.CompilerParams(vmem_limit_bytes=VMEM_LIMIT),
        cost_estimate=pl.CostEstimate(
            flops=6 * new_rows * model * w_down.shape[0],
            bytes_accessed=6 * model * w_down.shape[0],
            transcendentals=new_rows * w_down.shape[0],
        ),
        name="mlp",
    )(place, gain, w_down, left, right, *middle)


def shards(
    tokens,
    attn_gain,
    mlp_gain,
    w_query,
    w_key,
    w_value,
    w_gate,
    w_up,
    w_out,
    w_down,
    cache,
    slot_prompt,
    prefix_len,
    new_len,
):
    groups = lax.axis_size("kv")
    blk_index = lax.axis_index("blk")
    kv_index = lax.axis_index("kv")
    query_width = w_query.shape[1] // groups
    key_width = w_key.shape[1] // groups
    per_group = HEADS // KV_HEADS
    new_rows = tokens.shape[0]
    prompts = prefix_len.shape[0]
    slots = cache.shape[1]
    prefix_here = prefix_len[blk_index]
    live_count = new_len[blk_index]
    place = jnp.stack([blk_index, prefix_here, kv_index]).astype(jnp.int32)

    global_rank, local_rank = slot_ranks(slot_prompt, prompts, slots)
    own_prompts = lax.dynamic_slice_in_dim(slot_prompt, blk_index * slots, slots)
    own_ranks = lax.dynamic_slice_in_dim(local_rank, blk_index * slots, slots)
    placed = own_prompts * CAP + own_ranks
    buffer_ids = jnp.arange(prompts * CAP, dtype=jnp.int32)
    matches = placed[None, :] == buffer_ids[:, None]
    source_slot = jnp.sum(
        jnp.where(matches, jnp.arange(slots, dtype=jnp.int32)[None, :], 0), axis=1
    )
    outgoing = jnp.take(cache, source_slot, axis=1)
    arrived = lax.all_to_all(outgoing, "blk", split_axis=1, concat_axis=1, tiled=True)
    slot_ids = jnp.arange(prompts * slots, dtype=jnp.int32)
    landing = slot_ids // slots * CAP + local_rank
    for_me = slot_prompt == blk_index
    received = (landing[None, :] == buffer_ids[:, None]) & for_me[None, :]
    block_number = jnp.sum(jnp.where(received, global_rank[None, :], 0), axis=1)
    block_live = jnp.any(received, axis=1)
    key_pos = block_number[:, None] * BLOCK + jnp.arange(BLOCK, dtype=jnp.int32)[None, :]
    key_live = block_live[:, None] & (key_pos < prefix_here)
    cached_pos = jnp.where(key_live, jnp.where(key_pos < SINKS, FAR, key_pos), -FAR)
    cached_pos = cached_pos.reshape(1, -1)
    row_ids = jnp.arange(new_rows, dtype=jnp.int32)
    positions = prefix_here + row_ids
    own_pos = jnp.where(
        row_ids < live_count, jnp.where(positions < SINKS, FAR, positions), -FAR
    ).reshape(1, -1)

    hidden_width = w_gate.shape[1] // groups
    cut = hidden_width // (2 * TILE) * TILE
    widths = (cut, hidden_width - cut)
    layouts = []
    base = 0
    for width in widths:
        layout = []
        for first, units in hidden_chunks(width):
            start = base + first
            layout += [(0, start, start + units), (1, start, start + units)]
        layouts.append(layout)
        base += width
    packed = pack((w_gate, w_up), groups, layouts, "pack_pair")

    in_place = lax.axis_size("blk") == 8 and w_query.shape[0] % 16 == 0
    spans = [(0, 0, query_width), (1, 0, key_width), (2, 0, key_width)]
    (qkv_parts,) = pack((w_query, w_key, w_value), groups, [spans], "pack_qkv")
    if in_place:
        moved_qkv = exchange(qkv_parts)
        tied_tokens, tied_positions = after((tokens, positions), moved_qkv)
        normed = rms_scale(tied_tokens, attn_gain)
        tables = rope_tables(tied_positions)
        meanwhile = (place, normed, *tables, own_pos, cached_pos, arrived)
        qkv = plane_gather(after(moved_qkv, packed[0][0]), meanwhile)
        settled = [values for _, _, values in qkv]
        across = settled[3:5]
    else:
        normed = rms_scale(tokens, attn_gain)
        tables = rope_tables(positions)
        moved_qkv = exchange_in_order(qkv_parts, kv_index)
        qkv = [(None, 0, lax.all_gather(moved_qkv, "blk", axis=0, tiled=True))]
        settled = across = [moved_qkv]

    cached = cached_rows(arrived, cached_pos)

    moved = exchange_in_order(after(packed[0], moved_qkv), kv_index)
    first_half = lax.all_gather(after(moved, *across), "blk", axis=0, tiled=True)
    moved_second = exchange_in_order(after(packed[1], *settled), kv_index)

    queries, own = project_rows(
        place, normed, tables, own_pos, qkv, groups, cache.shape[2], per_group
    )
    half = queries[0].shape[0]
    upper = attend_rows(place, 0, queries[0], cached, own, cached_pos, own_pos)
    lower = attend_rows(place, half, queries[1], cached, own, cached_pos, own_pos)
    second_half = lax.all_gather(after(moved_second, upper, lower), "blk", axis=0, tiled=True)

    summed = sum_at_owner(out_terms(upper, lower, w_out, groups))
    count = new_rows // groups
    own_rows = lax.dynamic_slice_in_dim(tokens, kv_index * count, count, 0)
    middle = (own_rows.astype(jnp.float32) + summed).astype(jnp.bfloat16)
    *parts, residual = mlp_parts(
        place,
        mlp_gain.reshape(1, -1),
        gather_groups(middle),
        w_down,
        first_half,
        second_half,
        groups,
        widths,
    )
    reduced = sum_at_owner(parts)
    mixed = jnp.where(
        (row_ids < live_count)[:, None], residual.astype(jnp.float32) + reduced, 0.0
    )
    return mixed.astype(jnp.bfloat16)


def solution(mesh):
    return jax.shard_map(
        shards,
        mesh=mesh,
        in_specs=(
            P("blk", None),
            P(),
            P(),
            P(("blk", "kv"), None),
            P(("blk", "kv"), None),
            P(("blk", "kv"), None),
            P(("blk", "kv"), None),
            P(("blk", "kv"), None),
            P("kv", None),
            P("kv", None),
            P(None, "blk", "kv", None, None),
            P(),
            P(),
            P(),
        ),
        out_specs=P("blk", "kv"),
        check_vma=False,
    )
```

```python
import functools
import math

import jax
import jax.numpy as jnp
from jax import lax
from jax.experimental import pallas as pl
from jax.experimental.pallas import tpu as pltpu
from jax.sharding import PartitionSpec as P

HEADS = 32
KV_HEADS = 8
HD = 80
WINDOW = 4096
SINKS = 4
BLOCK = 128
CAP = 2


FLOOR_SCORE = -1e30
EPSILON = 1e-05
ROPE_BASE = 10000.0
FAR = 1 << 30
LANES = 128
TILE = 256
ROW_TILE = 128
VMEM_LIMIT = 56 * 1024 * 1024

ANY = pl.BlockSpec(memory_space=pl.ANY)
VMEM = pl.BlockSpec(memory_space=pltpu.VMEM)
SMEM = pl.BlockSpec(memory_space=pltpu.SMEM)


def rms_scale(row_data, gain_vec):
    values = row_data.astype(jnp.float32)
    mean_square = jnp.mean(values * values, axis=-1, keepdims=True)
    return (values * lax.rsqrt(mean_square + EPSILON) * gain_vec).astype(jnp.bfloat16)


def rope_tables(positions):
    half_width = HD // 2
    frequency = ROPE_BASE ** (-2.0 * jnp.arange(half_width, dtype=jnp.float32) / HD)
    angles = positions.astype(jnp.float32)[:, None] * frequency[None, :]
    cosine = jnp.cos(angles)
    sine = jnp.sin(angles)
    return (
        jnp.concatenate([cosine, cosine], axis=1),
        jnp.concatenate([-sine, sine], axis=1),
    )


def slot_ranks(slot_prompt, prompts, slots):
    onehot = (slot_prompt[:, None] == jnp.arange(prompts, dtype=jnp.int32)[None, :]).astype(
        jnp.int32
    )
    running = jnp.cumsum(onehot, axis=0)
    global_rank = jnp.sum(onehot * (running - 1), axis=1)
    local_count = jnp.cumsum(onehot.reshape(-1, slots, prompts), axis=1).reshape(-1, prompts)
    local_rank = jnp.sum(onehot * (local_count - 1), axis=1)
    return (global_rank, local_rank)


def swap(values, axis, bit):
    pairs = [(index, index ^ bit) for index in range(lax.axis_size(axis))]
    return lax.ppermute(values, axis, pairs)


def half_up(width):
    return (width // 2 + LANES - 1) // LANES * LANES


def pack_kernel(layouts, groups, *refs):
    kv_index = lax.axis_index("kv")
    outs = refs[len(refs) - groups * len(layouts) :]
    for choice in range(groups):

        @pl.when(kv_index == choice)
        def _():
            for which, spans in enumerate(layouts):
                for other in range(groups):
                    out = outs[which * groups + other]
                    column = 0
                    for matrix, first, last in spans:
                        start = (choice ^ other) * (refs[matrix].shape[1] // groups)
                        width = last - first
                        out[:, column : column + width] = refs[matrix][
                            :, start + first : start + last
                        ].astype(jnp.bfloat16)
                        column += width


def pack(matrices, groups, layouts, name):
    rows = matrices[0].shape[0]
    shapes = []
    for spans in layouts:
        width = sum(last - first for _, first, last in spans)
        shapes += [jax.ShapeDtypeStruct((rows, width), jnp.bfloat16)] * groups
    flat = pl.pallas_call(
        functools.partial(pack_kernel, layouts, groups),
        out_shape=tuple(shapes),
        in_specs=[VMEM] * len(matrices),
        out_specs=(VMEM,) * len(shapes),
        compiler_params=pltpu.CompilerParams(vmem_limit_bytes=VMEM_LIMIT),
        cost_estimate=pl.CostEstimate(
            flops=0,
            bytes_accessed=6 * rows * sum(matrix.shape[1] for matrix in matrices),
            transcendentals=0,
        ),
        name=name,
    )(*matrices)
    return [flat[first : first + groups] for first in range(0, len(flat), groups)]


def exchange_in_order(parts, kv_index):
    moved = jnp.stack(
        [parts[0]] + [swap(part, "kv", other) for other, part in enumerate(parts) if other], axis=0
    )
    order = jnp.arange(len(parts), dtype=jnp.int32) ^ kv_index
    return jnp.take(moved, order, axis=0).reshape(-1, moved.shape[2])


def after(values, *earlier):
    return lax.optimization_barrier((values, *earlier))[0]


def on_columns(body, index, width, count):
    if width % LANES == 0:
        body(pl.ds(pl.multiple_of(index * width, LANES), width))
        return
    for choice in range(count):
        pl.when(index == choice)(functools.partial(body, pl.ds(choice * width, width)))


EXTRA = 16


def cache_kernel(blocks_ref, flags_ref, keys, values):
    first_row = lax.broadcasted_iota(jnp.int32, (EXTRA, 1), 0) == 0
    bias = jnp.where((flags_ref[...] > -FAR) | jnp.logical_not(first_row), 0.0, FLOOR_SCORE)
    for head in range(blocks_ref.shape[2]):
        keys[head, HD:, :] = bias.astype(jnp.bfloat16)
        for block in range(blocks_ref.shape[1]):
            place = pl.ds(block * BLOCK, BLOCK)
            keys[head, :HD, place] = blocks_ref[0, block, head]
            values[head, place, :] = blocks_ref[1, block, head].astype(jnp.float32).T.astype(
                jnp.bfloat16
            )


def cached_rows(blocks, flags):
    kv_local = blocks.shape[2]
    cached = flags.shape[1]
    return pl.pallas_call(
        cache_kernel,
        out_shape=(
            jax.ShapeDtypeStruct((kv_local, HD + EXTRA, cached), jnp.bfloat16),
            jax.ShapeDtypeStruct((kv_local, cached, HD), jnp.bfloat16),
        ),
        in_specs=[VMEM, VMEM],
        out_specs=(VMEM, VMEM),
        compiler_params=pltpu.CompilerParams(vmem_limit_bytes=VMEM_LIMIT),
        cost_estimate=pl.CostEstimate(
            flops=0, bytes_accessed=4 * blocks.size, transcendentals=0
        ),
        name="cached",
    )(blocks, flags)


def project_kernel(
    kv_local,
    per_group,
    normed_ref,
    cos_ref,
    sin_ref,
    flags_ref,
    source_ref,
    upper,
    lower,
    keys,
    values,
    weights,
    projected,
    sems,
):
    half = upper.shape[0]
    width = weights.shape[1]
    spans = [pl.ds(first, min(2 * TILE, width - first)) for first in range(0, width, 2 * TILE)]
    copies = [
        pltpu.make_async_copy(source_ref.at[:, columns], weights.at[:, columns], sems.at[at])
        for at, columns in enumerate(spans)
    ]
    for copy in copies:
        copy.start()
    new_rows = normed_ref.shape[0]
    chunk_rows = per_group * ROW_TILE
    first_row = lax.broadcasted_iota(jnp.int32, (EXTRA, 1), 0) == 0
    bias = jnp.where((flags_ref[...] > -FAR) | jnp.logical_not(first_row), 0.0, FLOOR_SCORE)
    marker = jnp.where(
        lax.broadcasted_iota(jnp.int32, (chunk_rows, EXTRA), 1) == 0, 1.0, 0.0
    ).astype(jnp.bfloat16)
    for head in range(kv_local):
        keys[head, HD:, :] = bias.astype(jnp.bfloat16)
        for chunk in range(half):
            upper[chunk, head, :, HD:] = marker
            lower[chunk, head, :, HD:] = marker
    for columns, copy in zip(spans, copies):
        copy.wait()
        projected[:, columns] = jnp.dot(
            normed_ref[...], weights[:, columns], preferred_element_type=jnp.float32
        )

    def rotated(rows, column):
        part = projected[rows, column : column + HD]
        turned = jnp.concatenate([part[:, HD // 2 :], part[:, : HD // 2]], axis=1)
        return part * cos_ref[rows, :] + turned * sin_ref[rows, :]

    query_width = kv_local * per_group * HD
    for chunk in range(new_rows // ROW_TILE):
        rows = pl.ds(chunk * ROW_TILE, ROW_TILE)
        for head in range(kv_local):
            for sub in range(per_group):
                queries = upper if chunk < half else lower
                queries[chunk % half, head, sub * ROW_TILE : (sub + 1) * ROW_TILE, :HD] = rotated(
                    rows, (head * per_group + sub) * HD
                ).astype(jnp.bfloat16)
            keys[head, :HD, rows] = rotated(rows, query_width + head * HD).T.astype(jnp.bfloat16)
            column = query_width + (kv_local + head) * HD
            values[head, rows, :] = projected[rows, column : column + HD].astype(jnp.bfloat16)


def project_rows(normed, tables, flags, weights, kv_local, per_group):
    new_rows = normed.shape[0]
    width = weights.shape[1]
    queries = jax.ShapeDtypeStruct(
        (new_rows // ROW_TILE // 2, kv_local, per_group * ROW_TILE, HD + EXTRA), jnp.bfloat16
    )
    upper, lower, keys, values = pl.pallas_call(
        functools.partial(project_kernel, kv_local, per_group),
        out_shape=(
            queries,
            queries,
            jax.ShapeDtypeStruct((kv_local, HD + EXTRA, new_rows), jnp.bfloat16),
            jax.ShapeDtypeStruct((kv_local, new_rows, HD), jnp.bfloat16),
        ),
        in_specs=[VMEM] * 4 + [ANY],
        out_specs=(VMEM,) * 4,
        scratch_shapes=[
            pltpu.VMEM((normed.shape[1], width), jnp.bfloat16),
            pltpu.VMEM((new_rows, width), jnp.float32),
            pltpu.SemaphoreType.DMA((width // TILE,)),
        ],
        compiler_params=pltpu.CompilerParams(vmem_limit_bytes=VMEM_LIMIT),
        cost_estimate=pl.CostEstimate(
            flops=2 * new_rows * normed.shape[1] * width,
            bytes_accessed=2 * normed.shape[1] * width,
            transcendentals=0,
        ),
        name="project",
    )(normed, *tables, flags, weights)
    return (upper, lower), (keys, values)


def attention_kernel(
    first_step,
    place_ref,
    queries,
    cached_keys,
    cached_values,
    own_keys,
    own_values,
    cached_ref,
    own_ref,
    out_ref,
    scores,
    probs,
    folded,
    shifts,
    summed,
):
    prefix_here = place_ref[1]
    kv_local, _, cached = cached_keys.shape
    new_rows = own_keys.shape[2]
    chunk_rows = queries.shape[2]
    per_group = chunk_rows // ROW_TILE
    factor = math.log2(math.e) / math.sqrt(HD)
    group = 64
    widest = min(4 * LANES, cached)
    tiles = [
        (first, cached_keys, cached_values, first, widest) for first in range(0, cached, widest)
    ]
    tiles.append((cached, own_keys, own_values, 0, new_rows))

    def score(step, head, first, keys, _, begin, width):
        scores[head, :, pl.ds(first, width)] = jnp.dot(
            queries[step, head],
            keys[head, :, pl.ds(begin, width)],
            preferred_element_type=jnp.float32,
        )
        own = keys is own_keys
        for part in range(chunk_rows // group):
            rows = pl.ds(part * group, group)
            if own:
                row_id = (first_step + step) * ROW_TILE + (part * group) % ROW_TILE + (
                    lax.broadcasted_iota(jnp.int32, (group, LANES), 0)
                )
            top = folded[head, rows, :]
            for lane in range(0, width, LANES):
                place = pl.ds(first + lane, LANES)
                piece = scores[head, rows, place]
                if own:
                    own_id = lane + lax.broadcasted_iota(jnp.int32, (group, LANES), 1)
                    piece = jnp.where(own_id <= row_id, piece, FLOOR_SCORE)
                    scores[head, rows, place] = piece
                top = jnp.maximum(top, piece)
            folded[head, rows, :] = top

    def narrow(step, head):
        def some(part, inner):
            rows = pl.ds(pl.multiple_of(part * 16, 16), 16)
            row_id = (first_step + step) * ROW_TILE + lax.rem(part * 16, ROW_TILE) + (
                lax.broadcasted_iota(jnp.int32, (16, 1), 0)
            )
            oldest = prefix_here + row_id - WINDOW
            old = jnp.where(cached_ref[...] > oldest, scores[head, rows, :cached], FLOOR_SCORE)
            new = jnp.where(own_ref[...] > oldest, scores[head, rows, cached:], FLOOR_SCORE)
            scores[head, rows, :cached] = old
            scores[head, rows, cached:] = new
            top = jnp.maximum(
                jnp.max(old, axis=1, keepdims=True), jnp.max(new, axis=1, keepdims=True)
            )
            folded[head, rows, :] = jnp.broadcast_to(top, (16, LANES))
            return inner

        lax.fori_loop(0, chunk_rows // 16, some, 0)

    def weigh(head, start, first, _, values, begin, width):
        for part in range(chunk_rows // group):
            rows = pl.ds(part * group, group)
            shift = shifts[head, rows, :]
            total = None if start else folded[head, rows, :]
            for lane in range(0, width, LANES):
                place = pl.ds(first + lane, LANES)
                piece = jnp.exp2(scores[head, rows, place] * factor - shift)
                total = piece if total is None else total + piece
                probs[head, rows, place] = piece.astype(jnp.bfloat16)
            folded[head, rows, :] = total
        return jnp.dot(
            probs[head, :, pl.ds(first, width)],
            values[head, pl.ds(begin, width), :],
            preferred_element_type=jnp.float32,
        )

    def attend(windowed, step, carry):
        for head in range(kv_local):
            folded[head] = jnp.full(folded.shape[1:], FLOOR_SCORE, jnp.float32)
            for tile in tiles:
                score(step, head, *tile)
        for head in range(kv_local):
            if windowed:
                narrow(step, head)
            for part in range(chunk_rows // group):
                rows = pl.ds(part * group, group)
                top = jnp.max(folded[head, rows, :], axis=1, keepdims=True) * factor
                shifts[head, rows, :] = jnp.broadcast_to(top, (group, LANES))
            for which, tile in enumerate(tiles):
                part = weigh(head, which == 0, *tile)
                summed[head] = part if which == 0 else summed[head] + part
            rows = pl.ds(pl.multiple_of(step * ROW_TILE, ROW_TILE), ROW_TILE)
            for sub in range(per_group):
                part = pl.ds(sub * ROW_TILE, ROW_TILE)
                total = jnp.sum(folded[head, part, :], axis=1, keepdims=True)
                column = (head * per_group + sub) * HD
                out_ref[rows, column : column + HD] = (summed[head, part, :] / total).astype(
                    jnp.bfloat16
                )
        return carry

    behind = prefix_here + new_rows > WINDOW
    for windowed in (False, True):

        @pl.when(behind == windowed)
        def _():
            lax.fori_loop(0, queries.shape[0], functools.partial(attend, windowed), 0)


def attend_rows(place, first_step, queries, cached, own, cached_pos, own_pos):
    chunks, kv_local, chunk_rows, _ = queries.shape
    span = cached_pos.shape[1] + own_pos.shape[1]
    heads = kv_local * chunk_rows // ROW_TILE
    new_rows = chunks * ROW_TILE
    return pl.pallas_call(
        functools.partial(attention_kernel, first_step),
        out_shape=jax.ShapeDtypeStruct((new_rows, heads * HD), jnp.bfloat16),
        in_specs=[SMEM] + [VMEM] * 7,
        out_specs=VMEM,
        scratch_shapes=[
            pltpu.VMEM((kv_local, chunk_rows, span), jnp.float32),
            pltpu.VMEM((kv_local, chunk_rows, span), jnp.bfloat16),
            pltpu.VMEM((kv_local, chunk_rows, LANES), jnp.float32),
            pltpu.VMEM((kv_local, chunk_rows, LANES), jnp.float32),
            pltpu.VMEM((kv_local, chunk_rows, HD), jnp.float32),
        ],
        compiler_params=pltpu.CompilerParams(vmem_limit_bytes=VMEM_LIMIT),
        cost_estimate=pl.CostEstimate(
            flops=8 * heads * new_rows * span * LANES,
            bytes_accessed=4 * span * LANES * kv_local,
            transcendentals=heads * new_rows * span,
        ),
        name="attention",
    )(place, queries, *cached, *own, cached_pos, own_pos)


def gather_groups(piece):
    groups = lax.axis_size("kv")
    pieces = {0: piece}
    for other in sorted(range(1, groups), key=lambda other: (bin(other).count("1"), -other)):
        low = other & -other
        near = pieces[low] if other ^ low else piece
        pieces[other] = swap(after(pieces[other ^ low], near), "kv", low)
    return [pieces[other] for other in range(groups)]


def sum_at_owner(parts):
    parts = list(parts)
    earlier = []
    for other in sorted(range(1, len(parts)), key=lambda other: -bin(other).count("1")):
        low = other & -other
        target = other ^ low
        came = swap(after(parts[other], *earlier), "kv", low)
        if target:
            earlier.append(came)
        added = parts[target].astype(jnp.float32) + came.astype(jnp.float32)
        parts[target] = added.astype(jnp.bfloat16) if target else added
    return parts[0]


def middle_kernel(sources, groups, place_ref, tokens_ref, gain_ref, *refs):
    parts = len(refs) - len(sources) - 7
    att = refs[:parts]
    own_ref = refs[parts]
    rest = refs[parts + 1 :]
    shares = rest[: len(sources)]
    normed_ref, residual_ref, gathered, weights, middle, sem = rest[len(sources) :]
    blk_index = place_ref[0]
    kv_index = place_ref[2]
    group_rows = own_ref.shape[0]
    new_rows, model = tokens_ref.shape
    tile = 2 * TILE
    loads = []
    for step in range(model // tile):
        columns = pl.ds(step * tile, tile)
        copies = []
        if shares[0].ndim == 3:
            copies.append((own_ref.at[:, columns], weights.at[pl.ds(0, group_rows), columns]))
            for (indices, _, _), ref in zip(sources, shares):
                part = ref.shape[1]
                for at, index in enumerate(indices):
                    first = pl.multiple_of((blk_index ^ index) * part, 16)
                    for other in range(1, groups):
                        lead = at * (groups - 1) + other - 1
                        rows = pl.ds(other * group_rows + first, part)
                        copies.append((ref.at[lead, :, columns], weights.at[rows, columns]))
        else:
            for other in range(groups):
                first = pl.multiple_of((kv_index ^ other) * group_rows, 16)
                rows = pl.ds(other * group_rows, group_rows)
                copies.append(
                    (shares[0].at[pl.ds(first, group_rows), columns], weights.at[rows, columns])
                )
        loads.append(
            [pltpu.make_async_copy(source, target, sem.at[step]) for source, target in copies]
        )
        for copy in loads[-1]:
            copy.start()
    some_rows, feature = att[0].shape
    for at, part in enumerate(att):
        first, other = at // groups * some_rows, at % groups
        gathered[first : first + some_rows, other * feature : (other + 1) * feature] = part[...]
    for step in range(model // tile):
        columns = pl.ds(step * tile, tile)
        for copy in loads[step]:
            copy.wait()
        summed = jnp.dot(gathered[...], weights[:, columns], preferred_element_type=jnp.float32)
        middle[:, columns] = (tokens_ref[:, columns].astype(jnp.float32) + summed).astype(
            jnp.bfloat16
        )

    def scale(step, carry):
        rows = pl.ds(pl.multiple_of(step * 16, 16), 16)
        part = middle[rows, :].astype(jnp.float32)
        mean_square = jnp.mean(part * part, axis=1, keepdims=True)
        normed_ref[rows, :] = (part * lax.rsqrt(mean_square + EPSILON) * gain_ref[...]).astype(
            jnp.bfloat16
        )
        return carry

    lax.fori_loop(0, new_rows // 16, scale, 0, unroll=2)
    out_width = model // groups

    def keep(columns):
        residual_ref[...] = middle[:, columns]

    on_columns(keep, kv_index, out_width, groups)


def middle_rows(place, tokens, gain, attended, own, sources, groups):
    new_rows, model = tokens.shape
    arrays = [values for _, _, values in sources]
    return pl.pallas_call(
        functools.partial(middle_kernel, sources, groups),
        out_shape=(
            jax.ShapeDtypeStruct((new_rows, model), jnp.bfloat16),
            jax.ShapeDtypeStruct((new_rows, model // groups), jnp.bfloat16),
        ),
        in_specs=[SMEM, VMEM, VMEM] + [VMEM] * len(attended) + [ANY] * (1 + len(arrays)),
        out_specs=(VMEM, VMEM),
        scratch_shapes=[
            pltpu.VMEM((new_rows, model), jnp.bfloat16),
            pltpu.VMEM((model, model), jnp.bfloat16),
            pltpu.VMEM((new_rows, model), jnp.bfloat16),
            pltpu.SemaphoreType.DMA((model // (2 * TILE),)),
        ],
        compiler_params=pltpu.CompilerParams(vmem_limit_bytes=VMEM_LIMIT),
        cost_estimate=pl.CostEstimate(
            flops=2 * new_rows * model * model,
            bytes_accessed=2 * model * model,
            transcendentals=0,
        ),
        name="middle",
    )(place, tokens, gain, *attended, own, *arrays)


def hidden_chunks(width):
    return [(first, min(TILE, width - first)) for first in range(0, width, TILE)]


def mlp_kernel(groups, widths, place_ref, normed_ref, down_ref, left, right, *refs):
    outs = refs[:groups]
    first_half, second_half, down, hidden, sems = refs[groups:]
    kv_index = place_ref[2]
    chunks = []
    base = 0
    for width, source, buffer in zip(widths, (left, right), (first_half, second_half)):
        for first, units in hidden_chunks(width):
            columns = pl.ds(2 * first, 2 * units)
            copy = pltpu.make_async_copy(
                source.at[:, columns], buffer.at[:, columns], sems.at[len(chunks)]
            )
            chunks.append((buffer, columns, base + first, units, copy))
        base += width
    last = pltpu.make_async_copy(down_ref, down, sems.at[len(chunks)])
    ahead = 3
    for _, _, _, _, copy in chunks[:ahead]:
        copy.start()
    for at, (buffer, columns, first, units, copy) in enumerate(chunks):
        copy.wait()
        if at + ahead < len(chunks):
            chunks[at + ahead][4].start()
        elif at + ahead == len(chunks):
            last.start()
        both = jnp.dot(normed_ref[...], buffer[:, columns], preferred_element_type=jnp.float32)
        gated, raised = both[:, :units], both[:, units:]
        hidden[:, first : first + units] = (gated / (1.0 + jnp.exp(-gated)) * raised).astype(
            jnp.bfloat16
        )
    last.wait()
    out_width = outs[0].shape[1]
    for other in range(groups):

        def product(columns, out=outs[other]):
            out[...] = jnp.dot(
                hidden[...], down[:, columns], preferred_element_type=jnp.float32
            ).astype(out.dtype)

        on_columns(product, kv_index ^ other, out_width, groups)


def mlp_parts(place, normed, w_down, left, right, groups, widths):
    new_rows, model = normed.shape
    out_width = model // groups
    return pl.pallas_call(
        functools.partial(mlp_kernel, groups, widths),
        out_shape=tuple(
            jax.ShapeDtypeStruct((new_rows, out_width), jnp.bfloat16 if other else jnp.float32)
            for other in range(groups)
        ),
        in_specs=[SMEM, VMEM, ANY, ANY, ANY],
        out_specs=(VMEM,) * groups,
        scratch_shapes=[
            pltpu.VMEM(left.shape, jnp.bfloat16),
            pltpu.VMEM(right.shape, jnp.bfloat16),
            pltpu.VMEM(w_down.shape, jnp.bfloat16),
            pltpu.VMEM((new_rows, w_down.shape[0]), jnp.bfloat16),
            pltpu.SemaphoreType.DMA((1 + sum(len(hidden_chunks(width)) for width in widths),)),
        ],
        compiler_params=pltpu.CompilerParams(vmem_limit_bytes=VMEM_LIMIT),
        cost_estimate=pl.CostEstimate(
            flops=6 * new_rows * model * w_down.shape[0],
            bytes_accessed=6 * model * w_down.shape[0],
            transcendentals=new_rows * w_down.shape[0],
        ),
        name="mlp",
    )(place, normed, w_down, left, right)


def shards(
    tokens,
    attn_gain,
    mlp_gain,
    w_query,
    w_key,
    w_value,
    w_gate,
    w_up,
    w_out,
    w_down,
    cache,
    slot_prompt,
    prefix_len,
    new_len,
):
    groups = lax.axis_size("kv")
    blk_index = lax.axis_index("blk")
    kv_index = lax.axis_index("kv")
    query_width = w_query.shape[1] // groups
    key_width = w_key.shape[1] // groups
    per_group = HEADS // KV_HEADS
    new_rows = tokens.shape[0]
    prompts = prefix_len.shape[0]
    slots = cache.shape[1]
    prefix_here = prefix_len[blk_index]
    live_count = new_len[blk_index]
    place = jnp.stack([blk_index, prefix_here, kv_index]).astype(jnp.int32)

    global_rank, local_rank = slot_ranks(slot_prompt, prompts, slots)
    own_prompts = lax.dynamic_slice_in_dim(slot_prompt, blk_index * slots, slots)
    own_ranks = lax.dynamic_slice_in_dim(local_rank, blk_index * slots, slots)
    placed = own_prompts * CAP + own_ranks
    buffer_ids = jnp.arange(prompts * CAP, dtype=jnp.int32)
    matches = placed[None, :] == buffer_ids[:, None]
    source_slot = jnp.sum(
        jnp.where(matches, jnp.arange(slots, dtype=jnp.int32)[None, :], 0), axis=1
    )
    outgoing = jnp.take(cache, source_slot, axis=1)
    arrived = lax.all_to_all(outgoing, "blk", split_axis=1, concat_axis=1, tiled=True)
    slot_ids = jnp.arange(prompts * slots, dtype=jnp.int32)
    landing = slot_ids // slots * CAP + local_rank
    for_me = slot_prompt == blk_index
    received = (landing[None, :] == buffer_ids[:, None]) & for_me[None, :]
    block_number = jnp.sum(jnp.where(received, global_rank[None, :], 0), axis=1)
    block_live = jnp.any(received, axis=1)
    key_pos = block_number[:, None] * BLOCK + jnp.arange(BLOCK, dtype=jnp.int32)[None, :]
    key_live = block_live[:, None] & (key_pos < prefix_here)
    cached_pos = jnp.where(key_live, jnp.where(key_pos < SINKS, FAR, key_pos), -FAR)
    cached_pos = cached_pos.reshape(1, -1)
    row_ids = jnp.arange(new_rows, dtype=jnp.int32)
    positions = prefix_here + row_ids
    own_pos = jnp.where(
        row_ids < live_count, jnp.where(positions < SINKS, FAR, positions), -FAR
    ).reshape(1, -1)

    normed = rms_scale(tokens, attn_gain)
    tables = rope_tables(positions)
    cached = cached_rows(arrived, cached_pos)

    hidden_width = w_gate.shape[1] // groups
    cut = hidden_width // (2 * TILE) * TILE
    widths = (cut, hidden_width - cut)
    layouts = []
    base = 0
    for width in widths:
        layout = []
        for first, units in hidden_chunks(width):
            start = base + first
            layout += [(0, start, start + units), (1, start, start + units)]
        layouts.append(layout)
        base += width
    packed = pack((w_gate, w_up), groups, layouts, "pack_pair")

    spans = [(0, 0, query_width), (1, 0, key_width), (2, 0, key_width)]
    (qkv_parts,) = pack((w_query, w_key, w_value), groups, [spans], "pack_qkv")
    moved_qkv = exchange_in_order(qkv_parts, kv_index)
    w_qkv = lax.all_gather(moved_qkv, "blk", axis=0, tiled=True)

    moved = exchange_in_order(after(packed[0], moved_qkv, arrived), kv_index)
    first_half = lax.all_gather(after(moved, w_qkv, *cached), "blk", axis=0, tiled=True)

    eighth = w_out.shape[0] // lax.axis_size("blk")
    spread = lax.axis_size("blk") == 8 and eighth % 16 == 0
    if spread:
        share = lax.dynamic_slice_in_dim(w_out, blk_index * eighth, eighth, 0)
        share = after(share, moved)
        shares = [swap(share, "kv", other) for other in range(1, groups)]

    queries, own = project_rows(normed, tables, own_pos, w_qkv, cache.shape[2], per_group)
    half = queries[0].shape[0]
    upper = attend_rows(place, 0, queries[0], cached, own, cached_pos, own_pos)
    moved_second = exchange_in_order(after(packed[1], upper), kv_index)
    if spread:
        shares = jnp.stack(after(shares, upper), axis=0)
        near = (swap(shares, "blk", 2), swap(shares, "blk", 4))
    lower = attend_rows(
        place, half, after(queries[1], upper), cached, own, cached_pos, own_pos
    )
    earlier = (lower, *near) if spread else (lower,)
    second_half = lax.all_gather(after(moved_second, *earlier), "blk", axis=0, tiled=True)
    attended = jnp.concatenate([upper, lower], axis=0)
    everyone = gather_groups(attended)

    if spread:
        by_x, by_y = near
        by_y = after(by_y, upper, lower)
        diagonal = swap(by_y, "blk", 2)
        trio = swap(jnp.concatenate([shares, by_x, by_y], axis=0), "blk", 1)
        w_out_sources = [
            ((0,), 0, shares),
            ((2,), 0, by_x),
            ((4,), 0, by_y),
            ((6,), 0, diagonal),
            ((1, 3, 5), 0, trio),
            ((7,), 0, swap(after(diagonal, everyone[-1]), "blk", 1)),
        ]
    else:
        w_out_sources = [(0, 0, lax.all_gather(w_out, "kv", axis=0, tiled=True))]

    normed_mid, residual = middle_rows(
        place, tokens, mlp_gain.reshape(1, -1), everyone, w_out, w_out_sources, groups
    )
    parts = mlp_parts(place, normed_mid, w_down, first_half, second_half, groups, widths)
    reduced = sum_at_owner(parts)
    mixed = jnp.where(
        (row_ids < live_count)[:, None], residual.astype(jnp.float32) + reduced, 0.0
    )
    return mixed.astype(jnp.bfloat16)


def solution(mesh):
    return jax.shard_map(
        shards,
        mesh=mesh,
        in_specs=(
            P("blk", None),
            P(),
            P(),
            P(("blk", "kv"), None),
            P(("blk", "kv"), None),
            P(("blk", "kv"), None),
            P(("blk", "kv"), None),
            P(("blk", "kv"), None),
            P("kv", None),
            P("kv", None),
            P(None, "blk", "kv", None, None),
            P(),
            P(),
            P(),
        ),
        out_specs=P("blk", "kv"),
        check_vma=False,
    )
```

```python
import functools
import math

import jax
import jax.numpy as jnp
from jax import lax
from jax.experimental import pallas as pl
from jax.experimental.pallas import tpu as pltpu
from jax.sharding import PartitionSpec as P

HEADS = 32
KV_HEADS = 8
HD = 80
WINDOW = 4096
SINKS = 4
BLOCK = 128
CAP = 2


FLOOR_SCORE = -1e30
EPSILON = 1e-05
ROPE_BASE = 10000.0
FAR = 1 << 30
LANES = 128
TILE = 256
ROW_TILE = 128
VMEM_LIMIT = 56 * 1024 * 1024

ANY = pl.BlockSpec(memory_space=pl.ANY)
VMEM = pl.BlockSpec(memory_space=pltpu.VMEM)
SMEM = pl.BlockSpec(memory_space=pltpu.SMEM)


def rms_scale(row_data, gain_vec):
    values = row_data.astype(jnp.float32)
    mean_square = jnp.mean(values * values, axis=-1, keepdims=True)
    return (values * lax.rsqrt(mean_square + EPSILON) * gain_vec).astype(jnp.bfloat16)


def rope_tables(positions):
    half_width = HD // 2
    frequency = ROPE_BASE ** (-2.0 * jnp.arange(half_width, dtype=jnp.float32) / HD)
    angles = positions.astype(jnp.float32)[:, None] * frequency[None, :]
    cosine = jnp.cos(angles)
    sine = jnp.sin(angles)
    return (
        jnp.concatenate([cosine, cosine], axis=1),
        jnp.concatenate([-sine, sine], axis=1),
    )


def slot_ranks(slot_prompt, prompts, slots):
    onehot = (slot_prompt[:, None] == jnp.arange(prompts, dtype=jnp.int32)[None, :]).astype(
        jnp.int32
    )
    running = jnp.cumsum(onehot, axis=0)
    global_rank = jnp.sum(onehot * (running - 1), axis=1)
    local_count = jnp.cumsum(onehot.reshape(-1, slots, prompts), axis=1).reshape(-1, prompts)
    local_rank = jnp.sum(onehot * (local_count - 1), axis=1)
    return (global_rank, local_rank)


def swap(values, axis, bit):
    pairs = [(index, index ^ bit) for index in range(lax.axis_size(axis))]
    return lax.ppermute(values, axis, pairs)


def half_up(width):
    return (width // 2 + LANES - 1) // LANES * LANES


def pack_kernel(layouts, groups, *refs):
    kv_index = lax.axis_index("kv")
    outs = refs[len(refs) - groups * len(layouts) :]
    for choice in range(groups):

        @pl.when(kv_index == choice)
        def _():
            for which, spans in enumerate(layouts):
                for other in range(groups):
                    out = outs[which * groups + other]
                    column = 0
                    for matrix, first, last in spans:
                        start = (choice ^ other) * (refs[matrix].shape[1] // groups)
                        width = last - first
                        out[:, column : column + width] = refs[matrix][
                            :, start + first : start + last
                        ].astype(jnp.bfloat16)
                        column += width


def pack(matrices, groups, layouts, name):
    rows = matrices[0].shape[0]
    shapes = []
    for spans in layouts:
        width = sum(last - first for _, first, last in spans)
        shapes += [jax.ShapeDtypeStruct((rows, width), jnp.bfloat16)] * groups
    flat = pl.pallas_call(
        functools.partial(pack_kernel, layouts, groups),
        out_shape=tuple(shapes),
        in_specs=[VMEM] * len(matrices),
        out_specs=(VMEM,) * len(shapes),
        compiler_params=pltpu.CompilerParams(vmem_limit_bytes=VMEM_LIMIT),
        cost_estimate=pl.CostEstimate(
            flops=0,
            bytes_accessed=6 * rows * sum(matrix.shape[1] for matrix in matrices),
            transcendentals=0,
        ),
        name=name,
    )(*matrices)
    return [flat[first : first + groups] for first in range(0, len(flat), groups)]


def exchange(parts):
    return [parts[0]] + [swap(part, "kv", other) for other, part in enumerate(parts) if other]


def in_order(moved, kv_index):
    order = jnp.arange(len(moved), dtype=jnp.int32) ^ kv_index
    moved = jnp.stack(moved, axis=0)
    return jnp.take(moved, order, axis=0).reshape(-1, moved.shape[2])


def after(values, *earlier):
    return lax.optimization_barrier((values, *earlier))[0]


def plane_gather(piece, meanwhile):
    rows = piece.shape[0]
    by_x = swap(piece, "blk", 2)
    by_y = swap(piece, "blk", 4)
    upper = swap(after(by_y[: rows // 2], *meanwhile), "blk", 2)
    lower = swap(after(by_x[rows // 2 :], *meanwhile), "blk", 4)
    mine = [(0, 0, piece), (2, 0, by_x), (4, 0, by_y), (6, 0, upper), (6, rows // 2, lower)]
    across = jnp.concatenate([piece, by_x, by_y, upper, lower], axis=0)
    return mine + [((1, 3, 5, 7), 0, swap(across, "blk", 1))]


def on_columns(body, index, width, count):
    if width % LANES == 0:
        body(pl.ds(pl.multiple_of(index * width, LANES), width))
        return
    for choice in range(count):
        pl.when(index == choice)(functools.partial(body, pl.ds(choice * width, width)))


def row_copies(sources, refs, buffer, sem, blk_index, kv_index, groups):
    copies = []
    total = buffer.shape[0]
    for (index, begin, _), ref in zip(sources, refs):
        rows = ref.shape[0]
        piece = total // 8
        block = piece // groups
        if rows == total and index is None:
            copies.append(pltpu.make_async_copy(ref, buffer, sem))
            continue
        for first in range(0, rows, block):
            piece_index = index[first // piece] if isinstance(index, tuple) else index
            other = (begin + first) % piece // block
            target = (blk_index ^ piece_index) * piece + (kv_index ^ other) * block
            copies.append(
                pltpu.make_async_copy(
                    ref.at[pl.ds(first, block)],
                    buffer.at[pl.ds(pl.multiple_of(target, 16), block)],
                    sem,
                )
            )
    return copies


EXTRA = 16


def cache_kernel(blocks_ref, flags_ref, keys, values):
    first_row = lax.broadcasted_iota(jnp.int32, (EXTRA, 1), 0) == 0
    bias = jnp.where((flags_ref[...] > -FAR) | jnp.logical_not(first_row), 0.0, FLOOR_SCORE)
    for head in range(blocks_ref.shape[2]):
        keys[head, HD:, :] = bias.astype(jnp.bfloat16)
        for block in range(blocks_ref.shape[1]):
            place = pl.ds(block * BLOCK, BLOCK)
            keys[head, :HD, place] = blocks_ref[0, block, head]
            values[head, place, :] = blocks_ref[1, block, head].astype(jnp.float32).T.astype(
                jnp.bfloat16
            )


def cached_rows(blocks, flags):
    kv_local = blocks.shape[2]
    cached = flags.shape[1]
    return pl.pallas_call(
        cache_kernel,
        out_shape=(
            jax.ShapeDtypeStruct((kv_local, HD + EXTRA, cached), jnp.bfloat16),
            jax.ShapeDtypeStruct((kv_local, cached, HD), jnp.bfloat16),
        ),
        in_specs=[VMEM, VMEM],
        out_specs=(VMEM, VMEM),
        compiler_params=pltpu.CompilerParams(vmem_limit_bytes=VMEM_LIMIT),
        cost_estimate=pl.CostEstimate(
            flops=0, bytes_accessed=4 * blocks.size, transcendentals=0
        ),
        name="cached",
    )(blocks, flags)


def project_kernel(
    sources, groups, kv_local, per_group, place_ref, normed_ref, cos_ref, sin_ref, flags_ref, *refs
):
    count = len(sources)
    pieces = refs[:count]
    upper, lower, keys, values, weights, projected, sem = refs[count:]
    half = upper.shape[0]
    copies = row_copies(sources, pieces, weights, sem.at[0], place_ref[0], place_ref[2], groups)
    for copy in copies:
        copy.start()
    new_rows = normed_ref.shape[0]
    chunk_rows = per_group * ROW_TILE
    first_row = lax.broadcasted_iota(jnp.int32, (EXTRA, 1), 0) == 0
    bias = jnp.where((flags_ref[...] > -FAR) | jnp.logical_not(first_row), 0.0, FLOOR_SCORE)
    marker = jnp.where(
        lax.broadcasted_iota(jnp.int32, (chunk_rows, EXTRA), 1) == 0, 1.0, 0.0
    ).astype(jnp.bfloat16)
    for head in range(kv_local):
        keys[head, HD:, :] = bias.astype(jnp.bfloat16)
        for chunk in range(half):
            upper[chunk, head, :, HD:] = marker
            lower[chunk, head, :, HD:] = marker
    for copy in copies:
        copy.wait()
    width = weights.shape[1]
    for first in range(0, width, 2 * TILE):
        columns = slice(first, min(first + 2 * TILE, width))
        projected[:, columns] = jnp.dot(
            normed_ref[...], weights[:, columns], preferred_element_type=jnp.float32
        )

    def rotated(rows, column):
        part = projected[rows, column : column + HD]
        turned = jnp.concatenate([part[:, HD // 2 :], part[:, : HD // 2]], axis=1)
        return part * cos_ref[rows, :] + turned * sin_ref[rows, :]

    query_width = kv_local * per_group * HD
    for chunk in range(new_rows // ROW_TILE):
        rows = pl.ds(chunk * ROW_TILE, ROW_TILE)
        for head in range(kv_local):
            for sub in range(per_group):
                queries = upper if chunk < half else lower
                queries[chunk % half, head, sub * ROW_TILE : (sub + 1) * ROW_TILE, :HD] = rotated(
                    rows, (head * per_group + sub) * HD
                ).astype(jnp.bfloat16)
            keys[head, :HD, rows] = rotated(rows, query_width + head * HD).T.astype(jnp.bfloat16)
            column = query_width + (kv_local + head) * HD
            values[head, rows, :] = projected[rows, column : column + HD].astype(jnp.bfloat16)


def project_rows(place, normed, tables, flags, sources, groups, kv_local, per_group):
    new_rows = normed.shape[0]
    arrays = [values for _, _, values in sources]
    width = arrays[0].shape[1]
    queries = jax.ShapeDtypeStruct(
        (new_rows // ROW_TILE // 2, kv_local, per_group * ROW_TILE, HD + EXTRA), jnp.bfloat16
    )
    upper, lower, keys, values = pl.pallas_call(
        functools.partial(project_kernel, sources, groups, kv_local, per_group),
        out_shape=(
            queries,
            queries,
            jax.ShapeDtypeStruct((kv_local, HD + EXTRA, new_rows), jnp.bfloat16),
            jax.ShapeDtypeStruct((kv_local, new_rows, HD), jnp.bfloat16),
        ),
        in_specs=[SMEM] + [VMEM] * 4 + [ANY] * len(arrays),
        out_specs=(VMEM,) * 4,
        scratch_shapes=[
            pltpu.VMEM((normed.shape[1], width), jnp.bfloat16),
            pltpu.VMEM((new_rows, width), jnp.float32),
            pltpu.SemaphoreType.DMA((1,)),
        ],
        compiler_params=pltpu.CompilerParams(vmem_limit_bytes=VMEM_LIMIT),
        cost_estimate=pl.CostEstimate(
            flops=2 * new_rows * normed.shape[1] * width,
            bytes_accessed=2 * normed.shape[1] * width,
            transcendentals=0,
        ),
        name="project",
    )(place, normed, *tables, flags, *arrays)
    return (upper, lower), (keys, values)


def attention_kernel(
    first_step,
    place_ref,
    queries,
    cached_keys,
    cached_values,
    own_keys,
    own_values,
    cached_ref,
    own_ref,
    out_ref,
    scores,
    probs,
    folded,
    shifts,
    summed,
):
    prefix_here = place_ref[1]
    kv_local, _, cached = cached_keys.shape
    new_rows = own_keys.shape[2]
    chunk_rows = queries.shape[2]
    per_group = chunk_rows // ROW_TILE
    factor = math.log2(math.e) / math.sqrt(HD)
    group = 64
    widest = min(4 * LANES, cached)
    tiles = [
        (first, cached_keys, cached_values, first, widest) for first in range(0, cached, widest)
    ]
    tiles.append((cached, own_keys, own_values, 0, new_rows))

    def score(step, head, first, keys, _, begin, width):
        scores[head, :, pl.ds(first, width)] = jnp.dot(
            queries[step, head],
            keys[head, :, pl.ds(begin, width)],
            preferred_element_type=jnp.float32,
        )
        own = keys is own_keys
        for part in range(chunk_rows // group):
            rows = pl.ds(part * group, group)
            if own:
                row_id = (first_step + step) * ROW_TILE + (part * group) % ROW_TILE + (
                    lax.broadcasted_iota(jnp.int32, (group, LANES), 0)
                )
            top = folded[head, rows, :]
            for lane in range(0, width, LANES):
                place = pl.ds(first + lane, LANES)
                piece = scores[head, rows, place]
                if own:
                    own_id = lane + lax.broadcasted_iota(jnp.int32, (group, LANES), 1)
                    piece = jnp.where(own_id <= row_id, piece, FLOOR_SCORE)
                    scores[head, rows, place] = piece
                top = jnp.maximum(top, piece)
            folded[head, rows, :] = top

    def narrow(step, head):
        def some(part, inner):
            rows = pl.ds(pl.multiple_of(part * 16, 16), 16)
            row_id = (first_step + step) * ROW_TILE + lax.rem(part * 16, ROW_TILE) + (
                lax.broadcasted_iota(jnp.int32, (16, 1), 0)
            )
            oldest = prefix_here + row_id - WINDOW
            old = jnp.where(cached_ref[...] > oldest, scores[head, rows, :cached], FLOOR_SCORE)
            new = jnp.where(own_ref[...] > oldest, scores[head, rows, cached:], FLOOR_SCORE)
            scores[head, rows, :cached] = old
            scores[head, rows, cached:] = new
            top = jnp.maximum(
                jnp.max(old, axis=1, keepdims=True), jnp.max(new, axis=1, keepdims=True)
            )
            folded[head, rows, :] = jnp.broadcast_to(top, (16, LANES))
            return inner

        lax.fori_loop(0, chunk_rows // 16, some, 0)

    def weigh(head, start, first, _, values, begin, width):
        for part in range(chunk_rows // group):
            rows = pl.ds(part * group, group)
            shift = shifts[head, rows, :]
            total = None if start else folded[head, rows, :]
            for lane in range(0, width, LANES):
                place = pl.ds(first + lane, LANES)
                piece = jnp.exp2(scores[head, rows, place] * factor - shift)
                total = piece if total is None else total + piece
                probs[head, rows, place] = piece.astype(jnp.bfloat16)
            folded[head, rows, :] = total
        return jnp.dot(
            probs[head, :, pl.ds(first, width)],
            values[head, pl.ds(begin, width), :],
            preferred_element_type=jnp.float32,
        )

    def attend(windowed, step, carry):
        for head in range(kv_local):
            folded[head] = jnp.full(folded.shape[1:], FLOOR_SCORE, jnp.float32)
            for tile in tiles:
                score(step, head, *tile)
        for head in range(kv_local):
            if windowed:
                narrow(step, head)
            for part in range(chunk_rows // group):
                rows = pl.ds(part * group, group)
                top = jnp.max(folded[head, rows, :], axis=1, keepdims=True) * factor
                shifts[head, rows, :] = jnp.broadcast_to(top, (group, LANES))
            for which, tile in enumerate(tiles):
                part = weigh(head, which == 0, *tile)
                summed[head] = part if which == 0 else summed[head] + part
            rows = pl.ds(pl.multiple_of(step * ROW_TILE, ROW_TILE), ROW_TILE)
            for sub in range(per_group):
                part = pl.ds(sub * ROW_TILE, ROW_TILE)
                total = jnp.sum(folded[head, part, :], axis=1, keepdims=True)
                column = (head * per_group + sub) * HD
                out_ref[rows, column : column + HD] = (summed[head, part, :] / total).astype(
                    jnp.bfloat16
                )
        return carry

    behind = prefix_here + new_rows > WINDOW
    for windowed in (False, True):

        @pl.when(behind == windowed)
        def _():
            lax.fori_loop(0, queries.shape[0], functools.partial(attend, windowed), 0)


def attend_rows(place, first_step, queries, cached, own, cached_pos, own_pos):
    chunks, kv_local, chunk_rows, _ = queries.shape
    span = cached_pos.shape[1] + own_pos.shape[1]
    heads = kv_local * chunk_rows // ROW_TILE
    new_rows = chunks * ROW_TILE
    return pl.pallas_call(
        functools.partial(attention_kernel, first_step),
        out_shape=jax.ShapeDtypeStruct((new_rows, heads * HD), jnp.bfloat16),
        in_specs=[SMEM] + [VMEM] * 7,
        out_specs=VMEM,
        scratch_shapes=[
            pltpu.VMEM((kv_local, chunk_rows, span), jnp.float32),
            pltpu.VMEM((kv_local, chunk_rows, span), jnp.bfloat16),
            pltpu.VMEM((kv_local, chunk_rows, LANES), jnp.float32),
            pltpu.VMEM((kv_local, chunk_rows, LANES), jnp.float32),
            pltpu.VMEM((kv_local, chunk_rows, HD), jnp.float32),
        ],
        compiler_params=pltpu.CompilerParams(vmem_limit_bytes=VMEM_LIMIT),
        cost_estimate=pl.CostEstimate(
            flops=8 * heads * new_rows * span * LANES,
            bytes_accessed=4 * span * LANES * kv_local,
            transcendentals=heads * new_rows * span,
        ),
        name="attention",
    )(place, queries, *cached, *own, cached_pos, own_pos)


def out_kernel(groups, attended_ref, weights_ref, *refs):
    outs, rows_ref = refs[:groups], refs[groups]
    kv_index = lax.axis_index("kv")
    count = attended_ref.shape[0] // groups
    for other in range(groups):
        first = pl.multiple_of((kv_index ^ other) * count, 16)
        rows_ref[other * count : (other + 1) * count, :] = attended_ref[pl.ds(first, count), :]
    for column in range(0, weights_ref.shape[1], 2 * TILE):
        columns = slice(column, column + 2 * TILE)
        product = jnp.dot(
            rows_ref[...], weights_ref[:, columns], preferred_element_type=jnp.float32
        )
        for other in range(groups):
            outs[other][:, columns] = product[other * count : (other + 1) * count].astype(
                outs[other].dtype
            )


def out_terms(attended, w_out, groups):
    rows, feature = attended.shape
    model = w_out.shape[1]
    return pl.pallas_call(
        functools.partial(out_kernel, groups),
        out_shape=tuple(
            jax.ShapeDtypeStruct((rows // groups, model), jnp.bfloat16 if other else jnp.float32)
            for other in range(groups)
        ),
        in_specs=[VMEM] * 2,
        out_specs=(VMEM,) * groups,
        scratch_shapes=[pltpu.VMEM((rows, feature), jnp.bfloat16)],
        compiler_params=pltpu.CompilerParams(vmem_limit_bytes=VMEM_LIMIT),
        cost_estimate=pl.CostEstimate(
            flops=2 * rows * feature * model, bytes_accessed=2 * feature * model, transcendentals=0
        ),
        name="out",
    )(attended, w_out)


def gather_groups(piece):
    groups = lax.axis_size("kv")
    pieces = {0: piece}
    for other in sorted(range(1, groups), key=lambda other: (bin(other).count("1"), -other)):
        low = other & -other
        near = pieces[low] if other ^ low else piece
        pieces[other] = swap(after(pieces[other ^ low], near), "kv", low)
    return [pieces[other] for other in range(groups)]


def sum_at_owner(parts):
    parts = list(parts)
    earlier = []
    for other in sorted(range(1, len(parts)), key=lambda other: -bin(other).count("1")):
        low = other & -other
        target = other ^ low
        came = swap(after(parts[other], *earlier), "kv", low)
        if target:
            earlier.append(came)
        added = parts[target].astype(jnp.float32) + came.astype(jnp.float32)
        parts[target] = added.astype(jnp.bfloat16) if target else added
    return parts[0]


def hidden_chunks(width):
    return [(first, min(TILE, width - first)) for first in range(0, width, TILE)]


def mlp_kernel(groups, place_ref, gain_ref, down_ref, pair_ref, *refs):
    pieces = refs[:groups]
    outs = refs[groups : 2 * groups]
    residual_ref, normed_ref, pair, down, hidden, sems = refs[2 * groups :]
    kv_index = place_ref[2]
    chunks = []
    for first, units in hidden_chunks(down_ref.shape[0]):
        columns = pl.ds(2 * first, 2 * units)
        copy = pltpu.make_async_copy(
            pair_ref.at[:, columns], pair.at[:, columns], sems.at[len(chunks)]
        )
        chunks.append((columns, first, units, copy))
    last = pltpu.make_async_copy(down_ref, down, sems.at[len(chunks)])
    ahead = 3
    for _, _, _, copy in chunks[:ahead]:
        copy.start()
    count = pieces[0].shape[0]
    out_width = outs[0].shape[1]
    for other in range(groups):
        start = (kv_index ^ other) * count

        def scale(step, carry, piece=pieces[other], start=start):
            part = piece[pl.ds(pl.multiple_of(step * 16, 16), 16), :].astype(jnp.float32)
            mean_square = jnp.mean(part * part, axis=1, keepdims=True)
            place = pl.ds(pl.multiple_of(start + step * 16, 16), 16)
            normed_ref[place, :] = (
                part * lax.rsqrt(mean_square + EPSILON) * gain_ref[...]
            ).astype(jnp.bfloat16)
            return carry

        lax.fori_loop(0, count // 16, scale, 0, unroll=2)

        def keep(columns, piece=pieces[other], start=start):
            residual_ref[pl.ds(pl.multiple_of(start, 16), count), :] = piece[:, columns]

        on_columns(keep, kv_index, out_width, groups)
    for at, (columns, first, units, copy) in enumerate(chunks):
        copy.wait()
        if at + ahead < len(chunks):
            chunks[at + ahead][3].start()
        elif at + ahead == len(chunks):
            last.start()
        both = jnp.dot(normed_ref[...], pair[:, columns], preferred_element_type=jnp.float32)
        gated, raised = both[:, :units], both[:, units:]
        hidden[:, first : first + units] = (gated / (1.0 + jnp.exp(-gated)) * raised).astype(
            jnp.bfloat16
        )
    last.wait()
    for other in range(groups):

        def product(columns, out=outs[other]):
            out[...] = jnp.dot(
                hidden[...], down[:, columns], preferred_element_type=jnp.float32
            ).astype(out.dtype)

        on_columns(product, kv_index ^ other, out_width, groups)


def mlp_parts(place, gain, middle, w_down, pair, groups):
    count, model = middle[0].shape
    new_rows = groups * count
    out_width = model // groups
    chunk_count = len(hidden_chunks(w_down.shape[0]))
    return pl.pallas_call(
        functools.partial(mlp_kernel, groups),
        out_shape=tuple(
            jax.ShapeDtypeStruct((new_rows, out_width), jnp.bfloat16 if other else jnp.float32)
            for other in range(groups)
        )
        + (jax.ShapeDtypeStruct((new_rows, out_width), jnp.bfloat16),),
        in_specs=[SMEM, VMEM, ANY, ANY] + [VMEM] * groups,
        out_specs=(VMEM,) * (groups + 1),
        scratch_shapes=[
            pltpu.VMEM((new_rows, model), jnp.bfloat16),
            pltpu.VMEM(pair.shape, jnp.bfloat16),
            pltpu.VMEM(w_down.shape, jnp.bfloat16),
            pltpu.VMEM((new_rows, w_down.shape[0]), jnp.bfloat16),
            pltpu.SemaphoreType.DMA((1 + chunk_count,)),
        ],
        compiler_params=pltpu.CompilerParams(vmem_limit_bytes=VMEM_LIMIT),
        cost_estimate=pl.CostEstimate(
            flops=6 * new_rows * model * w_down.shape[0],
            bytes_accessed=6 * model * w_down.shape[0],
            transcendentals=new_rows * w_down.shape[0],
        ),
        name="mlp",
    )(place, gain, w_down, pair, *middle)


def shards(
    tokens,
    attn_gain,
    mlp_gain,
    w_query,
    w_key,
    w_value,
    w_gate,
    w_up,
    w_out,
    w_down,
    cache,
    slot_prompt,
    prefix_len,
    new_len,
):
    groups = lax.axis_size("kv")
    blk_index = lax.axis_index("blk")
    kv_index = lax.axis_index("kv")
    query_width = w_query.shape[1] // groups
    key_width = w_key.shape[1] // groups
    per_group = HEADS // KV_HEADS
    new_rows = tokens.shape[0]
    prompts = prefix_len.shape[0]
    slots = cache.shape[1]
    prefix_here = prefix_len[blk_index]
    live_count = new_len[blk_index]
    place = jnp.stack([blk_index, prefix_here, kv_index]).astype(jnp.int32)

    global_rank, local_rank = slot_ranks(slot_prompt, prompts, slots)
    own_prompts = lax.dynamic_slice_in_dim(slot_prompt, blk_index * slots, slots)
    own_ranks = lax.dynamic_slice_in_dim(local_rank, blk_index * slots, slots)
    placed = own_prompts * CAP + own_ranks
    buffer_ids = jnp.arange(prompts * CAP, dtype=jnp.int32)
    matches = placed[None, :] == buffer_ids[:, None]
    source_slot = jnp.sum(
        jnp.where(matches, jnp.arange(slots, dtype=jnp.int32)[None, :], 0), axis=1
    )
    outgoing = jnp.take(cache, source_slot, axis=1)
    arrived = lax.all_to_all(outgoing, "blk", split_axis=1, concat_axis=1, tiled=True)
    slot_ids = jnp.arange(prompts * slots, dtype=jnp.int32)
    landing = slot_ids // slots * CAP + local_rank
    for_me = slot_prompt == blk_index
    received = (landing[None, :] == buffer_ids[:, None]) & for_me[None, :]
    block_number = jnp.sum(jnp.where(received, global_rank[None, :], 0), axis=1)
    block_live = jnp.any(received, axis=1)
    key_pos = block_number[:, None] * BLOCK + jnp.arange(BLOCK, dtype=jnp.int32)[None, :]
    key_live = block_live[:, None] & (key_pos < prefix_here)
    cached_pos = jnp.where(key_live, jnp.where(key_pos < SINKS, FAR, key_pos), -FAR)
    cached_pos = cached_pos.reshape(1, -1)
    row_ids = jnp.arange(new_rows, dtype=jnp.int32)
    positions = prefix_here + row_ids
    own_pos = jnp.where(
        row_ids < live_count, jnp.where(positions < SINKS, FAR, positions), -FAR
    ).reshape(1, -1)

    hidden_width = w_gate.shape[1] // groups
    layout = []
    for first, units in hidden_chunks(hidden_width):
        layout += [(0, first, first + units), (1, first, first + units)]
    (packed,) = pack((w_gate, w_up), groups, [layout], "pack_pair")
    normed = rms_scale(tokens, attn_gain)
    tables = rope_tables(positions)

    in_place = lax.axis_size("blk") == 8 and w_query.shape[0] % 16 == 0
    spans = [(0, 0, query_width), (1, 0, key_width), (2, 0, key_width)]
    (qkv_parts,) = pack((w_query, w_key, w_value), groups, [spans], "pack_qkv")
    moved_qkv = exchange(qkv_parts)
    moved_pair = exchange(after(packed, moved_qkv, arrived))
    if in_place:
        rows = jnp.concatenate(moved_qkv, axis=0)
        rows = after(rows, normed, *tables, own_pos, cached_pos, place)
        qkv = plane_gather(rows, moved_pair[:2])
    else:
        rows = in_order(moved_qkv, kv_index)
        qkv = [(None, 0, lax.all_gather(rows, "blk", axis=0, tiled=True))]
    cached = cached_rows(arrived, cached_pos)
    queries, own = project_rows(
        place, normed, tables, own_pos, qkv, groups, cache.shape[2], per_group
    )
    half = queries[0].shape[0]
    upper = attend_rows(place, 0, queries[0], cached, own, cached_pos, own_pos)
    rows = in_order(after(moved_pair, upper), kv_index)
    pair = lax.all_gather(rows, "blk", axis=0, tiled=True)
    lower = attend_rows(place, half, after(queries[1], upper), cached, own, cached_pos, own_pos)
    attended = jnp.concatenate([upper, lower], axis=0)

    summed = sum_at_owner(out_terms(attended, w_out, groups))
    count = new_rows // groups
    own_rows = lax.dynamic_slice_in_dim(tokens, kv_index * count, count, 0)
    middle = (own_rows.astype(jnp.float32) + summed).astype(jnp.bfloat16)
    *parts, residual = mlp_parts(
        place,
        mlp_gain.reshape(1, -1),
        gather_groups(middle),
        w_down,
        pair,
        groups,
    )
    reduced = sum_at_owner(parts)
    mixed = jnp.where(
        (row_ids < live_count)[:, None], residual.astype(jnp.float32) + reduced, 0.0
    )
    return mixed.astype(jnp.bfloat16)


def solution(mesh):
    return jax.shard_map(
        shards,
        mesh=mesh,
        in_specs=(
            P("blk", None),
            P(),
            P(),
            P(("blk", "kv"), None),
            P(("blk", "kv"), None),
            P(("blk", "kv"), None),
            P(("blk", "kv"), None),
            P(("blk", "kv"), None),
            P("kv", None),
            P("kv", None),
            P(None, "blk", "kv", None, None),
            P(),
            P(),
            P(),
        ),
        out_specs=P("blk", "kv"),
        check_vma=False,
    )
```

```python
import functools
import math

import jax
import jax.numpy as jnp
from jax import lax
from jax.experimental import pallas as pl
from jax.experimental.pallas import tpu as pltpu
from jax.sharding import PartitionSpec as P

HEADS = 32
KV_HEADS = 8
HD = 80
WINDOW = 4096
SINKS = 4
BLOCK = 128
CAP = 2


FLOOR_SCORE = -1e30
EPSILON = 1e-05
ROPE_BASE = 10000.0
FAR = 1 << 30
LANES = 128
TILE = 256
ROW_TILE = 128
VMEM_LIMIT = 56 * 1024 * 1024

ANY = pl.BlockSpec(memory_space=pl.ANY)
VMEM = pl.BlockSpec(memory_space=pltpu.VMEM)
SMEM = pl.BlockSpec(memory_space=pltpu.SMEM)


def rms_scale(row_data, gain_vec):
    values = row_data.astype(jnp.float32)
    mean_square = jnp.mean(values * values, axis=-1, keepdims=True)
    return (values * lax.rsqrt(mean_square + EPSILON) * gain_vec).astype(jnp.bfloat16)


def rope_tables(positions):
    half_width = HD // 2
    frequency = ROPE_BASE ** (-2.0 * jnp.arange(half_width, dtype=jnp.float32) / HD)
    angles = positions.astype(jnp.float32)[:, None] * frequency[None, :]
    cosine = jnp.cos(angles)
    sine = jnp.sin(angles)
    return (
        jnp.concatenate([cosine, cosine], axis=1),
        jnp.concatenate([-sine, sine], axis=1),
    )


def slot_ranks(slot_prompt, prompts, slots):
    onehot = (slot_prompt[:, None] == jnp.arange(prompts, dtype=jnp.int32)[None, :]).astype(
        jnp.int32
    )
    running = jnp.cumsum(onehot, axis=0)
    global_rank = jnp.sum(onehot * (running - 1), axis=1)
    local_count = jnp.cumsum(onehot.reshape(-1, slots, prompts), axis=1).reshape(-1, prompts)
    local_rank = jnp.sum(onehot * (local_count - 1), axis=1)
    return (global_rank, local_rank)


def swap(values, axis, bit):
    pairs = [(index, index ^ bit) for index in range(lax.axis_size(axis))]
    return lax.ppermute(values, axis, pairs)


def half_up(width):
    return (width // 2 + LANES - 1) // LANES * LANES


def pack_kernel(layouts, groups, *refs):
    kv_index = lax.axis_index("kv")
    outs = refs[len(refs) - groups * len(layouts) :]
    for choice in range(groups):

        @pl.when(kv_index == choice)
        def _():
            for which, spans in enumerate(layouts):
                for other in range(groups):
                    out = outs[which * groups + other]
                    column = 0
                    for matrix, first, last in spans:
                        start = (choice ^ other) * (refs[matrix].shape[1] // groups)
                        width = last - first
                        out[:, column : column + width] = refs[matrix][
                            :, start + first : start + last
                        ].astype(jnp.bfloat16)
                        column += width


def pack(matrices, groups, layouts, name):
    rows = matrices[0].shape[0]
    shapes = []
    for spans in layouts:
        width = sum(last - first for _, first, last in spans)
        shapes += [jax.ShapeDtypeStruct((rows, width), jnp.bfloat16)] * groups
    flat = pl.pallas_call(
        functools.partial(pack_kernel, layouts, groups),
        out_shape=tuple(shapes),
        in_specs=[VMEM] * len(matrices),
        out_specs=(VMEM,) * len(shapes),
        compiler_params=pltpu.CompilerParams(vmem_limit_bytes=VMEM_LIMIT),
        cost_estimate=pl.CostEstimate(
            flops=0,
            bytes_accessed=6 * rows * sum(matrix.shape[1] for matrix in matrices),
            transcendentals=0,
        ),
        name=name,
    )(*matrices)
    return [flat[first : first + groups] for first in range(0, len(flat), groups)]


def exchange_in_order(parts, kv_index):
    moved = jnp.stack(
        [parts[0]] + [swap(part, "kv", other) for other, part in enumerate(parts) if other], axis=0
    )
    order = jnp.arange(len(parts), dtype=jnp.int32) ^ kv_index
    return jnp.take(moved, order, axis=0).reshape(-1, moved.shape[2])


def after(values, *earlier):
    return lax.optimization_barrier((values, *earlier))[0]


def on_columns(body, index, width, count):
    if width % LANES == 0:
        body(pl.ds(pl.multiple_of(index * width, LANES), width))
        return
    for choice in range(count):
        pl.when(index == choice)(functools.partial(body, pl.ds(choice * width, width)))


EXTRA = 16


def cache_kernel(blocks_ref, flags_ref, keys, values):
    first_row = lax.broadcasted_iota(jnp.int32, (EXTRA, 1), 0) == 0
    bias = jnp.where((flags_ref[...] > -FAR) | jnp.logical_not(first_row), 0.0, FLOOR_SCORE)
    for head in range(blocks_ref.shape[2]):
        keys[head, HD:, :] = bias.astype(jnp.bfloat16)
        for block in range(blocks_ref.shape[1]):
            place = pl.ds(block * BLOCK, BLOCK)
            keys[head, :HD, place] = blocks_ref[0, block, head]
            values[head, place, :] = blocks_ref[1, block, head].astype(jnp.float32).T.astype(
                jnp.bfloat16
            )


def cached_rows(blocks, flags):
    kv_local = blocks.shape[2]
    cached = flags.shape[1]
    return pl.pallas_call(
        cache_kernel,
        out_shape=(
            jax.ShapeDtypeStruct((kv_local, HD + EXTRA, cached), jnp.bfloat16),
            jax.ShapeDtypeStruct((kv_local, cached, HD), jnp.bfloat16),
        ),
        in_specs=[VMEM, VMEM],
        out_specs=(VMEM, VMEM),
        compiler_params=pltpu.CompilerParams(vmem_limit_bytes=VMEM_LIMIT),
        cost_estimate=pl.CostEstimate(
            flops=0, bytes_accessed=4 * blocks.size, transcendentals=0
        ),
        name="cached",
    )(blocks, flags)


def project_kernel(
    kv_local,
    per_group,
    normed_ref,
    cos_ref,
    sin_ref,
    flags_ref,
    source_ref,
    upper,
    lower,
    keys,
    values,
    weights,
    projected,
    sems,
):
    half = upper.shape[0]
    width = weights.shape[1]
    spans = [pl.ds(first, min(2 * TILE, width - first)) for first in range(0, width, 2 * TILE)]
    copies = [
        pltpu.make_async_copy(source_ref.at[:, columns], weights.at[:, columns], sems.at[at])
        for at, columns in enumerate(spans)
    ]
    for copy in copies:
        copy.start()
    new_rows = normed_ref.shape[0]
    chunk_rows = per_group * ROW_TILE
    first_row = lax.broadcasted_iota(jnp.int32, (EXTRA, 1), 0) == 0
    bias = jnp.where((flags_ref[...] > -FAR) | jnp.logical_not(first_row), 0.0, FLOOR_SCORE)
    marker = jnp.where(
        lax.broadcasted_iota(jnp.int32, (chunk_rows, EXTRA), 1) == 0, 1.0, 0.0
    ).astype(jnp.bfloat16)
    for head in range(kv_local):
        keys[head, HD:, :] = bias.astype(jnp.bfloat16)
        for chunk in range(half):
            upper[chunk, head, :, HD:] = marker
            lower[chunk, head, :, HD:] = marker
    for columns, copy in zip(spans, copies):
        copy.wait()
        projected[:, columns] = jnp.dot(
            normed_ref[...], weights[:, columns], preferred_element_type=jnp.float32
        )

    def rotated(rows, column):
        part = projected[rows, column : column + HD]
        turned = jnp.concatenate([part[:, HD // 2 :], part[:, : HD // 2]], axis=1)
        return part * cos_ref[rows, :] + turned * sin_ref[rows, :]

    query_width = kv_local * per_group * HD
    for chunk in range(new_rows // ROW_TILE):
        rows = pl.ds(chunk * ROW_TILE, ROW_TILE)
        for head in range(kv_local):
            for sub in range(per_group):
                queries = upper if chunk < half else lower
                queries[chunk % half, head, sub * ROW_TILE : (sub + 1) * ROW_TILE, :HD] = rotated(
                    rows, (head * per_group + sub) * HD
                ).astype(jnp.bfloat16)
            keys[head, :HD, rows] = rotated(rows, query_width + head * HD).T.astype(jnp.bfloat16)
            column = query_width + (kv_local + head) * HD
            values[head, rows, :] = projected[rows, column : column + HD].astype(jnp.bfloat16)


def project_rows(normed, tables, flags, weights, kv_local, per_group):
    new_rows = normed.shape[0]
    width = weights.shape[1]
    queries = jax.ShapeDtypeStruct(
        (new_rows // ROW_TILE // 2, kv_local, per_group * ROW_TILE, HD + EXTRA), jnp.bfloat16
    )
    upper, lower, keys, values = pl.pallas_call(
        functools.partial(project_kernel, kv_local, per_group),
        out_shape=(
            queries,
            queries,
            jax.ShapeDtypeStruct((kv_local, HD + EXTRA, new_rows), jnp.bfloat16),
            jax.ShapeDtypeStruct((kv_local, new_rows, HD), jnp.bfloat16),
        ),
        in_specs=[VMEM] * 4 + [ANY],
        out_specs=(VMEM,) * 4,
        scratch_shapes=[
            pltpu.VMEM((normed.shape[1], width), jnp.bfloat16),
            pltpu.VMEM((new_rows, width), jnp.float32),
            pltpu.SemaphoreType.DMA((width // TILE,)),
        ],
        compiler_params=pltpu.CompilerParams(vmem_limit_bytes=VMEM_LIMIT),
        cost_estimate=pl.CostEstimate(
            flops=2 * new_rows * normed.shape[1] * width,
            bytes_accessed=2 * normed.shape[1] * width,
            transcendentals=0,
        ),
        name="project",
    )(normed, *tables, flags, weights)
    return (upper, lower), (keys, values)


def attention_kernel(
    first_step,
    place_ref,
    queries,
    cached_keys,
    cached_values,
    own_keys,
    own_values,
    cached_ref,
    own_ref,
    out_ref,
    scores,
    probs,
    folded,
    shifts,
    summed,
):
    prefix_here = place_ref[1]
    kv_local, _, cached = cached_keys.shape
    new_rows = own_keys.shape[2]
    chunk_rows = queries.shape[2]
    per_group = chunk_rows // ROW_TILE
    factor = math.log2(math.e) / math.sqrt(HD)
    group = 64
    widest = min(4 * LANES, cached)
    tiles = [
        (first, cached_keys, cached_values, first, widest) for first in range(0, cached, widest)
    ]
    tiles.append((cached, own_keys, own_values, 0, new_rows))

    def score(step, head, first, keys, _, begin, width):
        scores[head, :, pl.ds(first, width)] = jnp.dot(
            queries[step, head],
            keys[head, :, pl.ds(begin, width)],
            preferred_element_type=jnp.float32,
        )
        own = keys is own_keys
        for part in range(chunk_rows // group):
            rows = pl.ds(part * group, group)
            if own:
                row_id = (first_step + step) * ROW_TILE + (part * group) % ROW_TILE + (
                    lax.broadcasted_iota(jnp.int32, (group, LANES), 0)
                )
            top = folded[head, rows, :]
            for lane in range(0, width, LANES):
                place = pl.ds(first + lane, LANES)
                piece = scores[head, rows, place]
                if own:
                    own_id = lane + lax.broadcasted_iota(jnp.int32, (group, LANES), 1)
                    piece = jnp.where(own_id <= row_id, piece, FLOOR_SCORE)
                    scores[head, rows, place] = piece
                top = jnp.maximum(top, piece)
            folded[head, rows, :] = top

    def narrow(step, head):
        def some(part, inner):
            rows = pl.ds(pl.multiple_of(part * 16, 16), 16)
            row_id = (first_step + step) * ROW_TILE + lax.rem(part * 16, ROW_TILE) + (
                lax.broadcasted_iota(jnp.int32, (16, 1), 0)
            )
            oldest = prefix_here + row_id - WINDOW
            old = jnp.where(cached_ref[...] > oldest, scores[head, rows, :cached], FLOOR_SCORE)
            new = jnp.where(own_ref[...] > oldest, scores[head, rows, cached:], FLOOR_SCORE)
            scores[head, rows, :cached] = old
            scores[head, rows, cached:] = new
            top = jnp.maximum(
                jnp.max(old, axis=1, keepdims=True), jnp.max(new, axis=1, keepdims=True)
            )
            folded[head, rows, :] = jnp.broadcast_to(top, (16, LANES))
            return inner

        lax.fori_loop(0, chunk_rows // 16, some, 0)

    def weigh(head, start, first, _, values, begin, width):
        for part in range(chunk_rows // group):
            rows = pl.ds(part * group, group)
            shift = shifts[head, rows, :]
            total = None if start else folded[head, rows, :]
            for lane in range(0, width, LANES):
                place = pl.ds(first + lane, LANES)
                piece = jnp.exp2(scores[head, rows, place] * factor - shift)
                total = piece if total is None else total + piece
                probs[head, rows, place] = piece.astype(jnp.bfloat16)
            folded[head, rows, :] = total
        return jnp.dot(
            probs[head, :, pl.ds(first, width)],
            values[head, pl.ds(begin, width), :],
            preferred_element_type=jnp.float32,
        )

    def attend(windowed, step, carry):
        for head in range(kv_local):
            folded[head] = jnp.full(folded.shape[1:], FLOOR_SCORE, jnp.float32)
            for tile in tiles:
                score(step, head, *tile)
        for head in range(kv_local):
            if windowed:
                narrow(step, head)
            for part in range(chunk_rows // group):
                rows = pl.ds(part * group, group)
                top = jnp.max(folded[head, rows, :], axis=1, keepdims=True) * factor
                shifts[head, rows, :] = jnp.broadcast_to(top, (group, LANES))
            for which, tile in enumerate(tiles):
                part = weigh(head, which == 0, *tile)
                summed[head] = part if which == 0 else summed[head] + part
            rows = pl.ds(pl.multiple_of(step * ROW_TILE, ROW_TILE), ROW_TILE)
            for sub in range(per_group):
                part = pl.ds(sub * ROW_TILE, ROW_TILE)
                total = jnp.sum(folded[head, part, :], axis=1, keepdims=True)
                column = (head * per_group + sub) * HD
                out_ref[rows, column : column + HD] = (summed[head, part, :] / total).astype(
                    jnp.bfloat16
                )
        return carry

    behind = prefix_here + new_rows > WINDOW
    for windowed in (False, True):

        @pl.when(behind == windowed)
        def _():
            lax.fori_loop(0, queries.shape[0], functools.partial(attend, windowed), 0)


def attend_rows(place, first_step, queries, cached, own, cached_pos, own_pos):
    chunks, kv_local, chunk_rows, _ = queries.shape
    span = cached_pos.shape[1] + own_pos.shape[1]
    heads = kv_local * chunk_rows // ROW_TILE
    new_rows = chunks * ROW_TILE
    return pl.pallas_call(
        functools.partial(attention_kernel, first_step),
        out_shape=jax.ShapeDtypeStruct((new_rows, heads * HD), jnp.bfloat16),
        in_specs=[SMEM] + [VMEM] * 7,
        out_specs=VMEM,
        scratch_shapes=[
            pltpu.VMEM((kv_local, chunk_rows, span), jnp.float32),
            pltpu.VMEM((kv_local, chunk_rows, span), jnp.bfloat16),
            pltpu.VMEM((kv_local, chunk_rows, LANES), jnp.float32),
            pltpu.VMEM((kv_local, chunk_rows, LANES), jnp.float32),
            pltpu.VMEM((kv_local, chunk_rows, HD), jnp.float32),
        ],
        compiler_params=pltpu.CompilerParams(vmem_limit_bytes=VMEM_LIMIT),
        cost_estimate=pl.CostEstimate(
            flops=8 * heads * new_rows * span * LANES,
            bytes_accessed=4 * span * LANES * kv_local,
            transcendentals=heads * new_rows * span,
        ),
        name="attention",
    )(place, queries, *cached, *own, cached_pos, own_pos)


def gather_groups(piece):
    groups = lax.axis_size("kv")
    pieces = {0: piece}
    for other in sorted(range(1, groups), key=lambda other: (bin(other).count("1"), -other)):
        low = other & -other
        source = piece if other == low else after(pieces[other ^ low], pieces[low])
        pieces[other] = swap(source, "kv", low)
    return [pieces[other] for other in range(groups)]


def sum_at_owner(parts):
    parts = list(parts)
    earlier = []
    for other in sorted(range(1, len(parts)), key=lambda other: -bin(other).count("1")):
        low = other & -other
        target = other ^ low
        came = swap(after(parts[other], *earlier), "kv", low)
        if target:
            earlier.append(came)
        added = parts[target].astype(jnp.float32) + came.astype(jnp.float32)
        parts[target] = added.astype(jnp.bfloat16) if target else added
    return parts[0]


def middle_kernel(sources, groups, place_ref, tokens_ref, gain_ref, *refs):
    parts = len(refs) - len(sources) - 7
    att = refs[:parts]
    own_ref = refs[parts]
    rest = refs[parts + 1 :]
    shares = rest[: len(sources)]
    normed_ref, residual_ref, gathered, weights, middle, sem = rest[len(sources) :]
    blk_index = place_ref[0]
    kv_index = place_ref[2]
    group_rows = own_ref.shape[0]
    new_rows, model = tokens_ref.shape
    tile = 2 * TILE
    loads = []
    for step in range(model // tile):
        columns = pl.ds(step * tile, tile)
        copies = []
        if shares[0].ndim == 3:
            copies.append((own_ref.at[:, columns], weights.at[pl.ds(0, group_rows), columns]))
            for (indices, _, _), ref in zip(sources, shares):
                part = ref.shape[1]
                for at, index in enumerate(indices):
                    first = pl.multiple_of((blk_index ^ index) * part, 16)
                    for other in range(1, groups):
                        lead = at * (groups - 1) + other - 1
                        rows = pl.ds(other * group_rows + first, part)
                        copies.append((ref.at[lead, :, columns], weights.at[rows, columns]))
        else:
            for other in range(groups):
                first = pl.multiple_of((kv_index ^ other) * group_rows, 16)
                rows = pl.ds(other * group_rows, group_rows)
                copies.append(
                    (shares[0].at[pl.ds(first, group_rows), columns], weights.at[rows, columns])
                )
        loads.append(
            [pltpu.make_async_copy(source, target, sem.at[step]) for source, target in copies]
        )
        for copy in loads[-1]:
            copy.start()
    some_rows, feature = att[0].shape
    for at, part in enumerate(att):
        first, other = at // groups * some_rows, at % groups
        gathered[first : first + some_rows, other * feature : (other + 1) * feature] = part[...]
    for step in range(model // tile):
        columns = pl.ds(step * tile, tile)
        for copy in loads[step]:
            copy.wait()
        summed = jnp.dot(gathered[...], weights[:, columns], preferred_element_type=jnp.float32)
        middle[:, columns] = (tokens_ref[:, columns].astype(jnp.float32) + summed).astype(
            jnp.bfloat16
        )

    def scale(step, carry):
        rows = pl.ds(pl.multiple_of(step * 16, 16), 16)
        part = middle[rows, :].astype(jnp.float32)
        mean_square = jnp.mean(part * part, axis=1, keepdims=True)
        normed_ref[rows, :] = (part * lax.rsqrt(mean_square + EPSILON) * gain_ref[...]).astype(
            jnp.bfloat16
        )
        return carry

    lax.fori_loop(0, new_rows // 16, scale, 0, unroll=2)
    out_width = model // groups

    def keep(columns):
        residual_ref[...] = middle[:, columns]

    on_columns(keep, kv_index, out_width, groups)


def middle_rows(place, tokens, gain, attended, own, sources, groups):
    new_rows, model = tokens.shape
    arrays = [values for _, _, values in sources]
    return pl.pallas_call(
        functools.partial(middle_kernel, sources, groups),
        out_shape=(
            jax.ShapeDtypeStruct((new_rows, model), jnp.bfloat16),
            jax.ShapeDtypeStruct((new_rows, model // groups), jnp.bfloat16),
        ),
        in_specs=[SMEM, VMEM, VMEM] + [VMEM] * len(attended) + [ANY] * (1 + len(arrays)),
        out_specs=(VMEM, VMEM),
        scratch_shapes=[
            pltpu.VMEM((new_rows, model), jnp.bfloat16),
            pltpu.VMEM((model, model), jnp.bfloat16),
            pltpu.VMEM((new_rows, model), jnp.bfloat16),
            pltpu.SemaphoreType.DMA((model // (2 * TILE),)),
        ],
        compiler_params=pltpu.CompilerParams(vmem_limit_bytes=VMEM_LIMIT),
        cost_estimate=pl.CostEstimate(
            flops=2 * new_rows * model * model,
            bytes_accessed=2 * model * model,
            transcendentals=0,
        ),
        name="middle",
    )(place, tokens, gain, *attended, own, *arrays)


def hidden_chunks(width):
    return [(first, min(TILE, width - first)) for first in range(0, width, TILE)]


def mlp_kernel(groups, place_ref, normed_ref, down_ref, pair_ref, *refs):
    outs = refs[:groups]
    pair, down, hidden, sems = refs[groups:]
    kv_index = place_ref[2]
    chunks = []
    for first, units in hidden_chunks(down_ref.shape[0]):
        columns = pl.ds(2 * first, 2 * units)
        copy = pltpu.make_async_copy(
            pair_ref.at[:, columns], pair.at[:, columns], sems.at[len(chunks)]
        )
        chunks.append((columns, first, units, copy))
    last = pltpu.make_async_copy(down_ref, down, sems.at[len(chunks)])
    ahead = 3
    for _, _, _, copy in chunks[:ahead]:
        copy.start()
    for at, (columns, first, units, copy) in enumerate(chunks):
        copy.wait()
        if at + ahead < len(chunks):
            chunks[at + ahead][3].start()
        elif at + ahead == len(chunks):
            last.start()
        both = jnp.dot(normed_ref[...], pair[:, columns], preferred_element_type=jnp.float32)
        gated, raised = both[:, :units], both[:, units:]
        hidden[:, first : first + units] = (gated / (1.0 + jnp.exp(-gated)) * raised).astype(
            jnp.bfloat16
        )
    last.wait()
    out_width = outs[0].shape[1]
    for other in range(groups):

        def product(columns, out=outs[other]):
            out[...] = jnp.dot(
                hidden[...], down[:, columns], preferred_element_type=jnp.float32
            ).astype(out.dtype)

        on_columns(product, kv_index ^ other, out_width, groups)


def mlp_parts(place, normed, w_down, pair, groups):
    new_rows, model = normed.shape
    out_width = model // groups
    return pl.pallas_call(
        functools.partial(mlp_kernel, groups),
        out_shape=tuple(
            jax.ShapeDtypeStruct((new_rows, out_width), jnp.bfloat16 if other else jnp.float32)
            for other in range(groups)
        ),
        in_specs=[SMEM, VMEM, ANY, ANY],
        out_specs=(VMEM,) * groups,
        scratch_shapes=[
            pltpu.VMEM(pair.shape, jnp.bfloat16),
            pltpu.VMEM(w_down.shape, jnp.bfloat16),
            pltpu.VMEM((new_rows, w_down.shape[0]), jnp.bfloat16),
            pltpu.SemaphoreType.DMA((1 + len(hidden_chunks(w_down.shape[0])),)),
        ],
        compiler_params=pltpu.CompilerParams(vmem_limit_bytes=VMEM_LIMIT),
        cost_estimate=pl.CostEstimate(
            flops=6 * new_rows * model * w_down.shape[0],
            bytes_accessed=6 * model * w_down.shape[0],
            transcendentals=new_rows * w_down.shape[0],
        ),
        name="mlp",
    )(place, normed, w_down, pair)


def shards(
    tokens,
    attn_gain,
    mlp_gain,
    w_query,
    w_key,
    w_value,
    w_gate,
    w_up,
    w_out,
    w_down,
    cache,
    slot_prompt,
    prefix_len,
    new_len,
):
    groups = lax.axis_size("kv")
    blk_index = lax.axis_index("blk")
    kv_index = lax.axis_index("kv")
    query_width = w_query.shape[1] // groups
    key_width = w_key.shape[1] // groups
    per_group = HEADS // KV_HEADS
    new_rows = tokens.shape[0]
    prompts = prefix_len.shape[0]
    slots = cache.shape[1]
    prefix_here = prefix_len[blk_index]
    live_count = new_len[blk_index]
    place = jnp.stack([blk_index, prefix_here, kv_index]).astype(jnp.int32)

    global_rank, local_rank = slot_ranks(slot_prompt, prompts, slots)
    own_prompts = lax.dynamic_slice_in_dim(slot_prompt, blk_index * slots, slots)
    own_ranks = lax.dynamic_slice_in_dim(local_rank, blk_index * slots, slots)
    placed = own_prompts * CAP + own_ranks
    buffer_ids = jnp.arange(prompts * CAP, dtype=jnp.int32)
    matches = placed[None, :] == buffer_ids[:, None]
    source_slot = jnp.sum(
        jnp.where(matches, jnp.arange(slots, dtype=jnp.int32)[None, :], 0), axis=1
    )
    outgoing = jnp.take(cache, source_slot, axis=1)
    arrived = lax.all_to_all(outgoing, "blk", split_axis=1, concat_axis=1, tiled=True)
    slot_ids = jnp.arange(prompts * slots, dtype=jnp.int32)
    landing = slot_ids // slots * CAP + local_rank
    for_me = slot_prompt == blk_index
    received = (landing[None, :] == buffer_ids[:, None]) & for_me[None, :]
    block_number = jnp.sum(jnp.where(received, global_rank[None, :], 0), axis=1)
    block_live = jnp.any(received, axis=1)
    key_pos = block_number[:, None] * BLOCK + jnp.arange(BLOCK, dtype=jnp.int32)[None, :]
    key_live = block_live[:, None] & (key_pos < prefix_here)
    cached_pos = jnp.where(key_live, jnp.where(key_pos < SINKS, FAR, key_pos), -FAR)
    cached_pos = cached_pos.reshape(1, -1)
    row_ids = jnp.arange(new_rows, dtype=jnp.int32)
    positions = prefix_here + row_ids
    own_pos = jnp.where(
        row_ids < live_count, jnp.where(positions < SINKS, FAR, positions), -FAR
    ).reshape(1, -1)

    normed = rms_scale(tokens, attn_gain)
    tables = rope_tables(positions)
    cached = cached_rows(arrived, cached_pos)

    hidden_width = w_gate.shape[1] // groups
    layout = []
    for first, units in hidden_chunks(hidden_width):
        layout += [(0, first, first + units), (1, first, first + units)]
    (packed,) = pack((w_gate, w_up), groups, [layout], "pack_pair")

    spans = [(0, 0, query_width), (1, 0, key_width), (2, 0, key_width)]
    (qkv_parts,) = pack((w_query, w_key, w_value), groups, [spans], "pack_qkv")
    moved_qkv = exchange_in_order(qkv_parts, kv_index)
    w_qkv = lax.all_gather(moved_qkv, "blk", axis=0, tiled=True)

    moved = exchange_in_order(after(packed, moved_qkv, arrived), kv_index)
    meanwhile = (*cached, normed, *tables, own_pos, place)
    pair = lax.all_gather(after(moved, w_qkv, *meanwhile), "blk", axis=0, tiled=True)

    eighth = w_out.shape[0] // lax.axis_size("blk")
    spread = lax.axis_size("blk") == 8 and eighth % 16 == 0
    if spread:
        share = lax.dynamic_slice_in_dim(w_out, blk_index * eighth, eighth, 0)
        share = after(share, moved)
        shares = [swap(share, "kv", other) for other in range(1, groups)]

    queries, own = project_rows(normed, tables, own_pos, w_qkv, cache.shape[2], per_group)
    half = queries[0].shape[0]
    upper = attend_rows(place, 0, queries[0], cached, own, cached_pos, own_pos)
    if spread:
        shares = jnp.stack(after(shares, upper), axis=0)
        near = (swap(shares, "blk", 2), swap(shares, "blk", 4))
    lower = attend_rows(
        place, half, after(queries[1], upper), cached, own, cached_pos, own_pos
    )
    attended = jnp.concatenate([upper, lower], axis=0)
    everyone = gather_groups(attended)

    if spread:
        by_x, by_y = near
        by_x, by_y = after((by_x, by_y), everyone[1], everyone[2])
        diagonal = swap(by_y, "blk", 2)
        trio = swap(jnp.concatenate([shares, by_x, by_y], axis=0), "blk", 1)
        w_out_sources = [
            ((0,), 0, shares),
            ((2,), 0, by_x),
            ((4,), 0, by_y),
            ((6,), 0, diagonal),
            ((1, 3, 5), 0, trio),
            ((7,), 0, swap(after(diagonal, everyone[-1]), "blk", 1)),
        ]
    else:
        w_out_sources = [(0, 0, lax.all_gather(w_out, "kv", axis=0, tiled=True))]

    normed_mid, residual = middle_rows(
        place, tokens, mlp_gain.reshape(1, -1), everyone, w_out, w_out_sources, groups
    )
    parts = mlp_parts(place, normed_mid, w_down, pair, groups)
    reduced = sum_at_owner(parts)
    mixed = jnp.where(
        (row_ids < live_count)[:, None], residual.astype(jnp.float32) + reduced, 0.0
    )
    return mixed.astype(jnp.bfloat16)


def solution(mesh):
    return jax.shard_map(
        shards,
        mesh=mesh,
        in_specs=(
            P("blk", None),
            P(),
            P(),
            P(("blk", "kv"), None),
            P(("blk", "kv"), None),
            P(("blk", "kv"), None),
            P(("blk", "kv"), None),
            P(("blk", "kv"), None),
            P("kv", None),
            P("kv", None),
            P(None, "blk", "kv", None, None),
            P(),
            P(),
            P(),
        ),
        out_specs=P("blk", "kv"),
        check_vma=False,
    )
```

```python
import functools
import math

import jax
import jax.numpy as jnp
from jax import lax
from jax.experimental import pallas as pl
from jax.experimental.pallas import tpu as pltpu
from jax.sharding import PartitionSpec as P

HEADS = 32
KV_HEADS = 8
HD = 80
WINDOW = 4096
SINKS = 4
BLOCK = 128
CAP = 2


FLOOR_SCORE = -1e30
EPSILON = 1e-05
ROPE_BASE = 10000.0
FAR = 1 << 30
LANES = 128
TILE = 256
ROW_TILE = 128
VMEM_LIMIT = 56 * 1024 * 1024

ANY = pl.BlockSpec(memory_space=pl.ANY)
VMEM = pl.BlockSpec(memory_space=pltpu.VMEM)
SMEM = pl.BlockSpec(memory_space=pltpu.SMEM)


def rms_scale(row_data, gain_vec):
    values = row_data.astype(jnp.float32)
    mean_square = jnp.mean(values * values, axis=-1, keepdims=True)
    return (values * lax.rsqrt(mean_square + EPSILON) * gain_vec).astype(jnp.bfloat16)


def rope_tables(positions):
    half_width = HD // 2
    frequency = ROPE_BASE ** (-2.0 * jnp.arange(half_width, dtype=jnp.float32) / HD)
    angles = positions.astype(jnp.float32)[:, None] * frequency[None, :]
    cosine = jnp.cos(angles)
    sine = jnp.sin(angles)
    return (
        jnp.concatenate([cosine, cosine], axis=1),
        jnp.concatenate([-sine, sine], axis=1),
    )


def slot_ranks(slot_prompt, prompts, slots):
    onehot = (slot_prompt[:, None] == jnp.arange(prompts, dtype=jnp.int32)[None, :]).astype(
        jnp.int32
    )
    running = jnp.cumsum(onehot, axis=0)
    global_rank = jnp.sum(onehot * (running - 1), axis=1)
    local_count = jnp.cumsum(onehot.reshape(-1, slots, prompts), axis=1).reshape(-1, prompts)
    local_rank = jnp.sum(onehot * (local_count - 1), axis=1)
    return (global_rank, local_rank)


def swap(values, axis, bit):
    pairs = [(index, index ^ bit) for index in range(lax.axis_size(axis))]
    return lax.ppermute(values, axis, pairs)


def half_up(width):
    return (width // 2 + LANES - 1) // LANES * LANES


def pack_kernel(layouts, groups, *refs):
    kv_index = lax.axis_index("kv")
    outs = refs[len(refs) - groups * len(layouts) :]
    for choice in range(groups):

        @pl.when(kv_index == choice)
        def _():
            for which, spans in enumerate(layouts):
                for other in range(groups):
                    out = outs[which * groups + other]
                    column = 0
                    for matrix, first, last in spans:
                        start = (choice ^ other) * (refs[matrix].shape[1] // groups)
                        width = last - first
                        out[:, column : column + width] = refs[matrix][
                            :, start + first : start + last
                        ].astype(jnp.bfloat16)
                        column += width


def pack(matrices, groups, layouts, name):
    rows = matrices[0].shape[0]
    shapes = []
    for spans in layouts:
        width = sum(last - first for _, first, last in spans)
        shapes += [jax.ShapeDtypeStruct((rows, width), jnp.bfloat16)] * groups
    flat = pl.pallas_call(
        functools.partial(pack_kernel, layouts, groups),
        out_shape=tuple(shapes),
        in_specs=[VMEM] * len(matrices),
        out_specs=(VMEM,) * len(shapes),
        compiler_params=pltpu.CompilerParams(vmem_limit_bytes=VMEM_LIMIT),
        cost_estimate=pl.CostEstimate(
            flops=0,
            bytes_accessed=6 * rows * sum(matrix.shape[1] for matrix in matrices),
            transcendentals=0,
        ),
        name=name,
    )(*matrices)
    return [flat[first : first + groups] for first in range(0, len(flat), groups)]


def exchange(parts):
    moved = [parts[0]] + [swap(part, "kv", other) for other, part in enumerate(parts) if other]
    return jnp.concatenate(moved, axis=0)


def exchange_in_order(parts, kv_index):
    moved = jnp.stack(
        [parts[0]] + [swap(part, "kv", other) for other, part in enumerate(parts) if other], axis=0
    )
    order = jnp.arange(len(parts), dtype=jnp.int32) ^ kv_index
    return jnp.take(moved, order, axis=0).reshape(-1, moved.shape[2])


def after(values, *earlier):
    return lax.optimization_barrier((values, *earlier))[0]


def plane_gather(piece):
    rows = piece.shape[0]
    by_x = swap(piece, "blk", 2)
    by_y = swap(piece, "blk", 4)
    upper = swap(by_y[: rows // 2], "blk", 2)
    lower = swap(by_x[rows // 2 :], "blk", 4)
    mine = [(0, 0, piece), (2, 0, by_x), (4, 0, by_y), (6, 0, upper), (6, rows // 2, lower)]
    return mine + [(index ^ 1, first, swap(part, "blk", 1)) for index, first, part in mine]


def on_columns(body, index, width, count):
    if width % LANES == 0:
        body(pl.ds(pl.multiple_of(index * width, LANES), width))
        return
    for choice in range(count):
        pl.when(index == choice)(functools.partial(body, pl.ds(choice * width, width)))


def row_copies(sources, refs, buffer, sem, blk_index, kv_index, groups):
    copies = []
    total = buffer.shape[0]
    for (index, begin, _), ref in zip(sources, refs):
        rows = ref.shape[0]
        piece = total // 8
        block = piece // groups
        if rows == total and index is None:
            copies.append(pltpu.make_async_copy(ref, buffer, sem))
            continue
        for first in range(0, rows, block):
            piece_index = index[first // piece] if isinstance(index, tuple) else index
            other = (begin + first) % piece // block
            target = (blk_index ^ piece_index) * piece + (kv_index ^ other) * block
            copies.append(
                pltpu.make_async_copy(
                    ref.at[pl.ds(first, block)],
                    buffer.at[pl.ds(pl.multiple_of(target, 16), block)],
                    sem,
                )
            )
    return copies


EXTRA = 16


def cache_kernel(blocks_ref, flags_ref, keys, values):
    first_row = lax.broadcasted_iota(jnp.int32, (EXTRA, 1), 0) == 0
    bias = jnp.where((flags_ref[...] > -FAR) | jnp.logical_not(first_row), 0.0, FLOOR_SCORE)
    for head in range(blocks_ref.shape[2]):
        keys[head, HD:, :] = bias.astype(jnp.bfloat16)
        for block in range(blocks_ref.shape[1]):
            place = pl.ds(block * BLOCK, BLOCK)
            keys[head, :HD, place] = blocks_ref[0, block, head]
            values[head, place, :] = blocks_ref[1, block, head].astype(jnp.float32).T.astype(
                jnp.bfloat16
            )


def cached_rows(blocks, flags):
    kv_local = blocks.shape[2]
    cached = flags.shape[1]
    return pl.pallas_call(
        cache_kernel,
        out_shape=(
            jax.ShapeDtypeStruct((kv_local, HD + EXTRA, cached), jnp.bfloat16),
            jax.ShapeDtypeStruct((kv_local, cached, HD), jnp.bfloat16),
        ),
        in_specs=[VMEM, VMEM],
        out_specs=(VMEM, VMEM),
        compiler_params=pltpu.CompilerParams(vmem_limit_bytes=VMEM_LIMIT),
        cost_estimate=pl.CostEstimate(
            flops=0, bytes_accessed=4 * blocks.size, transcendentals=0
        ),
        name="cached",
    )(blocks, flags)


def project_kernel(
    sources, groups, kv_local, per_group, place_ref, normed_ref, cos_ref, sin_ref, flags_ref, *refs
):
    count = len(sources)
    pieces = refs[:count]
    upper, lower, keys, values, weights, projected, sem = refs[count:]
    half = upper.shape[0]
    copies = row_copies(sources, pieces, weights, sem.at[0], place_ref[0], place_ref[2], groups)
    for copy in copies:
        copy.start()
    new_rows = normed_ref.shape[0]
    chunk_rows = per_group * ROW_TILE
    first_row = lax.broadcasted_iota(jnp.int32, (EXTRA, 1), 0) == 0
    bias = jnp.where((flags_ref[...] > -FAR) | jnp.logical_not(first_row), 0.0, FLOOR_SCORE)
    marker = jnp.where(
        lax.broadcasted_iota(jnp.int32, (chunk_rows, EXTRA), 1) == 0, 1.0, 0.0
    ).astype(jnp.bfloat16)
    for head in range(kv_local):
        keys[head, HD:, :] = bias.astype(jnp.bfloat16)
        for chunk in range(half):
            upper[chunk, head, :, HD:] = marker
            lower[chunk, head, :, HD:] = marker
    for copy in copies:
        copy.wait()
    width = weights.shape[1]
    for first in range(0, width, 2 * TILE):
        columns = slice(first, min(first + 2 * TILE, width))
        projected[:, columns] = jnp.dot(
            normed_ref[...], weights[:, columns], preferred_element_type=jnp.float32
        )

    def rotated(rows, column):
        part = projected[rows, column : column + HD]
        turned = jnp.concatenate([part[:, HD // 2 :], part[:, : HD // 2]], axis=1)
        return part * cos_ref[rows, :] + turned * sin_ref[rows, :]

    query_width = kv_local * per_group * HD
    for chunk in range(new_rows // ROW_TILE):
        rows = pl.ds(chunk * ROW_TILE, ROW_TILE)
        for head in range(kv_local):
            for sub in range(per_group):
                queries = upper if chunk < half else lower
                queries[chunk % half, head, sub * ROW_TILE : (sub + 1) * ROW_TILE, :HD] = rotated(
                    rows, (head * per_group + sub) * HD
                ).astype(jnp.bfloat16)
            keys[head, :HD, rows] = rotated(rows, query_width + head * HD).T.astype(jnp.bfloat16)
            column = query_width + (kv_local + head) * HD
            values[head, rows, :] = projected[rows, column : column + HD].astype(jnp.bfloat16)


def project_rows(place, normed, tables, flags, sources, groups, kv_local, per_group):
    new_rows = normed.shape[0]
    arrays = [values for _, _, values in sources]
    width = arrays[0].shape[1]
    queries = jax.ShapeDtypeStruct(
        (new_rows // ROW_TILE // 2, kv_local, per_group * ROW_TILE, HD + EXTRA), jnp.bfloat16
    )
    upper, lower, keys, values = pl.pallas_call(
        functools.partial(project_kernel, sources, groups, kv_local, per_group),
        out_shape=(
            queries,
            queries,
            jax.ShapeDtypeStruct((kv_local, HD + EXTRA, new_rows), jnp.bfloat16),
            jax.ShapeDtypeStruct((kv_local, new_rows, HD), jnp.bfloat16),
        ),
        in_specs=[SMEM] + [VMEM] * 4 + [ANY] * len(arrays),
        out_specs=(VMEM,) * 4,
        scratch_shapes=[
            pltpu.VMEM((normed.shape[1], width), jnp.bfloat16),
            pltpu.VMEM((new_rows, width), jnp.float32),
            pltpu.SemaphoreType.DMA((1,)),
        ],
        compiler_params=pltpu.CompilerParams(vmem_limit_bytes=VMEM_LIMIT),
        cost_estimate=pl.CostEstimate(
            flops=2 * new_rows * normed.shape[1] * width,
            bytes_accessed=2 * normed.shape[1] * width,
            transcendentals=0,
        ),
        name="project",
    )(place, normed, *tables, flags, *arrays)
    return (upper, lower), (keys, values)


def attention_kernel(
    first_step,
    place_ref,
    queries,
    cached_keys,
    cached_values,
    own_keys,
    own_values,
    cached_ref,
    own_ref,
    out_ref,
    scores,
    probs,
    folded,
    shifts,
    summed,
):
    prefix_here = place_ref[1]
    kv_local, _, cached = cached_keys.shape
    new_rows = own_keys.shape[2]
    chunk_rows = queries.shape[2]
    per_group = chunk_rows // ROW_TILE
    factor = math.log2(math.e) / math.sqrt(HD)
    group = 64
    widest = min(4 * LANES, cached)
    tiles = [
        (first, cached_keys, cached_values, first, widest) for first in range(0, cached, widest)
    ]
    tiles.append((cached, own_keys, own_values, 0, new_rows))

    def score(step, head, first, keys, _, begin, width):
        scores[head, :, pl.ds(first, width)] = jnp.dot(
            queries[step, head],
            keys[head, :, pl.ds(begin, width)],
            preferred_element_type=jnp.float32,
        )
        own = keys is own_keys
        for part in range(chunk_rows // group):
            rows = pl.ds(part * group, group)
            if own:
                row_id = (first_step + step) * ROW_TILE + (part * group) % ROW_TILE + (
                    lax.broadcasted_iota(jnp.int32, (group, LANES), 0)
                )
            top = folded[head, rows, :]
            for lane in range(0, width, LANES):
                place = pl.ds(first + lane, LANES)
                piece = scores[head, rows, place]
                if own:
                    own_id = lane + lax.broadcasted_iota(jnp.int32, (group, LANES), 1)
                    piece = jnp.where(own_id <= row_id, piece, FLOOR_SCORE)
                    scores[head, rows, place] = piece
                top = jnp.maximum(top, piece)
            folded[head, rows, :] = top

    def narrow(step, head):
        def some(part, inner):
            rows = pl.ds(pl.multiple_of(part * 16, 16), 16)
            row_id = (first_step + step) * ROW_TILE + lax.rem(part * 16, ROW_TILE) + (
                lax.broadcasted_iota(jnp.int32, (16, 1), 0)
            )
            oldest = prefix_here + row_id - WINDOW
            old = jnp.where(cached_ref[...] > oldest, scores[head, rows, :cached], FLOOR_SCORE)
            new = jnp.where(own_ref[...] > oldest, scores[head, rows, cached:], FLOOR_SCORE)
            scores[head, rows, :cached] = old
            scores[head, rows, cached:] = new
            top = jnp.maximum(
                jnp.max(old, axis=1, keepdims=True), jnp.max(new, axis=1, keepdims=True)
            )
            folded[head, rows, :] = jnp.broadcast_to(top, (16, LANES))
            return inner

        lax.fori_loop(0, chunk_rows // 16, some, 0)

    def weigh(head, start, first, _, values, begin, width):
        for part in range(chunk_rows // group):
            rows = pl.ds(part * group, group)
            shift = shifts[head, rows, :]
            total = None if start else folded[head, rows, :]
            for lane in range(0, width, LANES):
                place = pl.ds(first + lane, LANES)
                piece = jnp.exp2(scores[head, rows, place] * factor - shift)
                total = piece if total is None else total + piece
                probs[head, rows, place] = piece.astype(jnp.bfloat16)
            folded[head, rows, :] = total
        return jnp.dot(
            probs[head, :, pl.ds(first, width)],
            values[head, pl.ds(begin, width), :],
            preferred_element_type=jnp.float32,
        )

    def attend(windowed, step, carry):
        for head in range(kv_local):
            folded[head] = jnp.full(folded.shape[1:], FLOOR_SCORE, jnp.float32)
            for tile in tiles:
                score(step, head, *tile)
        for head in range(kv_local):
            if windowed:
                narrow(step, head)
            for part in range(chunk_rows // group):
                rows = pl.ds(part * group, group)
                top = jnp.max(folded[head, rows, :], axis=1, keepdims=True) * factor
                shifts[head, rows, :] = jnp.broadcast_to(top, (group, LANES))
            for which, tile in enumerate(tiles):
                part = weigh(head, which == 0, *tile)
                summed[head] = part if which == 0 else summed[head] + part
            rows = pl.ds(pl.multiple_of(step * ROW_TILE, ROW_TILE), ROW_TILE)
            for sub in range(per_group):
                part = pl.ds(sub * ROW_TILE, ROW_TILE)
                total = jnp.sum(folded[head, part, :], axis=1, keepdims=True)
                column = (head * per_group + sub) * HD
                out_ref[rows, column : column + HD] = (summed[head, part, :] / total).astype(
                    jnp.bfloat16
                )
        return carry

    behind = prefix_here + new_rows > WINDOW
    for windowed in (False, True):

        @pl.when(behind == windowed)
        def _():
            lax.fori_loop(0, queries.shape[0], functools.partial(attend, windowed), 0)


def attend_rows(place, first_step, queries, cached, own, cached_pos, own_pos):
    chunks, kv_local, chunk_rows, _ = queries.shape
    span = cached_pos.shape[1] + own_pos.shape[1]
    heads = kv_local * chunk_rows // ROW_TILE
    new_rows = chunks * ROW_TILE
    return pl.pallas_call(
        functools.partial(attention_kernel, first_step),
        out_shape=jax.ShapeDtypeStruct((new_rows, heads * HD), jnp.bfloat16),
        in_specs=[SMEM] + [VMEM] * 7,
        out_specs=VMEM,
        scratch_shapes=[
            pltpu.VMEM((kv_local, chunk_rows, span), jnp.float32),
            pltpu.VMEM((kv_local, chunk_rows, span), jnp.bfloat16),
            pltpu.VMEM((kv_local, chunk_rows, LANES), jnp.float32),
            pltpu.VMEM((kv_local, chunk_rows, LANES), jnp.float32),
            pltpu.VMEM((kv_local, chunk_rows, HD), jnp.float32),
        ],
        compiler_params=pltpu.CompilerParams(vmem_limit_bytes=VMEM_LIMIT),
        cost_estimate=pl.CostEstimate(
            flops=8 * heads * new_rows * span * LANES,
            bytes_accessed=4 * span * LANES * kv_local,
            transcendentals=heads * new_rows * span,
        ),
        name="attention",
    )(place, queries, *cached, *own, cached_pos, own_pos)


def gather_groups(piece):
    groups = lax.axis_size("kv")
    pieces = {0: piece}
    for other in sorted(range(1, groups), key=lambda other: (bin(other).count("1"), -other)):
        low = other & -other
        near = pieces[low] if other ^ low else piece
        pieces[other] = swap(after(pieces[other ^ low], near), "kv", low)
    return [pieces[other] for other in range(groups)]


def sum_at_owner(parts):
    parts = list(parts)
    earlier = []
    for other in sorted(range(1, len(parts)), key=lambda other: -bin(other).count("1")):
        low = other & -other
        target = other ^ low
        came = swap(after(parts[other], *earlier), "kv", low)
        if target:
            earlier.append(came)
        added = parts[target].astype(jnp.float32) + came.astype(jnp.float32)
        parts[target] = added.astype(jnp.bfloat16) if target else added
    return parts[0]


def middle_kernel(sources, groups, place_ref, tokens_ref, gain_ref, *refs):
    parts = len(refs) - len(sources) - 7
    att = refs[:parts]
    own_ref = refs[parts]
    rest = refs[parts + 1 :]
    shares = rest[: len(sources)]
    normed_ref, residual_ref, gathered, weights, middle, sem = rest[len(sources) :]
    blk_index = place_ref[0]
    kv_index = place_ref[2]
    group_rows = own_ref.shape[0]
    new_rows, model = tokens_ref.shape
    tile = 2 * TILE
    loads = []
    for step in range(model // tile):
        columns = pl.ds(step * tile, tile)
        copies = []
        if shares[0].ndim == 3:
            copies.append((own_ref.at[:, columns], weights.at[pl.ds(0, group_rows), columns]))
            for (indices, _, _), ref in zip(sources, shares):
                part = ref.shape[1]
                for at, index in enumerate(indices):
                    first = pl.multiple_of((blk_index ^ index) * part, 16)
                    for other in range(1, groups):
                        lead = at * (groups - 1) + other - 1
                        rows = pl.ds(other * group_rows + first, part)
                        copies.append((ref.at[lead, :, columns], weights.at[rows, columns]))
        else:
            for other in range(groups):
                first = pl.multiple_of((kv_index ^ other) * group_rows, 16)
                rows = pl.ds(other * group_rows, group_rows)
                copies.append(
                    (shares[0].at[pl.ds(first, group_rows), columns], weights.at[rows, columns])
                )
        loads.append(
            [pltpu.make_async_copy(source, target, sem.at[step]) for source, target in copies]
        )
        for copy in loads[-1]:
            copy.start()
    some_rows, feature = att[0].shape
    for at, part in enumerate(att):
        first, other = at // groups * some_rows, at % groups
        gathered[first : first + some_rows, other * feature : (other + 1) * feature] = part[...]
    for step in range(model // tile):
        columns = pl.ds(step * tile, tile)
        for copy in loads[step]:
            copy.wait()
        summed = jnp.dot(gathered[...], weights[:, columns], preferred_element_type=jnp.float32)
        middle[:, columns] = (tokens_ref[:, columns].astype(jnp.float32) + summed).astype(
            jnp.bfloat16
        )

    def scale(step, carry):
        rows = pl.ds(pl.multiple_of(step * 16, 16), 16)
        part = middle[rows, :].astype(jnp.float32)
        mean_square = jnp.mean(part * part, axis=1, keepdims=True)
        normed_ref[rows, :] = (part * lax.rsqrt(mean_square + EPSILON) * gain_ref[...]).astype(
            jnp.bfloat16
        )
        return carry

    lax.fori_loop(0, new_rows // 16, scale, 0, unroll=2)
    out_width = model // groups

    def keep(columns):
        residual_ref[...] = middle[:, columns]

    on_columns(keep, kv_index, out_width, groups)


def middle_rows(place, tokens, gain, attended, own, sources, groups):
    new_rows, model = tokens.shape
    arrays = [values for _, _, values in sources]
    return pl.pallas_call(
        functools.partial(middle_kernel, sources, groups),
        out_shape=(
            jax.ShapeDtypeStruct((new_rows, model), jnp.bfloat16),
            jax.ShapeDtypeStruct((new_rows, model // groups), jnp.bfloat16),
        ),
        in_specs=[SMEM, VMEM, VMEM] + [VMEM] * len(attended) + [ANY] * (1 + len(arrays)),
        out_specs=(VMEM, VMEM),
        scratch_shapes=[
            pltpu.VMEM((new_rows, model), jnp.bfloat16),
            pltpu.VMEM((model, model), jnp.bfloat16),
            pltpu.VMEM((new_rows, model), jnp.bfloat16),
            pltpu.SemaphoreType.DMA((model // (2 * TILE),)),
        ],
        compiler_params=pltpu.CompilerParams(vmem_limit_bytes=VMEM_LIMIT),
        cost_estimate=pl.CostEstimate(
            flops=2 * new_rows * model * model,
            bytes_accessed=2 * model * model,
            transcendentals=0,
        ),
        name="middle",
    )(place, tokens, gain, *attended, own, *arrays)


def hidden_chunks(width):
    return [(first, min(TILE, width - first)) for first in range(0, width, TILE)]


def mlp_kernel(groups, widths, place_ref, normed_ref, down_ref, left, right, *refs):
    outs = refs[:groups]
    first_half, second_half, down, hidden, sems = refs[groups:]
    kv_index = place_ref[2]
    chunks = []
    base = 0
    for width, source, buffer in zip(widths, (left, right), (first_half, second_half)):
        for first, units in hidden_chunks(width):
            columns = pl.ds(2 * first, 2 * units)
            copy = pltpu.make_async_copy(
                source.at[:, columns], buffer.at[:, columns], sems.at[len(chunks)]
            )
            chunks.append((buffer, columns, base + first, units, copy))
        base += width
    last = pltpu.make_async_copy(down_ref, down, sems.at[len(chunks)])
    ahead = 3
    for _, _, _, _, copy in chunks[:ahead]:
        copy.start()
    for at, (buffer, columns, first, units, copy) in enumerate(chunks):
        copy.wait()
        if at + ahead < len(chunks):
            chunks[at + ahead][4].start()
        elif at + ahead == len(chunks):
            last.start()
        both = jnp.dot(normed_ref[...], buffer[:, columns], preferred_element_type=jnp.float32)
        gated, raised = both[:, :units], both[:, units:]
        hidden[:, first : first + units] = (gated / (1.0 + jnp.exp(-gated)) * raised).astype(
            jnp.bfloat16
        )
    last.wait()
    out_width = outs[0].shape[1]
    for other in range(groups):

        def product(columns, out=outs[other]):
            out[...] = jnp.dot(
                hidden[...], down[:, columns], preferred_element_type=jnp.float32
            ).astype(out.dtype)

        on_columns(product, kv_index ^ other, out_width, groups)


def mlp_parts(place, normed, w_down, left, right, groups, widths):
    new_rows, model = normed.shape
    out_width = model // groups
    return pl.pallas_call(
        functools.partial(mlp_kernel, groups, widths),
        out_shape=tuple(
            jax.ShapeDtypeStruct((new_rows, out_width), jnp.bfloat16 if other else jnp.float32)
            for other in range(groups)
        ),
        in_specs=[SMEM, VMEM, ANY, ANY, ANY],
        out_specs=(VMEM,) * groups,
        scratch_shapes=[
            pltpu.VMEM(left.shape, jnp.bfloat16),
            pltpu.VMEM(right.shape, jnp.bfloat16),
            pltpu.VMEM(w_down.shape, jnp.bfloat16),
            pltpu.VMEM((new_rows, w_down.shape[0]), jnp.bfloat16),
            pltpu.SemaphoreType.DMA((1 + sum(len(hidden_chunks(width)) for width in widths),)),
        ],
        compiler_params=pltpu.CompilerParams(vmem_limit_bytes=VMEM_LIMIT),
        cost_estimate=pl.CostEstimate(
            flops=6 * new_rows * model * w_down.shape[0],
            bytes_accessed=6 * model * w_down.shape[0],
            transcendentals=new_rows * w_down.shape[0],
        ),
        name="mlp",
    )(place, normed, w_down, left, right)


def shards(
    tokens,
    attn_gain,
    mlp_gain,
    w_query,
    w_key,
    w_value,
    w_gate,
    w_up,
    w_out,
    w_down,
    cache,
    slot_prompt,
    prefix_len,
    new_len,
):
    groups = lax.axis_size("kv")
    blk_index = lax.axis_index("blk")
    kv_index = lax.axis_index("kv")
    query_width = w_query.shape[1] // groups
    key_width = w_key.shape[1] // groups
    per_group = HEADS // KV_HEADS
    new_rows = tokens.shape[0]
    prompts = prefix_len.shape[0]
    slots = cache.shape[1]
    prefix_here = prefix_len[blk_index]
    live_count = new_len[blk_index]
    place = jnp.stack([blk_index, prefix_here, kv_index]).astype(jnp.int32)

    global_rank, local_rank = slot_ranks(slot_prompt, prompts, slots)
    own_prompts = lax.dynamic_slice_in_dim(slot_prompt, blk_index * slots, slots)
    own_ranks = lax.dynamic_slice_in_dim(local_rank, blk_index * slots, slots)
    placed = own_prompts * CAP + own_ranks
    buffer_ids = jnp.arange(prompts * CAP, dtype=jnp.int32)
    matches = placed[None, :] == buffer_ids[:, None]
    source_slot = jnp.sum(
        jnp.where(matches, jnp.arange(slots, dtype=jnp.int32)[None, :], 0), axis=1
    )
    outgoing = jnp.take(cache, source_slot, axis=1)
    arrived = lax.all_to_all(outgoing, "blk", split_axis=1, concat_axis=1, tiled=True)
    slot_ids = jnp.arange(prompts * slots, dtype=jnp.int32)
    landing = slot_ids // slots * CAP + local_rank
    for_me = slot_prompt == blk_index
    received = (landing[None, :] == buffer_ids[:, None]) & for_me[None, :]
    block_number = jnp.sum(jnp.where(received, global_rank[None, :], 0), axis=1)
    block_live = jnp.any(received, axis=1)
    key_pos = block_number[:, None] * BLOCK + jnp.arange(BLOCK, dtype=jnp.int32)[None, :]
    key_live = block_live[:, None] & (key_pos < prefix_here)
    cached_pos = jnp.where(key_live, jnp.where(key_pos < SINKS, FAR, key_pos), -FAR)
    cached_pos = cached_pos.reshape(1, -1)
    row_ids = jnp.arange(new_rows, dtype=jnp.int32)
    positions = prefix_here + row_ids
    own_pos = jnp.where(
        row_ids < live_count, jnp.where(positions < SINKS, FAR, positions), -FAR
    ).reshape(1, -1)

    normed = rms_scale(tokens, attn_gain)
    tables = rope_tables(positions)
    cached = cached_rows(arrived, cached_pos)

    hidden_width = w_gate.shape[1] // groups
    cut = hidden_width // (2 * TILE) * TILE
    widths = (cut, hidden_width - cut)
    layouts = []
    base = 0
    for width in widths:
        layout = []
        for first, units in hidden_chunks(width):
            start = base + first
            layout += [(0, start, start + units), (1, start, start + units)]
        layouts.append(layout)
        base += width
    packed = pack((w_gate, w_up), groups, layouts, "pack_pair")

    in_place = lax.axis_size("blk") == 8 and w_query.shape[0] % 16 == 0
    spans = [(0, 0, query_width), (1, 0, key_width), (2, 0, key_width)]
    (qkv_parts,) = pack((w_query, w_key, w_value), groups, [spans], "pack_qkv")
    if in_place:
        moved_qkv = exchange(qkv_parts)
        qkv = plane_gather(after(moved_qkv, normed, *tables, own_pos))
        across = [qkv[at][2] for at in (3, 4)]
    else:
        moved_qkv = exchange_in_order(qkv_parts, kv_index)
        qkv = [(None, 0, lax.all_gather(moved_qkv, "blk", axis=0, tiled=True))]
        across = [moved_qkv]

    moved = exchange_in_order(after(packed[0], moved_qkv, arrived), kv_index)
    first_half = lax.all_gather(after(moved, *across), "blk", axis=0, tiled=True)

    eighth = w_out.shape[0] // lax.axis_size("blk")
    spread = in_place and eighth % 16 == 0
    if spread:
        share = lax.dynamic_slice_in_dim(w_out, blk_index * eighth, eighth, 0)
        share = after(share, *across)
        shares = [swap(share, "kv", other) for other in range(1, groups)]

    queries, own = project_rows(
        place, normed, tables, own_pos, qkv, groups, cache.shape[2], per_group
    )
    half = queries[0].shape[0]
    upper = attend_rows(place, 0, queries[0], cached, own, cached_pos, own_pos)
    moved_second = exchange_in_order(after(packed[1], upper), kv_index)
    if spread:
        shares = jnp.stack(after(shares, upper), axis=0)
        near = (swap(shares, "blk", 2), swap(shares, "blk", 4))
    lower = attend_rows(
        place, half, after(queries[1], upper), cached, own, cached_pos, own_pos
    )
    earlier = (lower, *near) if spread else (lower,)
    second_half = lax.all_gather(after(moved_second, *earlier), "blk", axis=0, tiled=True)
    attended = jnp.concatenate([upper, lower], axis=0)
    everyone = gather_groups(attended)

    if spread:
        by_x, by_y = near
        by_y = after(by_y, upper, lower)
        diagonal = swap(by_y, "blk", 2)
        trio = swap(jnp.concatenate([shares, by_x, by_y], axis=0), "blk", 1)
        w_out_sources = [
            ((0,), 0, shares),
            ((2,), 0, by_x),
            ((4,), 0, by_y),
            ((6,), 0, diagonal),
            ((1, 3, 5), 0, trio),
            ((7,), 0, swap(after(diagonal, everyone[-1]), "blk", 1)),
        ]
    else:
        w_out_sources = [(0, 0, lax.all_gather(w_out, "kv", axis=0, tiled=True))]

    normed_mid, residual = middle_rows(
        place, tokens, mlp_gain.reshape(1, -1), everyone, w_out, w_out_sources, groups
    )
    parts = mlp_parts(place, normed_mid, w_down, first_half, second_half, groups, widths)
    reduced = sum_at_owner(parts)
    mixed = jnp.where(
        (row_ids < live_count)[:, None], residual.astype(jnp.float32) + reduced, 0.0
    )
    return mixed.astype(jnp.bfloat16)


def solution(mesh):
    return jax.shard_map(
        shards,
        mesh=mesh,
        in_specs=(
            P("blk", None),
            P(),
            P(),
            P(("blk", "kv"), None),
            P(("blk", "kv"), None),
            P(("blk", "kv"), None),
            P(("blk", "kv"), None),
            P(("blk", "kv"), None),
            P("kv", None),
            P("kv", None),
            P(None, "blk", "kv", None, None),
            P(),
            P(),
            P(),
        ),
        out_specs=P("blk", "kv"),
        check_vma=False,
    )
```

```python
import functools
import math

import jax
import jax.numpy as jnp
from jax import lax
from jax.experimental import pallas as pl
from jax.experimental.pallas import tpu as pltpu
from jax.sharding import PartitionSpec as P

HEADS = 32
KV_HEADS = 8
HD = 80
WINDOW = 4096
SINKS = 4
BLOCK = 128
CAP = 2


FLOOR_SCORE = -1e30
EPSILON = 1e-05
ROPE_BASE = 10000.0
FAR = 1 << 30
LANES = 128
TILE = 256
ROW_TILE = 128
VMEM_LIMIT = 56 * 1024 * 1024

ANY = pl.BlockSpec(memory_space=pl.ANY)
VMEM = pl.BlockSpec(memory_space=pltpu.VMEM)
SMEM = pl.BlockSpec(memory_space=pltpu.SMEM)


def rms_scale(row_data, gain_vec):
    values = row_data.astype(jnp.float32)
    mean_square = jnp.mean(values * values, axis=-1, keepdims=True)
    return (values * lax.rsqrt(mean_square + EPSILON) * gain_vec).astype(jnp.bfloat16)


def rope_tables(positions):
    half_width = HD // 2
    frequency = ROPE_BASE ** (-2.0 * jnp.arange(half_width, dtype=jnp.float32) / HD)
    angles = positions.astype(jnp.float32)[:, None] * frequency[None, :]
    cosine = jnp.cos(angles)
    sine = jnp.sin(angles)
    return (
        jnp.concatenate([cosine, cosine], axis=1),
        jnp.concatenate([-sine, sine], axis=1),
    )


def slot_ranks(slot_prompt, prompts, slots):
    onehot = (slot_prompt[:, None] == jnp.arange(prompts, dtype=jnp.int32)[None, :]).astype(
        jnp.int32
    )
    running = jnp.cumsum(onehot, axis=0)
    global_rank = jnp.sum(onehot * (running - 1), axis=1)
    local_count = jnp.cumsum(onehot.reshape(-1, slots, prompts), axis=1).reshape(-1, prompts)
    local_rank = jnp.sum(onehot * (local_count - 1), axis=1)
    return (global_rank, local_rank)


def swap(values, axis, bit):
    pairs = [(index, index ^ bit) for index in range(lax.axis_size(axis))]
    return lax.ppermute(values, axis, pairs)


def half_up(width):
    return (width // 2 + LANES - 1) // LANES * LANES


def pack_kernel(layouts, groups, *refs):
    kv_index = lax.axis_index("kv")
    outs = refs[len(refs) - groups * len(layouts) :]
    for choice in range(groups):

        @pl.when(kv_index == choice)
        def _():
            for which, spans in enumerate(layouts):
                for other in range(groups):
                    out = outs[which * groups + other]
                    column = 0
                    for matrix, first, last in spans:
                        start = (choice ^ other) * (refs[matrix].shape[1] // groups)
                        width = last - first
                        out[:, column : column + width] = refs[matrix][
                            :, start + first : start + last
                        ].astype(jnp.bfloat16)
                        column += width


def pack(matrices, groups, layouts, name):
    rows = matrices[0].shape[0]
    shapes = []
    for spans in layouts:
        width = sum(last - first for _, first, last in spans)
        shapes += [jax.ShapeDtypeStruct((rows, width), jnp.bfloat16)] * groups
    flat = pl.pallas_call(
        functools.partial(pack_kernel, layouts, groups),
        out_shape=tuple(shapes),
        in_specs=[VMEM] * len(matrices),
        out_specs=(VMEM,) * len(shapes),
        compiler_params=pltpu.CompilerParams(vmem_limit_bytes=VMEM_LIMIT),
        cost_estimate=pl.CostEstimate(
            flops=0,
            bytes_accessed=6 * rows * sum(matrix.shape[1] for matrix in matrices),
            transcendentals=0,
        ),
        name=name,
    )(*matrices)
    return [flat[first : first + groups] for first in range(0, len(flat), groups)]


def exchange(parts):
    moved = [parts[0]] + [swap(part, "kv", other) for other, part in enumerate(parts) if other]
    return jnp.concatenate(moved, axis=0)


def exchange_in_order(parts, kv_index, earlier=()):
    moved = [parts[0]] + [swap(part, "kv", other) for other, part in enumerate(parts) if other]
    moved = jnp.stack(after(moved, *earlier), axis=0)
    order = jnp.arange(len(parts), dtype=jnp.int32) ^ kv_index
    return jnp.take(moved, order, axis=0).reshape(-1, moved.shape[2])


def after(values, *earlier):
    return lax.optimization_barrier((values, *earlier))[0]


def plane_gather(piece):
    rows = piece.shape[0]
    by_x = swap(piece, "blk", 2)
    by_y = swap(piece, "blk", 4)
    upper = swap(by_y[: rows // 2], "blk", 2)
    lower = swap(by_x[rows // 2 :], "blk", 4)
    mine = [(0, 0, piece), (2, 0, by_x), (4, 0, by_y), (6, 0, upper), (6, rows // 2, lower)]
    return mine + [(index ^ 1, first, swap(part, "blk", 1)) for index, first, part in mine]


def on_columns(body, index, width, count):
    if width % LANES == 0:
        body(pl.ds(pl.multiple_of(index * width, LANES), width))
        return
    for choice in range(count):
        pl.when(index == choice)(functools.partial(body, pl.ds(choice * width, width)))


def row_copies(sources, refs, buffer, sem, blk_index, kv_index, groups):
    copies = []
    total = buffer.shape[0]
    for (index, begin, _), ref in zip(sources, refs):
        rows = ref.shape[0]
        piece = total // 8
        block = piece // groups
        if rows == total and index is None:
            copies.append(pltpu.make_async_copy(ref, buffer, sem))
            continue
        for first in range(0, rows, block):
            piece_index = index[first // piece] if isinstance(index, tuple) else index
            other = (begin + first) % piece // block
            target = (blk_index ^ piece_index) * piece + (kv_index ^ other) * block
            copies.append(
                pltpu.make_async_copy(
                    ref.at[pl.ds(first, block)],
                    buffer.at[pl.ds(pl.multiple_of(target, 16), block)],
                    sem,
                )
            )
    return copies


EXTRA = 16


def cache_kernel(blocks_ref, flags_ref, keys, values):
    first_row = lax.broadcasted_iota(jnp.int32, (EXTRA, 1), 0) == 0
    bias = jnp.where((flags_ref[...] > -FAR) | jnp.logical_not(first_row), 0.0, FLOOR_SCORE)
    for head in range(blocks_ref.shape[2]):
        keys[head, HD:, :] = bias.astype(jnp.bfloat16)
        for block in range(blocks_ref.shape[1]):
            place = pl.ds(block * BLOCK, BLOCK)
            keys[head, :HD, place] = blocks_ref[0, block, head]
            values[head, place, :] = blocks_ref[1, block, head].astype(jnp.float32).T.astype(
                jnp.bfloat16
            )


def cached_rows(blocks, flags):
    kv_local = blocks.shape[2]
    cached = flags.shape[1]
    return pl.pallas_call(
        cache_kernel,
        out_shape=(
            jax.ShapeDtypeStruct((kv_local, HD + EXTRA, cached), jnp.bfloat16),
            jax.ShapeDtypeStruct((kv_local, cached, HD), jnp.bfloat16),
        ),
        in_specs=[VMEM, VMEM],
        out_specs=(VMEM, VMEM),
        compiler_params=pltpu.CompilerParams(vmem_limit_bytes=VMEM_LIMIT),
        cost_estimate=pl.CostEstimate(
            flops=0, bytes_accessed=4 * blocks.size, transcendentals=0
        ),
        name="cached",
    )(blocks, flags)


def project_kernel(
    sources, groups, kv_local, per_group, place_ref, normed_ref, cos_ref, sin_ref, flags_ref, *refs
):
    count = len(sources)
    pieces = refs[:count]
    upper, lower, keys, values, weights, projected, sem = refs[count:]
    half = upper.shape[0]
    copies = row_copies(sources, pieces, weights, sem.at[0], place_ref[0], place_ref[2], groups)
    for copy in copies:
        copy.start()
    new_rows = normed_ref.shape[0]
    chunk_rows = per_group * ROW_TILE
    first_row = lax.broadcasted_iota(jnp.int32, (EXTRA, 1), 0) == 0
    bias = jnp.where((flags_ref[...] > -FAR) | jnp.logical_not(first_row), 0.0, FLOOR_SCORE)
    marker = jnp.where(
        lax.broadcasted_iota(jnp.int32, (chunk_rows, EXTRA), 1) == 0, 1.0, 0.0
    ).astype(jnp.bfloat16)
    for head in range(kv_local):
        keys[head, HD:, :] = bias.astype(jnp.bfloat16)
        for chunk in range(half):
            upper[chunk, head, :, HD:] = marker
            lower[chunk, head, :, HD:] = marker
    for copy in copies:
        copy.wait()
    width = weights.shape[1]
    for first in range(0, width, 2 * TILE):
        columns = slice(first, min(first + 2 * TILE, width))
        projected[:, columns] = jnp.dot(
            normed_ref[...], weights[:, columns], preferred_element_type=jnp.float32
        )

    def rotated(rows, column):
        part = projected[rows, column : column + HD]
        turned = jnp.concatenate([part[:, HD // 2 :], part[:, : HD // 2]], axis=1)
        return part * cos_ref[rows, :] + turned * sin_ref[rows, :]

    query_width = kv_local * per_group * HD
    for chunk in range(new_rows // ROW_TILE):
        rows = pl.ds(chunk * ROW_TILE, ROW_TILE)
        for head in range(kv_local):
            for sub in range(per_group):
                queries = upper if chunk < half else lower
                queries[chunk % half, head, sub * ROW_TILE : (sub + 1) * ROW_TILE, :HD] = rotated(
                    rows, (head * per_group + sub) * HD
                ).astype(jnp.bfloat16)
            keys[head, :HD, rows] = rotated(rows, query_width + head * HD).T.astype(jnp.bfloat16)
            column = query_width + (kv_local + head) * HD
            values[head, rows, :] = projected[rows, column : column + HD].astype(jnp.bfloat16)


def project_rows(place, normed, tables, flags, sources, groups, kv_local, per_group):
    new_rows = normed.shape[0]
    arrays = [values for _, _, values in sources]
    width = arrays[0].shape[1]
    queries = jax.ShapeDtypeStruct(
        (new_rows // ROW_TILE // 2, kv_local, per_group * ROW_TILE, HD + EXTRA), jnp.bfloat16
    )
    upper, lower, keys, values = pl.pallas_call(
        functools.partial(project_kernel, sources, groups, kv_local, per_group),
        out_shape=(
            queries,
            queries,
            jax.ShapeDtypeStruct((kv_local, HD + EXTRA, new_rows), jnp.bfloat16),
            jax.ShapeDtypeStruct((kv_local, new_rows, HD), jnp.bfloat16),
        ),
        in_specs=[SMEM] + [VMEM] * 4 + [ANY] * len(arrays),
        out_specs=(VMEM,) * 4,
        scratch_shapes=[
            pltpu.VMEM((normed.shape[1], width), jnp.bfloat16),
            pltpu.VMEM((new_rows, width), jnp.float32),
            pltpu.SemaphoreType.DMA((1,)),
        ],
        compiler_params=pltpu.CompilerParams(vmem_limit_bytes=VMEM_LIMIT),
        cost_estimate=pl.CostEstimate(
            flops=2 * new_rows * normed.shape[1] * width,
            bytes_accessed=2 * normed.shape[1] * width,
            transcendentals=0,
        ),
        name="project",
    )(place, normed, *tables, flags, *arrays)
    return (upper, lower), (keys, values)


def attention_kernel(
    first_step,
    place_ref,
    queries,
    cached_keys,
    cached_values,
    own_keys,
    own_values,
    cached_ref,
    own_ref,
    out_ref,
    scores,
    probs,
    folded,
    shifts,
    summed,
):
    prefix_here = place_ref[1]
    kv_local, _, cached = cached_keys.shape
    new_rows = own_keys.shape[2]
    chunk_rows = queries.shape[2]
    per_group = chunk_rows // ROW_TILE
    factor = math.log2(math.e) / math.sqrt(HD)
    group = 64
    widest = min(4 * LANES, cached)
    tiles = [
        (first, cached_keys, cached_values, first, widest) for first in range(0, cached, widest)
    ]
    tiles.append((cached, own_keys, own_values, 0, new_rows))

    def score(step, head, first, keys, _, begin, width):
        scores[head, :, pl.ds(first, width)] = jnp.dot(
            queries[step, head],
            keys[head, :, pl.ds(begin, width)],
            preferred_element_type=jnp.float32,
        )
        own = keys is own_keys
        for part in range(chunk_rows // group):
            rows = pl.ds(part * group, group)
            if own:
                row_id = (first_step + step) * ROW_TILE + (part * group) % ROW_TILE + (
                    lax.broadcasted_iota(jnp.int32, (group, LANES), 0)
                )
            top = folded[head, rows, :]
            for lane in range(0, width, LANES):
                place = pl.ds(first + lane, LANES)
                piece = scores[head, rows, place]
                if own:
                    own_id = lane + lax.broadcasted_iota(jnp.int32, (group, LANES), 1)
                    piece = jnp.where(own_id <= row_id, piece, FLOOR_SCORE)
                    scores[head, rows, place] = piece
                top = jnp.maximum(top, piece)
            folded[head, rows, :] = top

    def narrow(step, head):
        def some(part, inner):
            rows = pl.ds(pl.multiple_of(part * 16, 16), 16)
            row_id = (first_step + step) * ROW_TILE + lax.rem(part * 16, ROW_TILE) + (
                lax.broadcasted_iota(jnp.int32, (16, 1), 0)
            )
            oldest = prefix_here + row_id - WINDOW
            old = jnp.where(cached_ref[...] > oldest, scores[head, rows, :cached], FLOOR_SCORE)
            new = jnp.where(own_ref[...] > oldest, scores[head, rows, cached:], FLOOR_SCORE)
            scores[head, rows, :cached] = old
            scores[head, rows, cached:] = new
            top = jnp.maximum(
                jnp.max(old, axis=1, keepdims=True), jnp.max(new, axis=1, keepdims=True)
            )
            folded[head, rows, :] = jnp.broadcast_to(top, (16, LANES))
            return inner

        lax.fori_loop(0, chunk_rows // 16, some, 0)

    def weigh(head, start, first, _, values, begin, width):
        for part in range(chunk_rows // group):
            rows = pl.ds(part * group, group)
            shift = shifts[head, rows, :]
            total = None if start else folded[head, rows, :]
            for lane in range(0, width, LANES):
                place = pl.ds(first + lane, LANES)
                piece = jnp.exp2(scores[head, rows, place] * factor - shift)
                total = piece if total is None else total + piece
                probs[head, rows, place] = piece.astype(jnp.bfloat16)
            folded[head, rows, :] = total
        return jnp.dot(
            probs[head, :, pl.ds(first, width)],
            values[head, pl.ds(begin, width), :],
            preferred_element_type=jnp.float32,
        )

    def attend(windowed, step, carry):
        for head in range(kv_local):
            folded[head] = jnp.full(folded.shape[1:], FLOOR_SCORE, jnp.float32)
            for tile in tiles:
                score(step, head, *tile)
        for head in range(kv_local):
            if windowed:
                narrow(step, head)
            for part in range(chunk_rows // group):
                rows = pl.ds(part * group, group)
                top = jnp.max(folded[head, rows, :], axis=1, keepdims=True) * factor
                shifts[head, rows, :] = jnp.broadcast_to(top, (group, LANES))
            for which, tile in enumerate(tiles):
                part = weigh(head, which == 0, *tile)
                summed[head] = part if which == 0 else summed[head] + part
            rows = pl.ds(pl.multiple_of(step * ROW_TILE, ROW_TILE), ROW_TILE)
            for sub in range(per_group):
                part = pl.ds(sub * ROW_TILE, ROW_TILE)
                total = jnp.sum(folded[head, part, :], axis=1, keepdims=True)
                column = (head * per_group + sub) * HD
                out_ref[rows, column : column + HD] = (summed[head, part, :] / total).astype(
                    jnp.bfloat16
                )
        return carry

    behind = prefix_here + new_rows > WINDOW
    for windowed in (False, True):

        @pl.when(behind == windowed)
        def _():
            lax.fori_loop(0, queries.shape[0], functools.partial(attend, windowed), 0)


def attend_rows(place, first_step, queries, cached, own, cached_pos, own_pos):
    chunks, kv_local, chunk_rows, _ = queries.shape
    span = cached_pos.shape[1] + own_pos.shape[1]
    heads = kv_local * chunk_rows // ROW_TILE
    new_rows = chunks * ROW_TILE
    return pl.pallas_call(
        functools.partial(attention_kernel, first_step),
        out_shape=jax.ShapeDtypeStruct((new_rows, heads * HD), jnp.bfloat16),
        in_specs=[SMEM] + [VMEM] * 7,
        out_specs=VMEM,
        scratch_shapes=[
            pltpu.VMEM((kv_local, chunk_rows, span), jnp.float32),
            pltpu.VMEM((kv_local, chunk_rows, span), jnp.bfloat16),
            pltpu.VMEM((kv_local, chunk_rows, LANES), jnp.float32),
            pltpu.VMEM((kv_local, chunk_rows, LANES), jnp.float32),
            pltpu.VMEM((kv_local, chunk_rows, HD), jnp.float32),
        ],
        compiler_params=pltpu.CompilerParams(vmem_limit_bytes=VMEM_LIMIT),
        cost_estimate=pl.CostEstimate(
            flops=8 * heads * new_rows * span * LANES,
            bytes_accessed=4 * span * LANES * kv_local,
            transcendentals=heads * new_rows * span,
        ),
        name="attention",
    )(place, queries, *cached, *own, cached_pos, own_pos)


def gather_groups(piece):
    groups = lax.axis_size("kv")
    pieces = {0: piece}
    for other in sorted(range(1, groups), key=lambda other: (bin(other).count("1"), -other)):
        low = other & -other
        near = pieces[low] if other ^ low else piece
        pieces[other] = swap(after(pieces[other ^ low], near), "kv", low)
    return [pieces[other] for other in range(groups)]


def sum_at_owner(parts):
    parts = list(parts)
    earlier = []
    for other in sorted(range(1, len(parts)), key=lambda other: -bin(other).count("1")):
        low = other & -other
        target = other ^ low
        came = swap(after(parts[other], *earlier), "kv", low)
        if target:
            earlier.append(came)
        added = parts[target].astype(jnp.float32) + came.astype(jnp.float32)
        parts[target] = added.astype(jnp.bfloat16) if target else added
    return parts[0]


def middle_kernel(sources, groups, place_ref, tokens_ref, gain_ref, *refs):
    parts = len(refs) - len(sources) - 7
    att = refs[:parts]
    own_ref = refs[parts]
    rest = refs[parts + 1 :]
    shares = rest[: len(sources)]
    normed_ref, residual_ref, gathered, weights, middle, sem = rest[len(sources) :]
    blk_index = place_ref[0]
    kv_index = place_ref[2]
    group_rows = own_ref.shape[0]
    new_rows, model = tokens_ref.shape
    tile = 2 * TILE
    loads = []
    for step in range(model // tile):
        columns = pl.ds(step * tile, tile)
        copies = []
        if shares[0].ndim == 3:
            copies.append((own_ref.at[:, columns], weights.at[pl.ds(0, group_rows), columns]))
            for (indices, _, _), ref in zip(sources, shares):
                part = ref.shape[1]
                for at, index in enumerate(indices):
                    first = pl.multiple_of((blk_index ^ index) * part, 16)
                    for other in range(1, groups):
                        lead = at * (groups - 1) + other - 1
                        rows = pl.ds(other * group_rows + first, part)
                        copies.append((ref.at[lead, :, columns], weights.at[rows, columns]))
        else:
            for other in range(groups):
                first = pl.multiple_of((kv_index ^ other) * group_rows, 16)
                rows = pl.ds(other * group_rows, group_rows)
                copies.append(
                    (shares[0].at[pl.ds(first, group_rows), columns], weights.at[rows, columns])
                )
        loads.append(
            [pltpu.make_async_copy(source, target, sem.at[step]) for source, target in copies]
        )
        for copy in loads[-1]:
            copy.start()
    some_rows, feature = att[0].shape
    for at, part in enumerate(att):
        first, other = at // groups * some_rows, at % groups
        gathered[first : first + some_rows, other * feature : (other + 1) * feature] = part[...]
    for step in range(model // tile):
        columns = pl.ds(step * tile, tile)
        for copy in loads[step]:
            copy.wait()
        summed = jnp.dot(gathered[...], weights[:, columns], preferred_element_type=jnp.float32)
        middle[:, columns] = (tokens_ref[:, columns].astype(jnp.float32) + summed).astype(
            jnp.bfloat16
        )

    def scale(step, carry):
        rows = pl.ds(pl.multiple_of(step * 16, 16), 16)
        part = middle[rows, :].astype(jnp.float32)
        mean_square = jnp.mean(part * part, axis=1, keepdims=True)
        normed_ref[rows, :] = (part * lax.rsqrt(mean_square + EPSILON) * gain_ref[...]).astype(
            jnp.bfloat16
        )
        return carry

    lax.fori_loop(0, new_rows // 16, scale, 0, unroll=2)
    out_width = model // groups

    def keep(columns):
        residual_ref[...] = middle[:, columns]

    on_columns(keep, kv_index, out_width, groups)


def middle_rows(place, tokens, gain, attended, own, sources, groups):
    new_rows, model = tokens.shape
    arrays = [values for _, _, values in sources]
    return pl.pallas_call(
        functools.partial(middle_kernel, sources, groups),
        out_shape=(
            jax.ShapeDtypeStruct((new_rows, model), jnp.bfloat16),
            jax.ShapeDtypeStruct((new_rows, model // groups), jnp.bfloat16),
        ),
        in_specs=[SMEM, VMEM, VMEM] + [VMEM] * len(attended) + [ANY] * (1 + len(arrays)),
        out_specs=(VMEM, VMEM),
        scratch_shapes=[
            pltpu.VMEM((new_rows, model), jnp.bfloat16),
            pltpu.VMEM((model, model), jnp.bfloat16),
            pltpu.VMEM((new_rows, model), jnp.bfloat16),
            pltpu.SemaphoreType.DMA((model // (2 * TILE),)),
        ],
        compiler_params=pltpu.CompilerParams(vmem_limit_bytes=VMEM_LIMIT),
        cost_estimate=pl.CostEstimate(
            flops=2 * new_rows * model * model,
            bytes_accessed=2 * model * model,
            transcendentals=0,
        ),
        name="middle",
    )(place, tokens, gain, *attended, own, *arrays)


def hidden_chunks(width):
    return [(first, min(TILE, width - first)) for first in range(0, width, TILE)]


def mlp_kernel(groups, widths, place_ref, normed_ref, down_ref, left, right, *refs):
    outs = refs[:groups]
    first_half, second_half, down, hidden, sems = refs[groups:]
    kv_index = place_ref[2]
    chunks = []
    base = 0
    for width, source, buffer in zip(widths, (left, right), (first_half, second_half)):
        for first, units in hidden_chunks(width):
            columns = pl.ds(2 * first, 2 * units)
            copy = pltpu.make_async_copy(
                source.at[:, columns], buffer.at[:, columns], sems.at[len(chunks)]
            )
            chunks.append((buffer, columns, base + first, units, copy))
        base += width
    last = pltpu.make_async_copy(down_ref, down, sems.at[len(chunks)])
    ahead = 3
    for _, _, _, _, copy in chunks[:ahead]:
        copy.start()
    for at, (buffer, columns, first, units, copy) in enumerate(chunks):
        copy.wait()
        if at + ahead < len(chunks):
            chunks[at + ahead][4].start()
        elif at + ahead == len(chunks):
            last.start()
        both = jnp.dot(normed_ref[...], buffer[:, columns], preferred_element_type=jnp.float32)
        gated, raised = both[:, :units], both[:, units:]
        hidden[:, first : first + units] = (gated / (1.0 + jnp.exp(-gated)) * raised).astype(
            jnp.bfloat16
        )
    last.wait()
    out_width = outs[0].shape[1]
    for other in range(groups):

        def product(columns, out=outs[other]):
            out[...] = jnp.dot(
                hidden[...], down[:, columns], preferred_element_type=jnp.float32
            ).astype(out.dtype)

        on_columns(product, kv_index ^ other, out_width, groups)


def mlp_parts(place, normed, w_down, left, right, groups, widths):
    new_rows, model = normed.shape
    out_width = model // groups
    return pl.pallas_call(
        functools.partial(mlp_kernel, groups, widths),
        out_shape=tuple(
            jax.ShapeDtypeStruct((new_rows, out_width), jnp.bfloat16 if other else jnp.float32)
            for other in range(groups)
        ),
        in_specs=[SMEM, VMEM, ANY, ANY, ANY],
        out_specs=(VMEM,) * groups,
        scratch_shapes=[
            pltpu.VMEM(left.shape, jnp.bfloat16),
            pltpu.VMEM(right.shape, jnp.bfloat16),
            pltpu.VMEM(w_down.shape, jnp.bfloat16),
            pltpu.VMEM((new_rows, w_down.shape[0]), jnp.bfloat16),
            pltpu.SemaphoreType.DMA((1 + sum(len(hidden_chunks(width)) for width in widths),)),
        ],
        compiler_params=pltpu.CompilerParams(vmem_limit_bytes=VMEM_LIMIT),
        cost_estimate=pl.CostEstimate(
            flops=6 * new_rows * model * w_down.shape[0],
            bytes_accessed=6 * model * w_down.shape[0],
            transcendentals=new_rows * w_down.shape[0],
        ),
        name="mlp",
    )(place, normed, w_down, left, right)


def shards(
    tokens,
    attn_gain,
    mlp_gain,
    w_query,
    w_key,
    w_value,
    w_gate,
    w_up,
    w_out,
    w_down,
    cache,
    slot_prompt,
    prefix_len,
    new_len,
):
    groups = lax.axis_size("kv")
    blk_index = lax.axis_index("blk")
    kv_index = lax.axis_index("kv")
    query_width = w_query.shape[1] // groups
    key_width = w_key.shape[1] // groups
    per_group = HEADS // KV_HEADS
    new_rows = tokens.shape[0]
    prompts = prefix_len.shape[0]
    slots = cache.shape[1]
    prefix_here = prefix_len[blk_index]
    live_count = new_len[blk_index]
    place = jnp.stack([blk_index, prefix_here, kv_index]).astype(jnp.int32)

    global_rank, local_rank = slot_ranks(slot_prompt, prompts, slots)
    own_prompts = lax.dynamic_slice_in_dim(slot_prompt, blk_index * slots, slots)
    own_ranks = lax.dynamic_slice_in_dim(local_rank, blk_index * slots, slots)
    placed = own_prompts * CAP + own_ranks
    buffer_ids = jnp.arange(prompts * CAP, dtype=jnp.int32)
    matches = placed[None, :] == buffer_ids[:, None]
    source_slot = jnp.sum(
        jnp.where(matches, jnp.arange(slots, dtype=jnp.int32)[None, :], 0), axis=1
    )
    outgoing = jnp.take(cache, source_slot, axis=1)
    arrived = lax.all_to_all(outgoing, "blk", split_axis=1, concat_axis=1, tiled=True)
    slot_ids = jnp.arange(prompts * slots, dtype=jnp.int32)
    landing = slot_ids // slots * CAP + local_rank
    for_me = slot_prompt == blk_index
    received = (landing[None, :] == buffer_ids[:, None]) & for_me[None, :]
    block_number = jnp.sum(jnp.where(received, global_rank[None, :], 0), axis=1)
    block_live = jnp.any(received, axis=1)
    key_pos = block_number[:, None] * BLOCK + jnp.arange(BLOCK, dtype=jnp.int32)[None, :]
    key_live = block_live[:, None] & (key_pos < prefix_here)
    cached_pos = jnp.where(key_live, jnp.where(key_pos < SINKS, FAR, key_pos), -FAR)
    cached_pos = cached_pos.reshape(1, -1)
    row_ids = jnp.arange(new_rows, dtype=jnp.int32)
    positions = prefix_here + row_ids
    own_pos = jnp.where(
        row_ids < live_count, jnp.where(positions < SINKS, FAR, positions), -FAR
    ).reshape(1, -1)

    normed = rms_scale(tokens, attn_gain)
    tables = rope_tables(positions)
    cached = cached_rows(arrived, cached_pos)

    hidden_width = w_gate.shape[1] // groups
    cut = hidden_width // (2 * TILE) * TILE
    widths = (cut, hidden_width - cut)
    layouts = []
    base = 0
    for width in widths:
        layout = []
        for first, units in hidden_chunks(width):
            start = base + first
            layout += [(0, start, start + units), (1, start, start + units)]
        layouts.append(layout)
        base += width
    packed = pack((w_gate, w_up), groups, layouts, "pack_pair")

    in_place = lax.axis_size("blk") == 8 and w_query.shape[0] % 16 == 0
    spans = [(0, 0, query_width), (1, 0, key_width), (2, 0, key_width)]
    (qkv_parts,) = pack((w_query, w_key, w_value), groups, [spans], "pack_qkv")
    if in_place:
        moved_qkv = exchange(qkv_parts)
        qkv = plane_gather(after(moved_qkv, normed, *tables, own_pos))
        across = [qkv[at][2] for at in (3, 4)]
    else:
        moved_qkv = exchange_in_order(qkv_parts, kv_index)
        qkv = [(None, 0, lax.all_gather(moved_qkv, "blk", axis=0, tiled=True))]
        across = [moved_qkv]

    moved = exchange_in_order(after(packed[0], moved_qkv, arrived), kv_index)
    first_half = lax.all_gather(after(moved, *across), "blk", axis=0, tiled=True)

    eighth = w_out.shape[0] // lax.axis_size("blk")
    spread = in_place and eighth % 16 == 0
    if spread:
        share = lax.dynamic_slice_in_dim(w_out, blk_index * eighth, eighth, 0)

    queries, own = project_rows(
        place, normed, tables, own_pos, qkv, groups, cache.shape[2], per_group
    )
    half = queries[0].shape[0]
    upper = attend_rows(place, 0, queries[0], cached, own, cached_pos, own_pos)
    moved_second = exchange_in_order(after(packed[1], *across), kv_index, (upper,))
    second_half = lax.all_gather(moved_second, "blk", axis=0, tiled=True)
    lower = attend_rows(
        place, half, after(queries[1], upper), cached, own, cached_pos, own_pos
    )
    if spread:
        share = after(share, upper)
        shares = [swap(share, "kv", other) for other in range(1, groups)]
        shares = jnp.stack(after(shares, lower), axis=0)
        near = (swap(shares, "blk", 2), swap(shares, "blk", 4))
    attended = jnp.concatenate([upper, lower], axis=0)
    everyone = gather_groups(attended)

    if spread:
        by_x, by_y = after(near, everyone[1], everyone[2])
        diagonal = swap(by_y, "blk", 2)
        trio = swap(jnp.concatenate([shares, by_x, by_y], axis=0), "blk", 1)
        w_out_sources = [
            ((0,), 0, shares),
            ((2,), 0, by_x),
            ((4,), 0, by_y),
            ((6,), 0, diagonal),
            ((1, 3, 5), 0, trio),
            ((7,), 0, swap(after(diagonal, everyone[-1]), "blk", 1)),
        ]
    else:
        w_out_sources = [(0, 0, lax.all_gather(w_out, "kv", axis=0, tiled=True))]

    normed_mid, residual = middle_rows(
        place, tokens, mlp_gain.reshape(1, -1), everyone, w_out, w_out_sources, groups
    )
    parts = mlp_parts(place, normed_mid, w_down, first_half, second_half, groups, widths)
    reduced = sum_at_owner(parts)
    mixed = jnp.where(
        (row_ids < live_count)[:, None], residual.astype(jnp.float32) + reduced, 0.0
    )
    return mixed.astype(jnp.bfloat16)


def solution(mesh):
    return jax.shard_map(
        shards,
        mesh=mesh,
        in_specs=(
            P("blk", None),
            P(),
            P(),
            P(("blk", "kv"), None),
            P(("blk", "kv"), None),
            P(("blk", "kv"), None),
            P(("blk", "kv"), None),
            P(("blk", "kv"), None),
            P("kv", None),
            P("kv", None),
            P(None, "blk", "kv", None, None),
            P(),
            P(),
            P(),
        ),
        out_specs=P("blk", "kv"),
        check_vma=False,
    )
```
